32 devices in a mesh: dp: 8 (over y, x, core), seq: 4 (over z).
Axes of the slice: x: 2, y: 2, z: 4, core: 2. Of those that a mesh axis runs over, the one named last changes fastest.
Arguments:
- inputs: float32 [8, 1024, 1024], P('dp', 'seq'), may hold values from -6 to 6
- memory: float32 [8, 1024, 1024], P('dp', 'seq'), may hold values from -6 to 6
- group_place: int32 [8, 4], P('dp'), may hold values from 0 to 3, each once within a row
- pair_mask: int32 [8], P('dp'), may hold values 0 or 1
- cotangent: float32 [8, 1024, 1024], P('dp', 'seq'), may hold values from -6 to 6
- self_inward: bfloat16 [1024, 3072], P(('dp', 'seq')), may hold values from -0.1875 to 0.1875
- self_outward: bfloat16 [1024, 1024], P(('dp', 'seq')), may hold values from -3 to 3
- self_query_bias: bfloat16 [1024], P(('dp', 'seq')), may hold values from -3 to 3
- self_value_bias: bfloat16 [1024], P(('dp', 'seq')), may hold values from -0.3125 to 0.3125
- self_output_bias: bfloat16 [1024], P(('dp', 'seq')), may hold values from -6 to 6
- first_gain: bfloat16 [1024], P(('dp', 'seq')), may hold values from 0.5 to 1.5
- first_shift: bfloat16 [1024], P(('dp', 'seq')), may hold values from -3 to 3
- cross_query: bfloat16 [1024, 1024], P(('dp', 'seq')), may hold values from -0.1875 to 0.1875
- cross_memory: bfloat16 [1024, 2048], P(('dp', 'seq')), may hold values from -0.1875 to 0.1875
- cross_outward: bfloat16 [1024, 1024], P(('dp', 'seq')), may hold values from -3 to 3
- cross_query_bias: bfloat16 [1024], P(('dp', 'seq')), may hold values from -3 to 3
- cross_value_bias: bfloat16 [1024], P(('dp', 'seq')), may hold values from -0.3125 to 0.3125
- cross_output_bias: bfloat16 [1024], P(('dp', 'seq')), may hold values from -6 to 6
- second_gain: bfloat16 [1024], P(('dp', 'seq')), may hold values from 0.5 to 1.5
- second_shift: bfloat16 [1024], P(('dp', 'seq')), may hold values from -3 to 3
- expand_weight: bfloat16 [1024, 4096], P(('dp', 'seq')), may hold values from -0.1875 to 0.1875
- expand_bias: bfloat16 [4096], P(('dp', 'seq')), may hold values from -3 to 3
- reduce_weight: bfloat16 [4096, 1024], P(('dp', 'seq')), may hold values from -0.25 to 0.25
- reduce_bias: bfloat16 [1024], P(('dp', 'seq')), may hold values from -6 to 6
- third_gain: bfloat16 [1024], P(('dp', 'seq')), may hold values from 0.5 to 1.5
- third_shift: bfloat16 [1024], P(('dp', 'seq')), may hold values from -3 to 3
Outputs:
- output: float32 [8, 1024, 1024], P('dp', 'seq')
- inputs_gradient: float32 [8, 1024, 1024], P('dp', 'seq')
- memory_gradient: float32 [8, 1024, 1024], P('dp', 'seq')
- self_inward_gradient: float32 [1024, 3072], P(('dp', 'seq'))
- self_outward_gradient: float32 [1024, 1024], P(('dp', 'seq'))
- self_query_bias_gradient: float32 [1024], P(('dp', 'seq'))
- self_value_bias_gradient: float32 [1024], P(('dp', 'seq'))
- self_output_bias_gradient: float32 [1024], P(('dp', 'seq'))
- first_gain_gradient: float32 [1024], P(('dp', 'seq'))
- first_shift_gradient: float32 [1024], P(('dp', 'seq'))
- cross_query_gradient: float32 [1024, 1024], P(('dp', 'seq'))
- cross_memory_gradient: float32 [1024, 2048], P(('dp', 'seq'))
- cross_outward_gradient: float32 [1024, 1024], P(('dp', 'seq'))
- cross_query_bias_gradient: float32 [1024], P(('dp', 'seq'))
- cross_value_bias_gradient: float32 [1024], P(('dp', 'seq'))
- cross_output_bias_gradient: float32 [1024], P(('dp', 'seq'))
- second_gain_gradient: float32 [1024], P(('dp', 'seq'))
- second_shift_gradient: float32 [1024], P(('dp', 'seq'))
- expand_weight_gradient: float32 [1024, 4096], P(('dp', 'seq'))
- expand_bias_gradient: float32 [4096], P(('dp', 'seq'))
- reduce_weight_gradient: float32 [4096, 1024], P(('dp', 'seq'))
- reduce_bias_gradient: float32 [1024], P(('dp', 'seq'))
- third_gain_gradient: float32 [1024], P(('dp', 'seq'))
- third_shift_gradient: float32 [1024], P(('dp', 'seq'))
The draws below stay inside these ranges and needn't reach their ends.
Inputs may be any that keep to these rules, and one draw needn't show every extreme that they name: `group_place`: each row is an ordering of the 4 blocks of positions. `pair_mask`: 1 marks a real pair, 0 a padding pair whose cotangent is ignored.
All inputs are finite; a program needn't handle non-finite values. No bound on the sum of `pair_mask` on one device may be relied on, other than what follows from the above.
Results may differ from the reference program's by a relative error of at most 0.019.
Values may be sent and summed in bfloat16 or wider, within the bound.
No kernel may reach another device: no remote copies, remote signals or barrier semaphores. Data moves between devices by JAX's collectives and lax.ppermute only.
A program may use at most 320 MiB of HBM per device.

```python
import jax
import jax.numpy as jnp
from jax import lax

D = 1024
HEADS = 16
HEAD_DIM = 64
FF = 4096
LENGTH = 1024
SEQ_PARTS = 4
GROUP = 256
PAIRS = 8


def place_ends(values, own_key, low, top_value):
    shape = values.shape
    place = [jax.random.randint(jax.random.fold_in(own_key, axis), (), 0, shape[axis]) for axis in range(len(shape))]
    values = values.at[tuple(place)].set(low)
    longest = shape.index(max(shape))
    place[longest] = (place[longest] + 1) % shape[longest]
    return values.at[tuple(place)].set(top_value)


def level_of(key, shape, split, low, largest):
    loudness = 1.0
    for axis_at, shards_of in split:
        draws = jax.random.uniform(jax.random.fold_in(jax.random.fold_in(key, 6), axis_at), (shards_of,), jnp.float32, low / len(split), largest / len(split))
        loudness = loudness * jnp.repeat(jnp.exp(draws), shape[axis_at] // shards_of).reshape((-1,) + (1,) * (len(shape) - 1 - axis_at))
    return loudness


def noise(own_key, dims, deviation, reach, split=(), kind=jnp.bfloat16):
    level = level_of(own_key, dims, split, -0.22, 0.18) if split else 1.0
    entries = jax.random.normal(own_key, dims, jnp.float32) * deviation * level
    return jnp.minimum(jnp.maximum(entries, -reach), reach).astype(kind)


def setup_inputs(seed: int = 0) -> dict:
    arg_keys = jax.random.split(jax.random.key(seed), 27)
    inputs = noise(arg_keys[0], (PAIRS, LENGTH, D), 1.0, 6.0, ((0, 8), (1, 4)), jnp.float32)
    memory = noise(arg_keys[1], (PAIRS, LENGTH, D), 1.0, 6.0, ((0, 8), (1, 4)), jnp.float32)
    group_place = jax.vmap(lambda own: jax.random.permutation(own, SEQ_PARTS))(jax.random.split(arg_keys[2], PAIRS)).reshape((PAIRS, SEQ_PARTS)).astype(jnp.int32)
    pair_mask = place_ends((jax.random.randint(arg_keys[3], (PAIRS,), 0, 4) < 1).astype(jnp.int32), jax.random.fold_in(arg_keys[3], 1), 0, 1)
    cotangent = noise(arg_keys[4], (PAIRS, LENGTH, D), 1.0, 6.0, ((0, 8), (1, 4)), jnp.float32)
    self_inward = noise(arg_keys[5], (D, 3 * D), D ** -0.5, 0.1875, ((0, 32),))
    self_outward = noise(arg_keys[6], (D, D), (D // 256) ** -0.5, 3.0, ((0, 32),))
    self_query_bias = noise(arg_keys[7], (D,), 0.5, 3.0, ((0, 32),))
    self_value_bias = noise(arg_keys[8], (D,), 0.05, 0.3125, ((0, 32),))
    self_output_bias = noise(arg_keys[9], (D,), 1.0, 6.0, ((0, 32),))
    first_gain = jnp.clip(1.0 + 0.1 * jax.random.normal(arg_keys[10], (D,), jnp.float32), 0.5, 1.5).astype(jnp.bfloat16)
    first_shift = noise(arg_keys[11], (D,), 0.5, 3.0, ((0, 32),))
    cross_query = noise(arg_keys[12], (D, D), D ** -0.5, 0.1875, ((0, 32),))
    cross_memory = noise(arg_keys[13], (D, 2 * D), D ** -0.5, 0.1875, ((0, 32),))
    cross_outward = noise(arg_keys[14], (D, D), (D // 256) ** -0.5, 3.0, ((0, 32),))
    cross_query_bias = noise(arg_keys[15], (D,), 0.5, 3.0, ((0, 32),))
    cross_value_bias = noise(arg_keys[16], (D,), 0.05, 0.3125, ((0, 32),))
    cross_output_bias = noise(arg_keys[17], (D,), 1.0, 6.0, ((0, 32),))
    second_gain = jnp.clip(1.0 + 0.1 * jax.random.normal(arg_keys[18], (D,), jnp.float32), 0.5, 1.5).astype(jnp.bfloat16)
    second_shift = noise(arg_keys[19], (D,), 0.5, 3.0, ((0, 32),))
    expand_weight = noise(arg_keys[20], (D, FF), D ** -0.5, 0.1875, ((0, 32),))
    expand_bias = noise(arg_keys[21], (FF,), 0.5, 3.0, ((0, 32),))
    reduce_weight = noise(arg_keys[22], (FF, D), (FF // 8) ** -0.5, 0.25, ((0, 32),))
    reduce_bias = noise(arg_keys[23], (D,), 1.0, 6.0, ((0, 32),))
    third_gain = jnp.clip(1.0 + 0.1 * jax.random.normal(arg_keys[24], (D,), jnp.float32), 0.5, 1.5).astype(jnp.bfloat16)
    third_shift = noise(arg_keys[25], (D,), 0.5, 3.0, ((0, 32),))
    return dict(inputs=inputs, memory=memory, group_place=group_place, pair_mask=pair_mask, cotangent=cotangent, self_inward=self_inward, self_outward=self_outward, self_query_bias=self_query_bias, self_value_bias=self_value_bias, self_output_bias=self_output_bias, first_gain=first_gain, first_shift=first_shift, cross_query=cross_query, cross_memory=cross_memory, cross_outward=cross_outward, cross_query_bias=cross_query_bias, cross_value_bias=cross_value_bias, cross_output_bias=cross_output_bias, second_gain=second_gain, second_shift=second_shift, expand_weight=expand_weight, expand_bias=expand_bias, reduce_weight=reduce_weight, reduce_bias=reduce_bias, third_gain=third_gain, third_shift=third_shift)


residual_scale = 4.16
epsilon = 1e-05
score_scale = 0.125
negative_fill = -1e+30
highest = lax.Precision.HIGHEST

@jax.custom_vjp
def low(v):
    return lax.optimization_barrier(v.astype(jnp.bfloat16)).astype(jnp.float32)

@jax.custom_vjp
def low_back(v):
    return v

def low_keep(v):
    return (low(v), None)

def low_pass(kept, grad):
    return (grad,)

def back_keep(v):
    return (v, None)

def back_low(kept, grad):
    return (low(grad),)
low.defvjp(low_keep, low_pass)
low_back.defvjp(back_keep, back_low)

def matmul(left_side, right_side):
    return jnp.dot(left_side, right_side, precision=highest, preferred_element_type=jnp.float32)

def norm_layer(values, gain_vector, shift_vector):
    middle = lax.optimization_barrier(jnp.mean(values, axis=-1, keepdims=True))
    centred = values - middle
    spread = lax.optimization_barrier(jnp.mean(centred * centred, axis=-1, keepdims=True))
    return centred * lax.rsqrt(spread + epsilon) * gain_vector + shift_vector

def gelu_tanh(values):
    return 0.5 * values * (1.0 + jnp.tanh(0.7978845608028654 * (values + 0.044715 * values * values * values)))

def head_split(values):
    return values.reshape(values.shape[0], HEADS, HEAD_DIM)

def attend(query_rows, key_rows, value_rows, allowed):
    scores = low_back(jnp.einsum('qhd,khd->hqk', head_split(query_rows), head_split(key_rows), precision=highest, preferred_element_type=jnp.float32)) * score_scale
    if allowed is not None:
        scores = jnp.where(allowed[None], scores, negative_fill)
    row_top = lax.optimization_barrier(jnp.max(scores, axis=-1, keepdims=True))
    exp_scores = jnp.exp(scores - row_top)
    probability = low(exp_scores / lax.optimization_barrier(jnp.sum(exp_scores, axis=-1, keepdims=True)))
    blended = jnp.einsum('hqk,khd->qhd', probability, head_split(value_rows), precision=highest, preferred_element_type=jnp.float32)
    return low(low_back(blended.reshape(query_rows.shape)))

def forward(inputs, memory, params, allowed):
    self_inward, self_outward, self_query_bias, self_value_bias, self_output_bias, first_gain, first_shift, cross_query, cross_memory, cross_outward, cross_query_bias, cross_value_bias, cross_output_bias, second_gain, second_shift, expand_weight, expand_bias, reduce_weight, reduce_bias, third_gain, third_shift = params
    projected = low_back(matmul(low(inputs), self_inward))
    query_rows = low(projected[:, :D] + self_query_bias)
    key_rows = low(projected[:, D:2 * D])
    value_rows = low(projected[:, 2 * D:] + self_value_bias)
    blended = attend(query_rows, key_rows, value_rows, allowed)
    branch = low_back(matmul(blended, self_outward)) + self_output_bias
    after_self = norm_layer(residual_scale * inputs + branch, first_gain, first_shift)
    cross_rows = low(low_back(matmul(low(after_self), cross_query)) + cross_query_bias)
    remembered = low_back(matmul(low(memory), cross_memory))
    blended = attend(cross_rows, low(remembered[:, :D]), low(remembered[:, D:] + cross_value_bias), None)
    branch = low_back(matmul(blended, cross_outward)) + cross_output_bias
    after_cross = norm_layer(residual_scale * after_self + branch, second_gain, second_shift)
    hidden = low(gelu_tanh(low_back(matmul(low(after_cross), expand_weight)) + expand_bias))
    branch = low_back(matmul(hidden, reduce_weight)) + reduce_bias
    return norm_layer(residual_scale * after_cross + branch, third_gain, third_shift)

def reference(inputs, memory, group_place, pair_mask, cotangent, self_inward, self_outward, self_query_bias, self_value_bias, self_output_bias, first_gain, first_shift, cross_query, cross_memory, cross_outward, cross_query_bias, cross_value_bias, cross_output_bias, second_gain, second_shift, expand_weight, expand_bias, reduce_weight, reduce_bias, third_gain, third_shift):
    params = tuple((weight.astype(jnp.float32) for weight in (self_inward, self_outward, self_query_bias, self_value_bias, self_output_bias, first_gain, first_shift, cross_query, cross_memory, cross_outward, cross_query_bias, cross_value_bias, cross_output_bias, second_gain, second_shift, expand_weight, expand_bias, reduce_weight, reduce_bias, third_gain, third_shift)))
    offsets = jnp.arange(GROUP, dtype=jnp.int32)

    def one_pair(totals, pieces):
        pair_inputs, pair_memory, place_row, keep_flag, pair_cotangent = pieces
        positions = (place_row[:, None] * GROUP + offsets[None, :]).reshape(LENGTH)
        allowed = positions[:, None] >= positions[None, :]

        def apply_layer(layer_inputs, layer_memory, layer_params):
            return forward(layer_inputs, layer_memory, layer_params, allowed)
        result, pullback = jax.vjp(apply_layer, pair_inputs, pair_memory, params)
        inputs_grad, memory_grad, param_grads = pullback(pair_cotangent * keep_flag.astype(jnp.float32))
        totals = jax.tree.map(jnp.add, totals, param_grads)
        return (totals, (result, inputs_grad, memory_grad))
    zero_grads = jax.tree.map(jnp.zeros_like, params)
    totals, (output, inputs_grad, memory_grad) = lax.scan(one_pair, zero_grads, (inputs, memory, group_place, pair_mask, cotangent))
    return (output, inputs_grad, memory_grad, totals[0], totals[1], totals[2], totals[3], totals[4], totals[5], totals[6], totals[7], totals[8], totals[9], totals[10], totals[11], totals[12], totals[13], totals[14], totals[15], totals[16], totals[17], totals[18], totals[19], totals[20])
```

```python
import functools

import jax
import jax.numpy as jnp
from jax import lax
from jax.experimental import pallas as pl
from jax.experimental.pallas import tpu as pltpu
from jax.sharding import PartitionSpec as P

HEADS = 16
HEAD_DIM = 64
PAIR = 2 * HEAD_DIM

residual_scale = 4.16
epsilon = 1e-05
score_scale = 0.125
negative_fill = -1e30
bf16 = jnp.bfloat16
f32 = jnp.float32


def norm_layer(values, gain_vector, shift_vector):
    middle = jnp.mean(values, axis=-1, keepdims=True)
    centred = values - middle
    spread = jnp.mean(centred * centred, axis=-1, keepdims=True)
    return centred * lax.rsqrt(spread + epsilon) * gain_vector + shift_vector


def gelu_tanh(values):
    return (
        0.5
        * values
        * (1.0 + jnp.tanh(0.7978845608028654 * (values + 0.044715 * values * values * values)))
    )


def dense(left_side, right_side):
    return jnp.dot(left_side, right_side, preferred_element_type=f32)


def times_transposed(left_side, right_side):
    return lax.dot_general(
        left_side, right_side, (((1,), (1,)), ((), ())), preferred_element_type=f32
    )


def transposed_times(left_side, right_side):
    return lax.dot_general(
        left_side, right_side, (((0,), (0,)), ((), ())), preferred_element_type=f32
    )


def lane_head(shape, head):
    lane = lax.broadcasted_iota(jnp.int32, shape, 1)
    return (lane < HEAD_DIM) if head == 0 else (lane >= HEAD_DIM)


def masked_scores(scores, place_ref, causal, group_len):
    if not causal:
        return scores
    blocks = scores.shape[0] // group_len
    own = place_ref[0, blocks]
    diff = lax.broadcasted_iota(jnp.int32, (group_len, group_len), 0) - lax.broadcasted_iota(
        jnp.int32, (group_len, group_len), 1
    )
    parts = []
    for block in range(blocks):
        reach = (own - place_ref[0, block]) * group_len
        part = scores[block * group_len : (block + 1) * group_len]
        parts.append(jnp.where(diff <= reach, part, negative_fill))
    return jnp.concatenate(parts, axis=0)


def attend_forward_kernel(causal, place_ref, q_ref, k_ref, v_ref, o_ref, total_ref):
    group_len = q_ref.shape[0]
    scaled = q_ref[...] * jnp.asarray(score_scale, bf16)
    keys = k_ref[...]
    values = v_ref[...]
    outs = []
    for head in range(2):
        own = jnp.where(lane_head(scaled.shape, head), scaled, jnp.zeros_like(scaled))
        scores = times_transposed(keys, own)
        scores = masked_scores(scores, place_ref, causal, group_len)
        top = jnp.max(scores, axis=0, keepdims=True)
        weights = jnp.exp(scores - top)
        total = jnp.sum(weights, axis=0, keepdims=True)
        blended = transposed_times(values, weights.astype(bf16)) / total
        outs.append(blended)
        total_ref[0, head : head + 1, :] = top + jnp.log(total)
    row = lax.broadcasted_iota(jnp.int32, outs[0].shape, 0)
    o_ref[...] = jnp.where(row < HEAD_DIM, outs[0], outs[1]).T.astype(bf16)


def attend_backward_kernel(
    causal, place_ref, q_ref, k_ref, v_ref, total_ref, g_ref, dq_ref, dk_ref, dv_ref
):
    group_len = q_ref.shape[0]
    scaled = q_ref[...] * jnp.asarray(score_scale, bf16)
    keys = k_ref[...]
    values = v_ref[...]
    grads = g_ref[...]
    dqs, dks, dvs = [], [], []
    for head in range(2):
        mine = lane_head(scaled.shape, head)
        own = jnp.where(mine, scaled, jnp.zeros_like(scaled))
        grad = jnp.where(mine, grads, jnp.zeros_like(grads))
        scores = times_transposed(keys, own)
        scores = masked_scores(scores, place_ref, causal, group_len)
        weights = jnp.exp(scores - total_ref[0, head : head + 1, :])
        dvs.append(dense(weights.astype(bf16), grad))
        dprob = times_transposed(values, grad)
        delta = jnp.sum(dprob * weights, axis=0, keepdims=True)
        dscore = (weights * (dprob - delta)).astype(bf16)
        dks.append(dense(dscore, own))
        dqs.append(transposed_times(keys, dscore))
    row = lax.broadcasted_iota(jnp.int32, dqs[0].shape, 0)
    dq_ref[...] = jnp.where(row < HEAD_DIM, dqs[0], dqs[1]).T * score_scale
    dk_ref[...] = (dks[0] + dks[1]).astype(bf16)
    dv_ref[...] = (dvs[0] + dvs[1]).astype(bf16)


def attention_specs(group_len, length):
    row = pl.BlockSpec((group_len, PAIR), lambda h: (0, h))
    context = pl.BlockSpec((length, PAIR), lambda h: (0, h))
    total = pl.BlockSpec((1, 2, group_len), lambda h: (h, 0, 0))
    place = pl.BlockSpec(memory_space=pltpu.SMEM)
    return place, row, context, total


def attend_forward(query_rows, keys, values, places, causal):
    group_len, width = query_rows.shape
    length = keys.shape[0]
    pairs = width // PAIR
    place, row, context, total = attention_specs(group_len, length)
    return pl.pallas_call(
        functools.partial(attend_forward_kernel, causal),
        grid=(pairs,),
        in_specs=[place, row, context, context],
        out_specs=[row, total],
        out_shape=[
            jax.ShapeDtypeStruct((group_len, width), bf16),
            jax.ShapeDtypeStruct((pairs, 2, group_len), f32),
        ],
        compiler_params=pltpu.CompilerParams(vmem_limit_bytes=48 * 1024 * 1024),
        cost_estimate=pl.CostEstimate(
            flops=16 * group_len * length * width,
            bytes_accessed=4 * (group_len + length) * width,
            transcendentals=HEADS * group_len * length,
        ),
    )(places, query_rows, keys, values)


def attend_backward(query_rows, keys, values, places, totals, grads, causal):
    group_len, width = query_rows.shape
    length = keys.shape[0]
    pairs = width // PAIR
    place, row, context, total = attention_specs(group_len, length)
    return pl.pallas_call(
        functools.partial(attend_backward_kernel, causal),
        grid=(pairs,),
        in_specs=[place, row, context, context, total, row],
        out_specs=[row, context, context],
        out_shape=[
            jax.ShapeDtypeStruct((group_len, width), f32),
            jax.ShapeDtypeStruct((length, width), bf16),
            jax.ShapeDtypeStruct((length, width), bf16),
        ],
        compiler_params=pltpu.CompilerParams(vmem_limit_bytes=48 * 1024 * 1024),
        cost_estimate=pl.CostEstimate(
            flops=40 * group_len * length * width,
            bytes_accessed=8 * (group_len + length) * width,
            transcendentals=HEADS * group_len * length,
        ),
    )(places, query_rows, keys, values, totals, grads)


class Grid:
    def __init__(self, mesh):
        self.dp = mesh.shape["dp"]
        depth = mesh.shape["seq"]
        core = 2 if self.dp % 2 == 0 else 1
        chips = self.dp // core
        outer = 1
        while outer * outer < chips:
            outer *= 2
        inner = chips // outer
        self.sizes = {"outer": outer, "inner": inner, "core": core, "depth": depth}
        self.strides = {"outer": inner * core, "inner": core, "core": 1}

    def index(self, dim):
        if dim == "depth":
            return lax.axis_index("seq")
        return (lax.axis_index("dp") // self.strides[dim]) % self.sizes[dim]

    def shift(self, value, dim, step):
        size = self.sizes[dim]
        if dim == "depth":
            return lax.ppermute(value, "seq", [(i, (i + step) % size) for i in range(size)])
        stride = self.strides[dim]
        pairs = []
        for device in range(self.dp):
            at = (device // stride) % size
            pairs.append((device, device + ((at + step) % size - at) * stride))
        return lax.ppermute(value, "dp", pairs)

    def steps(self, dim):
        return range(1, self.sizes[dim])

    def from_depth(self, shard):
        return [self.shift(shard, "depth", step) for step in self.steps("depth")]

    def depth_block(self, shard, pieces):
        size, me = self.sizes["depth"], self.index("depth")
        return jnp.stack(
            [lax.select_n((me - at) % size, shard, *pieces) for at in range(size)]
        )

    def from_sides(self, block):
        return (
            [self.shift(block, "inner", step) for step in self.steps("inner")],
            [self.shift(block, "outer", step) for step in self.steps("outer")],
        )

    def from_corners(self, sides):
        along_inner, along_outer = sides
        half = along_inner[0].shape[0] // 2
        top = jnp.stack([block[:half] for block in along_inner])
        bottom = jnp.stack([block[half:] for block in along_outer])
        return (
            [self.shift(top, "outer", step) for step in self.steps("outer")],
            [self.shift(bottom, "inner", step) for step in self.steps("inner")],
        )

    def swap(self, pieces):
        return jax.tree.map(lambda piece: self.shift(piece, "core", 1), pieces)

    def place(self, matrix, pieces, other):
        outer, inner, core = (self.sizes[n] for n in ("outer", "inner", "core"))
        a, b = self.index("outer"), self.index("inner")
        c = (self.index("core") + other) % core
        block, (along_inner, along_outer), (top, bottom) = pieces
        depth, half = block.shape[0], block.shape[0] // 2

        def put(matrix, piece, at_a, at_b, start):
            return lax.dynamic_update_slice(
                matrix, piece[None, None, None], (at_a % outer, at_b % inner, c, start, 0, 0)
            )

        matrix = put(matrix, block, a, b, 0)
        for j, piece in enumerate(along_inner):
            matrix = put(matrix, piece, a, b - j - 1, 0)
        for i, piece in enumerate(along_outer):
            matrix = put(matrix, piece, a - i - 1, b, 0)
        for i in range(outer - 1):
            for j in range(inner - 1):
                matrix = put(matrix, top[i][j], a - i - 1, b - j - 1, 0)
                matrix = put(matrix, bottom[j][i], a - i - 1, b - j - 1, half)
        return matrix

    def whole(self, own, others):
        block = own[0]
        shape = tuple(self.sizes[n] for n in ("outer", "inner", "core")) + block.shape
        matrix = jnp.zeros(shape, block.dtype)
        matrix = self.place(matrix, own, 0)
        if self.sizes["core"] > 1:
            matrix = self.place(matrix, others, 1)
        return matrix.reshape(-1, block.shape[-1])

    def halves(self, left_side, right_side):
        height = left_side.shape[1]
        core = self.sizes["core"]
        outer, inner, depth = self.sizes["outer"], self.sizes["inner"], self.sizes["depth"]
        block = height // (outer * inner * core)
        me = self.index("core")
        shape = (outer, inner, depth, block // depth, right_side.shape[1])
        even, odd = [
            [left_side[:, (core * j + i) * block : (core * j + i + 1) * block] for j in range(outer * inner)]
            for i in range(core)
        ]

        def part(own):
            chosen = [
                jnp.where(me == 0, *((e, o) if own else (o, e))) for e, o in zip(even, odd)
            ]
            return transposed_times(jnp.concatenate(chosen, axis=1), right_side).astype(bf16)

        return part(False).reshape(shape), part(True).reshape(shape)

    def vector_halves(self, packed):
        core = self.sizes["core"]
        outer, inner, depth = self.sizes["outer"], self.sizes["inner"], self.sizes["depth"]
        split = packed.reshape((outer, inner, core, depth) + packed.shape[1:])
        me = self.index("core")
        even, odd = split[:, :, 0], split[:, :, 1]
        return jnp.where(me == 0, odd, even).astype(bf16), jnp.where(me == 0, even, odd)

    def sums(self, terms):
        return sum(term.astype(f32) for term in terms)

    def corner_sends(self, group):
        outer, inner = self.sizes["outer"], self.sizes["inner"]
        a, b = self.index("outer"), self.index("inner")
        half = group[0][0].shape[2] // 2

        def block(terms, at_a, at_b, low, high):
            cut = [
                lax.dynamic_slice(
                    term,
                    (at_a % outer, at_b % inner, low, 0, 0),
                    (1, 1, high - low) + term.shape[3:],
                )
                for term in terms
            ]
            return self.sums(cut)[0, 0].astype(bf16)

        def joined(blocks):
            return jnp.concatenate(blocks, axis=-1) if len(blocks) > 1 else blocks[0]

        top = [
            jnp.stack(
                [
                    joined([block(terms, a + i, b + j, 0, half) for terms in group])
                    for j in self.steps("inner")
                ]
            )
            for i in self.steps("outer")
        ]
        bottom = [
            jnp.stack(
                [
                    joined([block(terms, a + i, b + j, half, 2 * half) for terms in group])
                    for i in self.steps("outer")
                ]
            )
            for j in self.steps("inner")
        ]
        return top, bottom

    def corner_moves(self, sends):
        top, bottom = sends
        return (
            [self.shift(send, "outer", step) for send, step in zip(top, self.steps("outer"))],
            [self.shift(send, "inner", step) for send, step in zip(bottom, self.steps("inner"))],
        )

    def side_sends(self, group, corners):
        outer, inner = self.sizes["outer"], self.sizes["inner"]
        a, b = self.index("outer"), self.index("inner")
        half = group[0][0].shape[2] // 2
        top, bottom = corners

        def block(at_a, at_b, low, high, extra):
            sums, start = [], 0
            for terms in group:
                columns = terms[0].shape[-1]
                cut = [
                    lax.dynamic_slice(
                        term,
                        (at_a % outer, at_b % inner, low, 0, 0),
                        (1, 1, high - low) + term.shape[3:],
                    )[0, 0]
                    for term in terms
                ]
                cut += [piece[..., start : start + columns] for piece in extra]
                sums.append(self.sums(cut).astype(bf16))
                start += columns
            return jnp.concatenate(sums, axis=-1) if len(sums) > 1 else sums[0]

        to_inner = [
            jnp.concatenate(
                [
                    block(a, b + j, 0, half, [piece[j - 1] for piece in top]),
                    block(a, b + j, half, 2 * half, []),
                ]
            )
            for j in self.steps("inner")
        ]
        to_outer = [
            jnp.concatenate(
                [
                    block(a + i, b, 0, half, []),
                    block(a + i, b, half, 2 * half, [piece[i - 1] for piece in bottom]),
                ]
            )
            for i in self.steps("outer")
        ]
        return to_inner, to_outer

    def side_moves(self, sends):
        to_inner, to_outer = sends
        return [self.shift(send, "inner", step) for send, step in zip(to_inner, self.steps("inner"))] + [
            self.shift(send, "outer", step) for send, step in zip(to_outer, self.steps("outer"))
        ]

    def chip_terms(self, group, sides):
        a, b = self.index("outer"), self.index("inner")
        out, start = [], 0
        for terms in group:
            columns = terms[0].shape[-1]
            own = [
                lax.dynamic_slice(term, (a, b, 0, 0, 0), (1, 1) + term.shape[2:])[0, 0]
                for term in terms
            ]
            out.append(own + [piece[..., start : start + columns] for piece in sides])
            start += columns
        return out

    def depth_sends(self, group):
        size, me = self.sizes["depth"], self.index("depth")
        sends = []
        for step in self.steps("depth"):
            sums = [
                self.sums(
                    [
                        lax.dynamic_index_in_dim(term, (me + step) % size, 0, keepdims=False)
                        for term in terms
                    ]
                ).astype(bf16)
                for terms in group
            ]
            sends.append(jnp.concatenate(sums, axis=-1) if len(sums) > 1 else sums[0])
        return sends

    def depth_moves(self, sends):
        return [self.shift(send, "depth", step) for send, step in zip(sends, self.steps("depth"))]

    def shares(self, group, received):
        me = self.index("depth")
        out, start = [], 0
        for terms in group:
            columns = terms[0].shape[-1]
            own = [lax.dynamic_index_in_dim(term, me, 0, keepdims=False) for term in terms]
            out.append(self.sums(own + [piece[..., start : start + columns] for piece in received]))
            start += columns
        return out


def together(*values):
    return lax.optimization_barrier(values)


def local(grid, *args):
    (
        inputs,
        memory,
        group_place,
        pair_mask,
        cotangent,
        self_inward,
        self_outward,
        self_query_bias,
        self_value_bias,
        self_output_bias,
        first_gain,
        first_shift,
        cross_query,
        cross_memory,
        cross_outward,
        cross_query_bias,
        cross_value_bias,
        cross_output_bias,
        second_gain,
        second_shift,
        expand_weight,
        expand_bias,
        reduce_weight,
        reduce_bias,
        third_gain,
        third_shift,
    ) = args
    pair_count, group_len, width = inputs.shape
    rows_in = inputs.reshape(group_len, width)
    rows_low = rows_in.astype(bf16)
    memory_low = memory.reshape(group_len, width).astype(bf16)

    vectors = (
        self_query_bias,
        self_value_bias,
        self_output_bias,
        first_gain,
        first_shift,
        cross_query_bias,
        cross_value_bias,
        cross_output_bias,
        second_gain,
        second_shift,
        expand_bias,
        reduce_bias,
        third_gain,
        third_shift,
    )
    lengths = [vector.shape[0] for vector in vectors]
    starts = [sum(lengths[:i]) for i in range(len(lengths))]
    rows = self_inward.shape[0]
    spread = sum(lengths) // rows
    packed = jnp.concatenate(vectors).reshape(rows, spread)
    packed = jnp.pad(packed, ((0, 0), (0, 128 - spread)))
    places = jnp.concatenate(
        [
            group_place.reshape(1, -1),
            lax.dynamic_slice_in_dim(group_place, lax.axis_index("seq"), 1, axis=1),
        ],
        axis=1,
    )

    all_low = lax.all_gather(rows_low, "seq", axis=0, tiled=True)
    one = jnp.concatenate([self_inward, packed], axis=1)
    two = jnp.concatenate([self_outward, cross_query, cross_memory, cross_outward], axis=1)

    one_depth = grid.from_depth(one)
    one_depth, two, memory_low = together(one_depth, two, memory_low)

    all_memory = lax.all_gather(memory_low, "seq", axis=0, tiled=True)
    one_block = grid.depth_block(one, one_depth)
    one_sides = grid.from_sides(one_block)
    two_depth = grid.from_depth(two)
    one_block_other = grid.swap(one_block)
    one_block_other, one_sides = together(one_block_other, one_sides)

    one_corners = grid.from_corners(one_sides)
    one_sides_other = grid.swap(one_sides)
    one_corners, two_depth, expand_weight = together(one_corners, two_depth, expand_weight)

    one_corners_other = grid.swap(one_corners)
    two_block = grid.depth_block(two, two_depth)
    two_sides = grid.from_sides(two_block)
    expand_depth = grid.from_depth(expand_weight)
    one_all = grid.whole(
        (one_block, one_sides, one_corners),
        (one_block_other, one_sides_other, one_corners_other),
    )
    devices = width // rows
    packed = one_all[:, 3 * width : 3 * width + spread].reshape(devices, rows * spread)
    (
        self_query_bias,
        self_value_bias,
        self_output_bias,
        first_gain,
        first_shift,
        cross_query_bias,
        cross_value_bias,
        cross_output_bias,
        second_gain,
        second_shift,
        expand_bias,
        reduce_bias,
        third_gain,
        third_shift,
    ) = [
        packed[:, start : start + length].reshape(-1).astype(f32)
        for start, length in zip(starts, lengths)
    ]


    self_query, self_key, self_value = (
        one_all[:, :width],
        one_all[:, width : 2 * width],
        one_all[:, 2 * width : 3 * width],
    )
    query_self = (dense(rows_low, self_query) + self_query_bias).astype(bf16)
    keys_self = dense(all_low, self_key).astype(bf16)
    values_self = (dense(all_low, self_value) + self_value_bias).astype(bf16)
    two_block_other = grid.swap(two_block)
    two_sides, two_block_other, expand_depth, query_self, reduce_weight = together(
        two_sides, two_block_other, expand_depth, query_self, reduce_weight
    )

    two_corners = grid.from_corners(two_sides)
    two_sides_other = grid.swap(two_sides)
    expand_block = grid.depth_block(expand_weight, expand_depth)
    expand_sides = grid.from_sides(expand_block)
    expand_block_other = grid.swap(expand_block)
    reduce_depth = grid.from_depth(reduce_weight)
    blended_self, total_self = attend_forward(query_self, keys_self, values_self, places, True)
    blended_self, two_corners, two_sides_other = together(
        blended_self, two_corners, two_sides_other
    )

    two_corners_other = grid.swap(two_corners)
    two_all = grid.whole(
        (two_block, two_sides, two_corners),
        (two_block_other, two_sides_other, two_corners_other),
    )
    self_outward, cross_query, cross_key, cross_value, cross_outward = [
        two_all[:, i * width : (i + 1) * width] for i in range(5)
    ]
    pre_first = residual_scale * rows_in + dense(blended_self, self_outward) + self_output_bias
    after_self = norm_layer(pre_first, first_gain, first_shift)
    after_self_low = after_self.astype(bf16)
    query_cross = (dense(after_self_low, cross_query) + cross_query_bias).astype(bf16)
    keys_cross = dense(all_memory, cross_key).astype(bf16)
    values_cross = (dense(all_memory, cross_value) + cross_value_bias).astype(bf16)
    query_cross, expand_sides, expand_block_other, reduce_depth = together(
        query_cross, expand_sides, expand_block_other, reduce_depth
    )

    expand_corners = grid.from_corners(expand_sides)
    expand_sides_other = grid.swap(expand_sides)
    reduce_block = grid.depth_block(reduce_weight, reduce_depth)
    reduce_sides = grid.from_sides(reduce_block)
    reduce_block_other = grid.swap(reduce_block)
    blended_cross, total_cross = attend_forward(
        query_cross, keys_cross, values_cross, places, False
    )
    blended_cross, expand_corners, expand_sides_other = together(
        blended_cross, expand_corners, expand_sides_other
    )

    expand_corners_other = grid.swap(expand_corners)
    expand_all = grid.whole(
        (expand_block, expand_sides, expand_corners),
        (expand_block_other, expand_sides_other, expand_corners_other),
    )
    pre_second = (
        residual_scale * after_self + dense(blended_cross, cross_outward) + cross_output_bias
    )
    after_cross = norm_layer(pre_second, second_gain, second_shift)
    cross_low = after_cross.astype(bf16)
    cross_low, reduce_sides, reduce_block_other = together(
        cross_low, reduce_sides, reduce_block_other
    )

    reduce_corners = grid.from_corners(reduce_sides)
    reduce_sides_other = grid.swap(reduce_sides)
    expanded = dense(cross_low, expand_all) + expand_bias
    hidden = gelu_tanh(expanded).astype(bf16)
    hidden, reduce_corners, reduce_sides_other = together(
        hidden, reduce_corners, reduce_sides_other
    )

    reduce_corners_other = grid.swap(reduce_corners)
    reduce_all = grid.whole(
        (reduce_block, reduce_sides, reduce_corners),
        (reduce_block_other, reduce_sides_other, reduce_corners_other),
    )
    pre_third = residual_scale * after_cross + dense(hidden, reduce_all) + reduce_bias
    result = norm_layer(pre_third, third_gain, third_shift)

    grad_out = cotangent.reshape(group_len, width) * pair_mask.astype(f32)[0]
    norm_back = jax.vjp(norm_layer, pre_third, third_gain, third_shift)[1]
    grad_third, third_gain_grad, third_shift_grad = norm_back(grad_out)
    reduce_bias_grad = jnp.sum(grad_third, axis=0)
    low_third = grad_third.astype(bf16)
    reduce_sent, reduce_kept = grid.halves(hidden, low_third)
    reduce_sent, low_third = together(reduce_sent, low_third)

    reduce_got = grid.swap(reduce_sent)
    grad_hidden = times_transposed(low_third, reduce_all)
    grad_expanded = jax.vjp(gelu_tanh, expanded)[1](grad_hidden)[0]
    expand_bias_grad = jnp.sum(grad_expanded, axis=0)
    expanded_low = grad_expanded.astype(bf16)
    expanded_low, reduce_got, reduce_kept = together(expanded_low, reduce_got, reduce_kept)

    reduce_group = [[reduce_kept, reduce_got]]
    reduce_sends = grid.corner_sends(reduce_group)
    reduce_sends, expanded_low = together(reduce_sends, expanded_low)
    reduce_corners = grid.corner_moves(reduce_sends)
    expand_sent, expand_kept = grid.halves(cross_low, expanded_low)
    expand_sent, expanded_low = together(expand_sent, expanded_low)
    expand_got = grid.swap(expand_sent)
    grad_cross = residual_scale * grad_third + times_transposed(expanded_low, expand_all)
    norm_back = jax.vjp(norm_layer, pre_second, second_gain, second_shift)[1]
    grad_second, second_gain_grad, second_shift_grad = norm_back(grad_cross)
    cross_output_bias_grad = jnp.sum(grad_second, axis=0)
    second_low = grad_second.astype(bf16)
    grad_blended = times_transposed(second_low, cross_outward).astype(bf16)
    out_sent, out_kept = grid.halves(blended_cross, second_low)
    grad_blended, reduce_corners, expand_got, expand_kept, out_sent, out_kept = together(
        grad_blended, reduce_corners, expand_got, expand_kept, out_sent, out_kept
    )

    reduce_sends = grid.side_sends(reduce_group, reduce_corners)
    expand_group = [[expand_kept, expand_got]]
    expand_sends = grid.corner_sends(expand_group)
    reduce_sends, expand_sends, grad_blended = together(reduce_sends, expand_sends, grad_blended)
    reduce_sides = grid.side_moves(reduce_sends)
    expand_corners = grid.corner_moves(expand_sends)
    out_got = grid.swap(out_sent)
    grad_query_cross, grad_key_cross, grad_value_cross = attend_backward(
        query_cross, keys_cross, values_cross, places, total_cross, grad_blended, False
    )
    (
        grad_query_cross,
        grad_key_cross,
        grad_value_cross,
        reduce_sides,
        expand_corners,
        out_got,
    ) = together(
        grad_query_cross, grad_key_cross, grad_value_cross, reduce_sides, expand_corners, out_got
    )

    reduce_terms = grid.chip_terms(reduce_group, reduce_sides)
    reduce_sends = grid.depth_sends(reduce_terms)
    expand_sends = grid.side_sends(expand_group, expand_corners)
    reduce_sends, expand_sends, grad_query_cross, grad_key_cross, grad_value_cross = together(
        reduce_sends, expand_sends, grad_query_cross, grad_key_cross, grad_value_cross
    )
    expand_sides = grid.side_moves(expand_sends)
    reduce_depths = grid.depth_moves(reduce_sends)
    cross_value_bias_grad = jnp.sum(grad_value_cross.astype(f32), axis=0)
    cross_query_bias_grad = jnp.sum(grad_query_cross, axis=0)
    query_cross_low = grad_query_cross.astype(bf16)
    query_sent, query_kept = grid.halves(after_self_low, query_cross_low)
    key_sent, key_kept = grid.halves(all_memory, grad_key_cross)
    value_sent, value_kept = grid.halves(all_memory, grad_value_cross)
    query_sent, key_sent, value_sent, query_cross_low = together(
        query_sent, key_sent, value_sent, query_cross_low
    )
    query_got, key_got, value_got = grid.swap((query_sent, key_sent, value_sent))
    grad_self = residual_scale * grad_second + times_transposed(query_cross_low, cross_query)
    norm_back = jax.vjp(norm_layer, pre_first, first_gain, first_shift)[1]
    grad_first, first_gain_grad, first_shift_grad = norm_back(grad_self)
    self_output_bias_grad = jnp.sum(grad_first, axis=0)
    first_low = grad_first.astype(bf16)
    cross_group = [
        [out_kept, out_got],
        [query_kept, query_got],
        [key_kept, key_got],
        [value_kept, value_got],
    ]
    first_low, cross_group = together(first_low, cross_group)

    cross_sends = grid.corner_sends(cross_group)
    cross_sends, first_low = together(cross_sends, first_low)
    cross_corners = grid.corner_moves(cross_sends)
    grad_blended = times_transposed(first_low, self_outward).astype(bf16)
    outward_sent, outward_kept = grid.halves(blended_self, first_low)
    memory_part = times_transposed(grad_key_cross, cross_key) + times_transposed(
        grad_value_cross, cross_value
    )
    (
        grad_blended,
        outward_sent,
        outward_kept,
        memory_part,
        expand_sides,
        reduce_depths,
        cross_corners,
    ) = together(
        grad_blended,
        outward_sent,
        outward_kept,
        memory_part.astype(bf16),
        expand_sides,
        reduce_depths,
        cross_corners,
    )

    memory_grad = lax.psum_scatter(memory_part, "seq", scatter_dimension=0, tiled=True)
    expand_terms = grid.chip_terms(expand_group, expand_sides)
    expand_sends = grid.depth_sends(expand_terms)
    cross_sends = grid.side_sends(cross_group, cross_corners)
    expand_sends, cross_sends, grad_blended = together(expand_sends, cross_sends, grad_blended)
    cross_sides = grid.side_moves(cross_sends)
    expand_depths = grid.depth_moves(expand_sends)
    outward_got = grid.swap(outward_sent)
    (reduce_grad,) = grid.shares(reduce_terms, reduce_depths)
    grad_query_self, grad_key_self, grad_value_self = attend_backward(
        query_self, keys_self, values_self, places, total_self, grad_blended, True
    )
    self_query_bias_grad = jnp.sum(grad_query_self, axis=0)
    self_value_bias_grad = jnp.sum(grad_value_self.astype(f32), axis=0)
    query_self_low = grad_query_self.astype(bf16)
    query_sent, query_kept = grid.halves(rows_low, query_self_low)
    key_sent, key_kept = grid.halves(all_low, grad_key_self)
    value_sent, value_kept = grid.halves(all_low, grad_value_self)
    vector_grads = (
        self_query_bias_grad,
        self_value_bias_grad,
        self_output_bias_grad,
        first_gain_grad,
        first_shift_grad,
        cross_query_bias_grad,
        cross_value_bias_grad,
        cross_output_bias_grad,
        second_gain_grad,
        second_shift_grad,
        expand_bias_grad,
        reduce_bias_grad,
        third_gain_grad,
        third_shift_grad,
    )
    vector_grads = jnp.concatenate([grad.reshape(devices, -1) for grad in vector_grads], axis=1)
    vector_grads = vector_grads.reshape(devices, rows, spread)
    vector_grads = jnp.pad(vector_grads, ((0, 0), (0, 0), (0, 128 - spread)))
    vector_sent, vector_kept = grid.vector_halves(vector_grads)
    query_sent, key_sent, value_sent, vector_sent, grad_key_self, grad_value_self = together(
        query_sent, key_sent, value_sent, vector_sent, grad_key_self, grad_value_self
    )
    query_got, key_got, value_got, vector_got = grid.swap(
        (query_sent, key_sent, value_sent, vector_sent)
    )
    inputs_part = times_transposed(grad_key_self, self_key) + times_transposed(
        grad_value_self, self_value
    )
    self_group = [
        [outward_kept, outward_got],
        [query_kept, query_got],
        [key_kept, key_got],
        [value_kept, value_got],
        [vector_kept, vector_got],
    ]
    self_group, inputs_part, cross_sides, expand_depths = together(
        self_group, inputs_part.astype(bf16), cross_sides, expand_depths
    )

    inputs_grad = lax.psum_scatter(inputs_part, "seq", scatter_dimension=0, tiled=True)
    self_sends = grid.corner_sends(self_group)
    cross_terms = grid.chip_terms(cross_group, cross_sides)
    cross_sends = grid.depth_sends(cross_terms)
    self_sends, cross_sends, query_self_low = together(self_sends, cross_sends, query_self_low)
    self_corners = grid.corner_moves(self_sends)
    cross_depths = grid.depth_moves(cross_sends)
    inputs_base = residual_scale * grad_first + times_transposed(query_self_low, self_query)
    (expand_grad,) = grid.shares(expand_terms, expand_depths)
    inputs_base, self_corners = together(inputs_base, self_corners)

    self_sends = grid.side_sends(self_group, self_corners)
    self_sides = grid.side_moves(self_sends)
    self_sides, cross_depths = together(self_sides, cross_depths)

    self_terms = grid.chip_terms(self_group, self_sides)
    self_sends = grid.depth_sends(self_terms)
    self_depths = grid.depth_moves(self_sends)
    cross_out_grad, cross_query_grad, cross_key_grad, cross_value_grad = grid.shares(
        cross_terms, cross_depths
    )
    inputs_grad = inputs_base + inputs_grad.astype(f32)
    memory_grad = memory_grad.astype(f32)
    self_out_grad, self_query_grad, self_key_grad, self_value_grad, share = grid.shares(
        self_terms, self_depths
    )
    share = share[:, :spread].reshape(-1)
    (
        self_query_bias_grad,
        self_value_bias_grad,
        self_output_bias_grad,
        first_gain_grad,
        first_shift_grad,
        cross_query_bias_grad,
        cross_value_bias_grad,
        cross_output_bias_grad,
        second_gain_grad,
        second_shift_grad,
        expand_bias_grad,
        reduce_bias_grad,
        third_gain_grad,
        third_shift_grad,
    ) = [share[start : start + length] for start, length in zip(starts, lengths)]


    return (
        result.reshape(pair_count, group_len, width),
        inputs_grad.reshape(pair_count, group_len, width),
        memory_grad.reshape(pair_count, group_len, width),
        jnp.concatenate([self_query_grad, self_key_grad, self_value_grad], axis=1),
        self_out_grad,
        self_query_bias_grad,
        self_value_bias_grad,
        self_output_bias_grad,
        first_gain_grad,
        first_shift_grad,
        cross_query_grad,
        jnp.concatenate([cross_key_grad, cross_value_grad], axis=1),
        cross_out_grad,
        cross_query_bias_grad,
        cross_value_bias_grad,
        cross_output_bias_grad,
        second_gain_grad,
        second_shift_grad,
        expand_grad,
        expand_bias_grad,
        reduce_grad,
        reduce_bias_grad,
        third_gain_grad,
        third_shift_grad,
    )


def solution(mesh):
    rows = P(("dp", "seq"), None)
    vector = P(("dp", "seq"))
    tokens = P("dp", "seq", None)
    in_specs = (
        (tokens, tokens, P("dp", None), P("dp"), tokens)
        + (rows, rows)
        + (vector,) * 5
        + (rows,) * 3
        + (vector,) * 5
        + (rows, vector, rows)
        + (vector,) * 3
    )
    out_specs = (
        (tokens,) * 3
        + (rows, rows)
        + (vector,) * 5
        + (rows,) * 3
        + (vector,) * 5
        + (rows, vector, rows)
        + (vector,) * 3
    )
    return jax.shard_map(
        functools.partial(local, Grid(mesh)),
        mesh=mesh,
        in_specs=in_specs,
        out_specs=out_specs,
        check_vma=False,
    )
```

```python
import functools

import jax
import jax.numpy as jnp
from jax import lax
from jax.experimental import pallas as pl
from jax.experimental.pallas import tpu as pltpu
from jax.sharding import PartitionSpec as P

HEADS = 16
HEAD_DIM = 64
PAIR = 2 * HEAD_DIM

residual_scale = 4.16
epsilon = 1e-05
score_scale = 0.125
negative_fill = -1e30
bf16 = jnp.bfloat16
f32 = jnp.float32


def norm_layer(values, gain_vector, shift_vector):
    middle = jnp.mean(values, axis=-1, keepdims=True)
    centred = values - middle
    spread = jnp.mean(centred * centred, axis=-1, keepdims=True)
    return centred * lax.rsqrt(spread + epsilon) * gain_vector + shift_vector


def gelu_tanh(values):
    return (
        0.5
        * values
        * (1.0 + jnp.tanh(0.7978845608028654 * (values + 0.044715 * values * values * values)))
    )


def dense(left_side, right_side):
    return jnp.dot(left_side, right_side, preferred_element_type=f32)


def times_transposed(left_side, right_side):
    return lax.dot_general(
        left_side, right_side, (((1,), (1,)), ((), ())), preferred_element_type=f32
    )


def transposed_times(left_side, right_side):
    return lax.dot_general(
        left_side, right_side, (((0,), (0,)), ((), ())), preferred_element_type=f32
    )


def lane_head(shape, head):
    lane = lax.broadcasted_iota(jnp.int32, shape, 1)
    return (lane < HEAD_DIM) if head == 0 else (lane >= HEAD_DIM)


def masked_scores(scores, place_ref, causal, group_len):
    if not causal:
        return scores
    blocks = scores.shape[0] // group_len
    own = place_ref[0, blocks]
    diff = lax.broadcasted_iota(jnp.int32, (group_len, group_len), 0) - lax.broadcasted_iota(
        jnp.int32, (group_len, group_len), 1
    )
    parts = []
    for block in range(blocks):
        reach = (own - place_ref[0, block]) * group_len
        part = scores[block * group_len : (block + 1) * group_len]
        parts.append(jnp.where(diff <= reach, part, negative_fill))
    return jnp.concatenate(parts, axis=0)


def attend_forward_kernel(causal, place_ref, q_ref, k_ref, v_ref, o_ref, total_ref):
    group_len = q_ref.shape[0]
    scaled = q_ref[...] * jnp.asarray(score_scale, bf16)
    keys = k_ref[...]
    values = v_ref[...]
    scores, outs = [], []
    for head in range(2):
        own = jnp.where(lane_head(scaled.shape, head), scaled, jnp.zeros_like(scaled))
        scores.append(times_transposed(keys, own))
    for head in range(2):
        here = masked_scores(scores[head], place_ref, causal, group_len)
        top = jnp.max(here, axis=0, keepdims=True)
        weights = jnp.exp(here - top)
        total = jnp.sum(weights, axis=0, keepdims=True)
        blended = transposed_times(values, weights.astype(bf16)) / total
        outs.append(blended)
        total_ref[0, head : head + 1, :] = top + jnp.log(total)
    row = lax.broadcasted_iota(jnp.int32, outs[0].shape, 0)
    o_ref[...] = jnp.where(row < HEAD_DIM, outs[0], outs[1]).T.astype(bf16)


def attend_backward_kernel(
    causal, place_ref, q_ref, k_ref, v_ref, total_ref, g_ref, dq_ref, dkv_ref, held, sems
):
    group_len = q_ref.shape[0]
    scaled = q_ref[...] * jnp.asarray(score_scale, bf16)
    keys = k_ref[...]
    values = v_ref[...]
    grads = g_ref[...]
    dqs, dks, dvs = [], [], []
    owns, masked, scores, dprobs = [], [], [], []
    for head in range(2):
        mine = lane_head(scaled.shape, head)
        owns.append(jnp.where(mine, scaled, jnp.zeros_like(scaled)))
        masked.append(jnp.where(mine, grads, jnp.zeros_like(grads)))
        scores.append(times_transposed(keys, owns[head]))
        dprobs.append(times_transposed(values, masked[head]))
    for head in range(2):
        here = masked_scores(scores[head], place_ref, causal, group_len)
        weights = jnp.exp(here - total_ref[0, head : head + 1, :])
        dvs.append(dense(weights.astype(bf16), masked[head]))
        dprob = dprobs[head]
        delta = jnp.sum(dprob * weights, axis=0, keepdims=True)
        dscore = (weights * (dprob - delta)).astype(bf16)
        dks.append(dense(dscore, owns[head]))
        dqs.append(transposed_times(keys, dscore))
    row = lax.broadcasted_iota(jnp.int32, dqs[0].shape, 0)
    dq_ref[...] = jnp.where(row < HEAD_DIM, dqs[0], dqs[1]).T * score_scale
    step, steps = pl.program_id(0), pl.num_programs(0)
    slot = lax.rem(step, 2)
    width = dkv_ref.shape[1] // 2

    def moves(at, slot):
        return [
            pltpu.make_async_copy(
                held.at[slot, part],
                dkv_ref.at[:, pl.ds(pl.multiple_of(part * width + at * PAIR, PAIR), PAIR)],
                sems.at[slot, part],
            )
            for part in range(2)
        ]

    @pl.when(step >= 2)
    def _():
        for move in moves(step - 2, slot):
            move.wait()

    held[slot, 0] = (dks[0] + dks[1]).astype(bf16)
    held[slot, 1] = (dvs[0] + dvs[1]).astype(bf16)
    for move in moves(step, slot):
        move.start()

    @pl.when(step == steps - 1)
    def _():
        for move in moves(step - 1, 1 - slot):
            move.wait()
        for move in moves(step, slot):
            move.wait()


def attention_specs(group_len, length, pairs):
    row = pl.BlockSpec((group_len, PAIR), lambda h: (0, h))
    keys = pl.BlockSpec((length, PAIR), lambda h: (0, h))
    values = pl.BlockSpec((length, PAIR), lambda h: (0, h + pairs))
    total = pl.BlockSpec((1, 2, group_len), lambda h: (h, 0, 0))
    place = pl.BlockSpec(memory_space=pltpu.SMEM)
    return place, row, keys, values, total


FREE = pl.CostEstimate(flops=1, bytes_accessed=1, transcendentals=0)
ROOM = pltpu.CompilerParams(vmem_limit_bytes=24 * 1024 * 1024)
WIDE_ROOM = pltpu.CompilerParams(vmem_limit_bytes=48 * 1024 * 1024)


def attend_forward(query_rows, context_rows, places, causal):
    group_len, width = query_rows.shape
    length = context_rows.shape[0]
    pairs = width // PAIR
    place, row, keys, values, total = attention_specs(group_len, length, pairs)
    return pl.pallas_call(
        functools.partial(attend_forward_kernel, causal),
        grid=(pairs,),
        in_specs=[place, row, keys, values],
        out_specs=[row, total],
        out_shape=[
            jax.ShapeDtypeStruct((group_len, width), bf16),
            jax.ShapeDtypeStruct((pairs, 2, group_len), f32),
        ],
        compiler_params=ROOM,
        cost_estimate=FREE,
    )(places, query_rows, context_rows, context_rows)


def attend_backward(query_rows, context_rows, places, totals, grads, causal):
    group_len, width = query_rows.shape
    length = context_rows.shape[0]
    pairs = width // PAIR
    place, row, keys, values, total = attention_specs(group_len, length, pairs)
    return pl.pallas_call(
        functools.partial(attend_backward_kernel, causal),
        grid=(pairs,),
        in_specs=[place, row, keys, values, total, row],
        out_specs=[row, pl.BlockSpec(memory_space=pl.ANY)],
        out_shape=[
            jax.ShapeDtypeStruct((group_len, width), f32),
            jax.ShapeDtypeStruct((length, 2 * width), bf16),
        ],
        scratch_shapes=[
            pltpu.VMEM((2, 2, length, PAIR), bf16),
            pltpu.SemaphoreType.DMA((2, 2)),
        ],
        compiler_params=WIDE_ROOM,
        cost_estimate=FREE,
    )(places, query_rows, context_rows, context_rows, totals, grads)


def feed_forward_kernel(x_ref, e_ref, r_ref, b_ref, expanded_ref, hidden_ref, out_ref):
    step = pl.program_id(0)
    wide = b_ref.shape[-1]
    expanded = dense(x_ref[...], e_ref[...].reshape(-1, wide)) + b_ref[...]
    expanded_ref[...] = expanded
    hidden = gelu_tanh(expanded).astype(bf16)
    hidden_ref[...] = hidden
    part = dense(hidden, r_ref[...].reshape(wide, -1))

    @pl.when(step == 0)
    def _():
        out_ref[...] = part

    @pl.when(step > 0)
    def _():
        out_ref[...] += part


def feed_backward_kernel(g_ref, e_ref, r_ref, expanded_ref, low_ref, bias_ref, out_ref):
    step = pl.program_id(0)
    wide = low_ref.shape[-1]
    grad_hidden = times_transposed(g_ref[...], r_ref[...].reshape(wide, -1))
    u = expanded_ref[...]
    square = u * u
    bent = jnp.tanh(0.7978845608028654 * (u + 0.044715 * square * u))
    slope = 0.5 * (1.0 + bent) + 0.5 * u * (1.0 - bent * bent) * (
        0.7978845608028654 * (1.0 + 3.0 * 0.044715 * square)
    )
    grad = grad_hidden * slope
    bias_ref[...] = jnp.sum(grad, axis=0, keepdims=True)
    low = grad.astype(bf16)
    low_ref[...] = low
    part = times_transposed(low, e_ref[...].reshape(-1, wide))

    @pl.when(step == 0)
    def _():
        out_ref[...] = part

    @pl.when(step > 0)
    def _():
        out_ref[...] += part


def feed_specs(count, width, start, each):
    return (
        pl.BlockSpec((count, width), lambda j: (0, 0)),
        pl.BlockSpec((width, each), lambda j: (0, j + start // each)),
        pl.BlockSpec((each, width), lambda j: (j, 0)),
        pl.BlockSpec((count, each), lambda j: (0, j)),
        pl.BlockSpec((1, each), lambda j: (0, j)),
    )


def feed_forward(rows, expand_all, start, reduce_all, bias):
    count, width = rows.shape
    wide = reduce_all.shape[0]
    each = wide // 8
    whole, first, second, part, line = feed_specs(count, width, start, each)
    return pl.pallas_call(
        feed_forward_kernel,
        grid=(wide // each,),
        in_specs=[whole, first, second, line],
        out_specs=[part, part, whole],
        out_shape=[
            jax.ShapeDtypeStruct((count, wide), f32),
            jax.ShapeDtypeStruct((count, wide), bf16),
            jax.ShapeDtypeStruct((count, width), f32),
        ],
        compiler_params=WIDE_ROOM,
        cost_estimate=FREE,
    )(rows, expand_all, reduce_all, bias.reshape(1, -1))


def feed_backward(grads, expand_all, start, reduce_all, expanded):
    count, width = grads.shape
    wide = reduce_all.shape[0]
    each = wide // 8
    whole, first, second, part, line = feed_specs(count, width, start, each)
    return pl.pallas_call(
        feed_backward_kernel,
        grid=(wide // each,),
        in_specs=[whole, first, second, part],
        out_specs=[part, line, whole],
        out_shape=[
            jax.ShapeDtypeStruct((count, wide), bf16),
            jax.ShapeDtypeStruct((1, wide), f32),
            jax.ShapeDtypeStruct((count, width), f32),
        ],
        compiler_params=WIDE_ROOM,
        cost_estimate=FREE,
    )(grads, expand_all, reduce_all, expanded)


class Grid:
    def __init__(self, mesh):
        self.dp = mesh.shape["dp"]
        depth = mesh.shape["seq"]
        core = 2 if self.dp % 2 == 0 else 1
        chips = self.dp // core
        outer = 1
        while outer * outer < chips:
            outer *= 2
        inner = chips // outer
        self.sizes = {"outer": outer, "inner": inner, "core": core, "depth": depth}
        self.strides = {"outer": inner * core, "inner": core, "core": 1}

    def index(self, dim):
        if dim == "depth":
            return lax.axis_index("seq")
        return (lax.axis_index("dp") // self.strides[dim]) % self.sizes[dim]

    def shift(self, value, dim, step):
        size = self.sizes[dim]
        if dim == "depth":
            return lax.ppermute(value, "seq", [(i, (i + step) % size) for i in range(size)])
        stride = self.strides[dim]
        pairs = []
        for device in range(self.dp):
            at = (device // stride) % size
            pairs.append((device, device + ((at + step) % size - at) * stride))
        return lax.ppermute(value, "dp", pairs)

    def steps(self, dim):
        return range(1, self.sizes[dim])

    def from_depth(self, shard):
        return [self.shift(shard, "depth", step) for step in self.steps("depth")]

    def depth_block(self, shard, pieces):
        size, me = self.sizes["depth"], self.index("depth")
        return jnp.stack(
            [lax.select_n((me - at) % size, shard, *pieces) for at in range(size)]
        )

    def from_sides(self, block):
        return (
            [self.shift(block, "inner", step) for step in self.steps("inner")],
            [self.shift(block, "outer", step) for step in self.steps("outer")],
        )

    def from_corners(self, sides):
        along_inner, along_outer = sides
        half = along_inner[0].shape[0] // 2
        top = jnp.stack([block[:half] for block in along_inner])
        bottom = jnp.stack([block[half:] for block in along_outer])
        return (
            [self.shift(top, "outer", step) for step in self.steps("outer")],
            [self.shift(bottom, "inner", step) for step in self.steps("inner")],
        )

    def swap(self, pieces):
        return jax.tree.map(lambda piece: self.shift(piece, "core", 1), pieces)

    def whole(self, own, others):
        outer, inner, core = (self.sizes[n] for n in ("outer", "inner", "core"))
        each, columns = own[0].shape[-2], own[0].shape[-1]
        height = self.sizes["depth"] * each
        half = height // 2
        pieces, places = [], []

        def add(piece, back_a, back_b, other, start):
            pieces.append(piece.reshape(-1, columns))
            places.append((back_a, back_b, other, start))

        for other, (block, (along_inner, along_outer), (top, bottom)) in enumerate([own, others]):
            add(block, 0, 0, other, 0)
            for j, piece in enumerate(along_inner):
                add(piece, 0, j + 1, other, 0)
            for i, piece in enumerate(along_outer):
                add(piece, i + 1, 0, other, 0)
            for i in range(outer - 1):
                for j in range(inner - 1):
                    add(top[i][j], i + 1, j + 1, other, 0)
                    add(bottom[j][i], i + 1, j + 1, other, half)

        def kernel(*refs):
            out, sems = refs[len(pieces)], refs[len(pieces) + 1]
            device = lax.axis_index("dp")
            a = device // self.strides["outer"]
            b = lax.rem(device // self.strides["inner"], inner)
            c = lax.rem(device, core)
            copies = []
            for at, (ref, (back_a, back_b, other, start)) in enumerate(zip(refs, places)):
                to_a = lax.rem(a + (outer - back_a), outer)
                to_b = lax.rem(b + (inner - back_b), inner)
                to_c = lax.rem(c + other, core)
                index = (to_a * inner + to_b) * core + to_c
                copies.append(
                    pltpu.make_async_copy(
                        ref, out.at[index, pl.ds(start, ref.shape[0])], sems.at[at]
                    )
                )
            for copy in copies:
                copy.start()
            for copy in copies:
                copy.wait()

        anywhere = pl.BlockSpec(memory_space=pl.ANY)
        matrix = pl.pallas_call(
            kernel,
            in_specs=[anywhere] * len(pieces),
            out_specs=pl.BlockSpec(memory_space=pltpu.VMEM),
            out_shape=jax.ShapeDtypeStruct((outer * inner * core, height, columns), bf16),
            scratch_shapes=[pltpu.SemaphoreType.DMA((len(pieces),))],
            compiler_params=WIDE_ROOM,
            cost_estimate=FREE,
        )(*pieces)
        return matrix.reshape(-1, columns)

    def halves(self, left_side, right_side):
        height = left_side.shape[1]
        core = self.sizes["core"]
        outer, inner, depth = self.sizes["outer"], self.sizes["inner"], self.sizes["depth"]
        block = height // (outer * inner * core)
        me = self.index("core")
        shape = (outer, inner, depth, block // depth, right_side.shape[1])
        even, odd = [
            [left_side[:, (core * j + i) * block : (core * j + i + 1) * block] for j in range(outer * inner)]
            for i in range(core)
        ]

        def part(own):
            chosen = [
                jnp.where(me == 0, *((e, o) if own else (o, e))) for e, o in zip(even, odd)
            ]
            return transposed_times(jnp.concatenate(chosen, axis=1), right_side).astype(bf16)

        return part(False).reshape(shape), part(True).reshape(shape)

    def vector_halves(self, packed):
        core = self.sizes["core"]
        outer, inner, depth = self.sizes["outer"], self.sizes["inner"], self.sizes["depth"]
        split = packed.reshape((outer, inner, core, depth) + packed.shape[1:])
        me = self.index("core")
        even, odd = split[:, :, 0], split[:, :, 1]
        return jnp.where(me == 0, odd, even).astype(bf16), jnp.where(me == 0, even, odd)

    def sums(self, terms):
        return sum(term.astype(f32) for term in terms)

    def corner_sends(self, group):
        if self.square:
            top, bottom = self.block_sums(group, "corner", [])
            return [top], [bottom]
        outer, inner = self.sizes["outer"], self.sizes["inner"]
        a, b = self.index("outer"), self.index("inner")
        half = group[0][0].shape[2] // 2

        def block(terms, at_a, at_b, low, high):
            cut = [
                lax.dynamic_slice(
                    term,
                    (at_a % outer, at_b % inner, low, 0, 0),
                    (1, 1, high - low) + term.shape[3:],
                )
                for term in terms
            ]
            return self.sums(cut)[0, 0].astype(bf16)

        def joined(blocks):
            return jnp.concatenate(blocks, axis=-1) if len(blocks) > 1 else blocks[0]

        top = [
            jnp.stack(
                [
                    joined([block(terms, a + i, b + j, 0, half) for terms in group])
                    for j in self.steps("inner")
                ]
            )
            for i in self.steps("outer")
        ]
        bottom = [
            jnp.stack(
                [
                    joined([block(terms, a + i, b + j, half, 2 * half) for terms in group])
                    for i in self.steps("outer")
                ]
            )
            for j in self.steps("inner")
        ]
        return top, bottom

    def corner_moves(self, sends):
        top, bottom = sends
        return (
            [self.shift(send, "outer", step) for send, step in zip(top, self.steps("outer"))],
            [self.shift(send, "inner", step) for send, step in zip(bottom, self.steps("inner"))],
        )

    def side_sends(self, group, corners):
        top, bottom = corners
        if self.square:
            to_inner, to_outer = self.block_sums(group, "sides", [top[0], bottom[0]])
            return [to_inner], [to_outer]
        outer, inner = self.sizes["outer"], self.sizes["inner"]
        a, b = self.index("outer"), self.index("inner")
        half = group[0][0].shape[2] // 2

        def block(at_a, at_b, low, high, extra):
            sums, start = [], 0
            for terms in group:
                columns = terms[0].shape[-1]
                cut = [
                    lax.dynamic_slice(
                        term,
                        (at_a % outer, at_b % inner, low, 0, 0),
                        (1, 1, high - low) + term.shape[3:],
                    )[0, 0]
                    for term in terms
                ]
                cut += [piece[..., start : start + columns] for piece in extra]
                sums.append(self.sums(cut).astype(bf16))
                start += columns
            return jnp.concatenate(sums, axis=-1) if len(sums) > 1 else sums[0]

        to_inner = [
            jnp.concatenate(
                [
                    block(a, b + j, 0, half, [piece[j - 1] for piece in top]),
                    block(a, b + j, half, 2 * half, []),
                ]
            )
            for j in self.steps("inner")
        ]
        to_outer = [
            jnp.concatenate(
                [
                    block(a + i, b, 0, half, []),
                    block(a + i, b, half, 2 * half, [piece[i - 1] for piece in bottom]),
                ]
            )
            for i in self.steps("outer")
        ]
        return to_inner, to_outer

    def side_moves(self, sends):
        to_inner, to_outer = sends
        return [self.shift(send, "inner", step) for send, step in zip(to_inner, self.steps("inner"))] + [
            self.shift(send, "outer", step) for send, step in zip(to_outer, self.steps("outer"))
        ]

    def chip_terms(self, group, sides):
        a, b = self.index("outer"), self.index("inner")
        out, start = [], 0
        for terms in group:
            columns = terms[0].shape[-1]
            own = [
                lax.dynamic_slice(term, (a, b, 0, 0, 0), (1, 1) + term.shape[2:])[0, 0]
                for term in terms
            ]
            out.append(own + [piece[..., start : start + columns] for piece in sides])
            start += columns
        return out

    def chip_sum(self, group, sides):
        if self.square:
            total = sum(terms[0].shape[-1] for terms in group)
            return self.block_sums(group, "own", sides).reshape(
                self.sizes["depth"], -1, total
            )
        sums = [self.sums(terms).astype(bf16) for terms in self.chip_terms(group, sides)]
        return jnp.concatenate(sums, axis=-1) if len(sums) > 1 else sums[0]

    @property
    def square(self):
        return self.sizes["outer"] == 2 and self.sizes["inner"] == 2

    def block_sums(self, group, what, received):
        a, b = self.index("outer"), self.index("inner")
        place = {
            "corner": [(1 - a) * 2 + 1 - b],
            "sides": [a * 2 + 1 - b, (1 - a) * 2 + b],
            "own": [a * 2 + b],
        }[what]
        terms = [
            [term.reshape(4, -1, term.shape[-1]) for term in matrix] for matrix in group
        ]
        rows = terms[0][0].shape[1]
        half = rows // 2
        widths = [matrix[0].shape[-1] for matrix in terms]
        counts = [len(matrix) for matrix in terms]
        flat = [term for matrix in terms for term in matrix]
        received = [piece.reshape(-1, sum(widths)) for piece in received]

        def spec(term, at):
            return pl.BlockSpec(
                (1, rows, term.shape[-1]), lambda i, where, at=at: (where[at], 0, 0)
            )

        def kernel(where_ref, *refs):
            blocks = [
                refs[at * len(flat) : (at + 1) * len(flat)] for at in range(len(place))
            ]
            rest = refs[len(place) * len(flat) :]
            got, outs = rest[: len(received)], rest[len(received) :]
            for at, block in enumerate(blocks):
                first, start = 0, 0
                for count, columns in zip(counts, widths):
                    for low in range(0, columns, 512):
                        high = min(low + 512, columns)
                        here = slice(start + low, start + high)
                        value = sum(
                            ref[0, :, low:high].astype(f32) for ref in block[first : first + count]
                        )
                        if what == "corner":
                            outs[0][:, here] = value[:half].astype(bf16)
                            outs[1][:, here] = value[half:].astype(bf16)
                        elif what == "sides":
                            top, bottom = value[:half], value[half:]
                            if at == 0:
                                top = top + got[0][:, here].astype(f32)
                            else:
                                bottom = bottom + got[1][:, here].astype(f32)
                            outs[at][:half, here] = top.astype(bf16)
                            outs[at][half:, here] = bottom.astype(bf16)
                        else:
                            value = value + sum(ref[:, here].astype(f32) for ref in got)
                            outs[0][:, here] = value.astype(bf16)
                    first += count
                    start += columns

        def full(height):
            return pl.BlockSpec((height, sum(widths)), lambda i, where: (0, 0))

        heights = {"corner": [half, half], "sides": [rows, rows], "own": [rows]}[what]
        out = pl.pallas_call(
            kernel,
            grid_spec=pltpu.PrefetchScalarGridSpec(
                num_scalar_prefetch=1,
                grid=(1,),
                in_specs=[spec(term, at) for at in range(len(place)) for term in flat]
                + [full(piece.shape[0]) for piece in received],
                out_specs=[full(height) for height in heights],
            ),
            out_shape=[jax.ShapeDtypeStruct((height, sum(widths)), bf16) for height in heights],
            compiler_params=WIDE_ROOM,
            cost_estimate=FREE,
        )(jnp.stack(place).astype(jnp.int32), *(flat * len(place)), *received)
        return out[0] if what == "own" else out

    def depth_sends(self, chip):
        size, me = self.sizes["depth"], self.index("depth")
        return [
            lax.dynamic_index_in_dim(chip, (me + step) % size, 0, keepdims=False)
            for step in self.steps("depth")
        ]

    def depth_moves(self, sends):
        return [self.shift(send, "depth", step) for send, step in zip(sends, self.steps("depth"))]

    def share(self, chip, received):
        own = lax.dynamic_index_in_dim(chip, self.index("depth"), 0, keepdims=False)
        return self.sums([own] + received)


def together(*values):
    return lax.optimization_barrier(values)


def local(grid, *args):
    (
        inputs,
        memory,
        group_place,
        pair_mask,
        cotangent,
        self_inward,
        self_outward,
        self_query_bias,
        self_value_bias,
        self_output_bias,
        first_gain,
        first_shift,
        cross_query,
        cross_memory,
        cross_outward,
        cross_query_bias,
        cross_value_bias,
        cross_output_bias,
        second_gain,
        second_shift,
        expand_weight,
        expand_bias,
        reduce_weight,
        reduce_bias,
        third_gain,
        third_shift,
    ) = args
    pair_count, group_len, width = inputs.shape
    rows_in = inputs.reshape(group_len, width)
    rows_low = rows_in.astype(bf16)
    memory_low = memory.reshape(group_len, width).astype(bf16)

    vectors = (
        self_query_bias,
        self_value_bias,
        self_output_bias,
        first_gain,
        first_shift,
        cross_query_bias,
        cross_value_bias,
        cross_output_bias,
        second_gain,
        second_shift,
        reduce_bias,
        third_gain,
        third_shift,
    )
    rows = self_inward.shape[0]
    devices = width // rows
    places = jnp.concatenate(
        [
            group_place.reshape(1, -1),
            lax.dynamic_slice_in_dim(group_place, lax.axis_index("seq"), 1, axis=1),
        ],
        axis=1,
    )

    lane = 128
    one = jnp.concatenate(
        [self_inward, jnp.pad(self_query_bias[:, None], ((0, 0), (0, lane - 1)))], axis=1
    )
    packed = jnp.concatenate(
        [jnp.stack(vectors).T, expand_bias.reshape(rows, -1)], axis=1
    )
    spread = packed.shape[1]
    packed = jnp.pad(packed, ((0, 0), (0, lane - spread)))
    two = jnp.concatenate(
        [self_outward, cross_query, cross_outward, cross_memory, packed], axis=1
    )

    one_depth = grid.from_depth(one)
    one_depth, two, rows_low_sent = together(one_depth, two, rows_low)

    one_block = grid.depth_block(one, one_depth)
    one_sides = grid.from_sides(one_block)
    two_depth = grid.from_depth(two)
    one_sides, two_depth, rows_low_sent = together(one_sides, two_depth, rows_low_sent)

    all_low = lax.all_gather(rows_low_sent, "seq", axis=0, tiled=True)
    one_corners = grid.from_corners(one_sides)
    two_block = grid.depth_block(two, two_depth)
    one_corners, two_block = together(one_corners, two_block)

    two_sides = grid.from_sides(two_block)
    one_block_other, one_sides_other, one_corners_other = grid.swap(
        (one_block, one_sides, one_corners)
    )
    one_all = grid.whole(
        (one_block, one_sides, one_corners),
        (one_block_other, one_sides_other, one_corners_other),
    )
    self_query, self_context = one_all[:, :width], one_all[:, width : 3 * width]
    self_query_bias = one_all[:, 3 * width].astype(f32)
    query_self = (dense(rows_low, self_query) + self_query_bias).astype(bf16)
    two_sides, query_self, all_low, expand_weight, memory_low = together(
        two_sides, query_self, all_low, expand_weight, memory_low
    )

    all_memory = lax.all_gather(memory_low, "seq", axis=0, tiled=True)
    two_corners = grid.from_corners(two_sides)
    expand_depth = grid.from_depth(expand_weight)
    context_self = dense(all_low, self_context).astype(bf16)
    blended_self, total_self = attend_forward(query_self, context_self, places, True)
    blended_self, two_corners, expand_depth, reduce_weight = together(
        blended_self, two_corners, expand_depth, reduce_weight
    )

    expand_block = grid.depth_block(expand_weight, expand_depth)
    two_block_other, two_sides_other, two_corners_other = grid.swap(
        (two_block, two_sides, two_corners)
    )
    two_block_other, two_sides_other, two_corners_other, expand_block = together(
        two_block_other, two_sides_other, two_corners_other, expand_block
    )
    expand_sides = grid.from_sides(expand_block)
    reduce_depth = grid.from_depth(reduce_weight)
    two_all = grid.whole(
        (two_block, two_sides, two_corners),
        (two_block_other, two_sides_other, two_corners_other),
    )
    packed = two_all[:, 5 * width : 5 * width + spread].astype(f32)
    (
        self_query_bias,
        self_value_bias,
        self_output_bias,
        first_gain,
        first_shift,
        cross_query_bias,
        cross_value_bias,
        cross_output_bias,
        second_gain,
        second_shift,
        reduce_bias,
        third_gain,
        third_shift,
    ) = [line for line in packed[:, : len(vectors)].T]
    expand_bias = packed[:, len(vectors) :].reshape(-1)
    self_outward, cross_query, cross_outward = [
        two_all[:, i * width : (i + 1) * width] for i in range(3)
    ]
    cross_context = two_all[:, 3 * width : 5 * width]
    blended_self = (blended_self + self_value_bias).astype(bf16)
    pre_first = residual_scale * rows_in + dense(blended_self, self_outward) + self_output_bias
    after_self = norm_layer(pre_first, first_gain, first_shift)
    after_self_low = after_self.astype(bf16)
    query_cross = (dense(after_self_low, cross_query) + cross_query_bias).astype(bf16)
    query_cross, expand_sides, reduce_depth, all_memory = together(
        query_cross, expand_sides, reduce_depth, all_memory
    )

    reduce_block = grid.depth_block(reduce_weight, reduce_depth)
    expand_corners = grid.from_corners(expand_sides)
    reduce_sides = grid.from_sides(reduce_block)
    context_cross = dense(all_memory, cross_context).astype(bf16)
    blended_cross, total_cross = attend_forward(query_cross, context_cross, places, False)
    expand_corners, reduce_sides, blended_cross = together(
        expand_corners, reduce_sides, blended_cross
    )

    reduce_corners = grid.from_corners(reduce_sides)
    expand_block_other, expand_sides_other, expand_corners_other = grid.swap(
        (expand_block, expand_sides, expand_corners)
    )
    expand_block_other, expand_sides_other, expand_corners_other = together(
        expand_block_other, expand_sides_other, expand_corners_other
    )
    expand_all = grid.whole(
        (expand_block, expand_sides, expand_corners),
        (expand_block_other, expand_sides_other, expand_corners_other),
    )
    blended_cross = (blended_cross + cross_value_bias).astype(bf16)
    pre_second = (
        residual_scale * after_self + dense(blended_cross, cross_outward) + cross_output_bias
    )
    after_cross = norm_layer(pre_second, second_gain, second_shift)
    cross_low = after_cross.astype(bf16)
    cross_low, reduce_corners, expand_all = together(cross_low, reduce_corners, expand_all)
    reduce_block_other, reduce_sides_other, reduce_corners_other = grid.swap(
        (reduce_block, reduce_sides, reduce_corners)
    )
    reduce_all = grid.whole(
        (reduce_block, reduce_sides, reduce_corners),
        (reduce_block_other, reduce_sides_other, reduce_corners_other),
    )
    expanded, hidden, reduced = feed_forward(cross_low, expand_all, 0, reduce_all, expand_bias)
    pre_third = residual_scale * after_cross + reduced + reduce_bias
    result = norm_layer(pre_third, third_gain, third_shift)

    grad_out = cotangent.reshape(group_len, width) * pair_mask.astype(f32)[0]
    norm_back = jax.vjp(norm_layer, pre_third, third_gain, third_shift)[1]
    grad_third, third_gain_grad, third_shift_grad = norm_back(grad_out)
    reduce_bias_grad = jnp.sum(grad_third, axis=0)
    low_third = grad_third.astype(bf16)
    reduce_sent, reduce_kept = grid.halves(hidden, low_third)
    reduce_sent, low_third = together(reduce_sent, low_third)

    reduce_got = grid.swap(reduce_sent)
    expanded_low, expand_bias_grad, grad_cross = feed_backward(
        low_third, expand_all, 0, reduce_all, expanded
    )
    expanded_low, reduce_got, reduce_kept = together(expanded_low, reduce_got, reduce_kept)

    reduce_group = [[reduce_kept, reduce_got]]
    reduce_sends = grid.corner_sends(reduce_group)
    reduce_sends, expanded_low = together(reduce_sends, expanded_low)
    reduce_corners = grid.corner_moves(reduce_sends)
    expand_sent, expand_kept = grid.halves(cross_low, expanded_low)
    expand_sent, grad_cross = together(expand_sent, grad_cross)
    expand_got = grid.swap(expand_sent)
    grad_cross = residual_scale * grad_third + grad_cross
    norm_back = jax.vjp(norm_layer, pre_second, second_gain, second_shift)[1]
    grad_second, second_gain_grad, second_shift_grad = norm_back(grad_cross)
    cross_output_bias_grad = jnp.sum(grad_second, axis=0)
    second_low = grad_second.astype(bf16)
    grad_blended = times_transposed(second_low, cross_outward).astype(bf16)
    out_sent, out_kept = grid.halves(blended_cross, second_low)
    grad_blended, reduce_corners, expand_got, expand_kept, out_sent = together(
        grad_blended, reduce_corners, expand_got, expand_kept, out_sent
    )

    reduce_sends = grid.side_sends(reduce_group, reduce_corners)
    expand_group = [[expand_kept, expand_got]]
    expand_sends = grid.corner_sends(expand_group)
    reduce_sends, expand_sends, grad_blended = together(reduce_sends, expand_sends, grad_blended)
    reduce_sides = grid.side_moves(reduce_sends)
    expand_corners = grid.corner_moves(expand_sends)
    out_got = grid.swap(out_sent)
    grad_query_cross, grad_context_cross = attend_backward(
        query_cross, context_cross, places, total_cross, grad_blended, False
    )
    grad_query_cross, grad_context_cross, reduce_sides, expand_corners, out_got = together(
        grad_query_cross, grad_context_cross, reduce_sides, expand_corners, out_got
    )

    expand_sends = grid.side_sends(expand_group, expand_corners)
    reduce_chip = grid.chip_sum(reduce_group, reduce_sides)
    expand_sends, reduce_chip, grad_query_cross, grad_context_cross = together(
        expand_sends, reduce_chip, grad_query_cross, grad_context_cross
    )
    expand_sides = grid.side_moves(expand_sends)
    reduce_grad = lax.psum_scatter(reduce_chip, "seq", scatter_dimension=0)
    cross_value_bias_grad = jnp.sum(grad_context_cross[:, width:].astype(f32), axis=0)
    cross_query_bias_grad = jnp.sum(grad_query_cross, axis=0)
    query_cross_low = grad_query_cross.astype(bf16)
    context_sent, context_kept = grid.halves(all_memory, grad_context_cross)
    context_sent, query_cross_low = together(context_sent, query_cross_low)
    context_got = grid.swap(context_sent)
    query_sent, query_kept = grid.halves(after_self_low, query_cross_low)
    query_got = grid.swap(query_sent)
    grad_self = residual_scale * grad_second + times_transposed(query_cross_low, cross_query)
    norm_back = jax.vjp(norm_layer, pre_first, first_gain, first_shift)[1]
    grad_first, first_gain_grad, first_shift_grad = norm_back(grad_self)
    self_output_bias_grad = jnp.sum(grad_first, axis=0)
    first_low = grad_first.astype(bf16)
    first_low, context_got, query_got = together(first_low, context_got, query_got)
    outward_sent, outward_kept = grid.halves(blended_self, first_low)
    outward_got = grid.swap(outward_sent)
    grad_blended = times_transposed(first_low, self_outward).astype(bf16)
    cross_group = [
        [out_kept, out_got],
        [query_kept, query_got],
        [context_kept, context_got],
        [outward_kept, outward_got],
    ]
    grad_blended, cross_group = together(grad_blended, cross_group)

    cross_sends = grid.corner_sends(cross_group)
    cross_sends, grad_blended = together(cross_sends, grad_blended)
    cross_corners = grid.corner_moves(cross_sends)
    grad_query_self, grad_context_self = attend_backward(
        query_self, context_self, places, total_self, grad_blended, True
    )
    grad_query_self, grad_context_self, cross_corners, expand_sides = together(
        grad_query_self, grad_context_self, cross_corners, expand_sides
    )

    cross_sends = grid.side_sends(cross_group, cross_corners)
    expand_chip = grid.chip_sum(expand_group, expand_sides)
    cross_sends, expand_chip, grad_query_self, grad_context_self, grad_context_cross = together(
        cross_sends, expand_chip, grad_query_self, grad_context_self, grad_context_cross
    )
    cross_sides = grid.side_moves(cross_sends)
    expand_grad = lax.psum_scatter(expand_chip, "seq", scatter_dimension=0)
    inputs_part = times_transposed(grad_context_self, self_context).astype(bf16)
    inputs_grad = lax.psum_scatter(inputs_part, "seq", scatter_dimension=0, tiled=True)
    memory_part = times_transposed(grad_context_cross, cross_context).astype(bf16)
    memory_grad = lax.psum_scatter(memory_part, "seq", scatter_dimension=0, tiled=True)
    self_query_bias_grad = jnp.sum(grad_query_self, axis=0)
    self_value_bias_grad = jnp.sum(grad_context_self[:, width:].astype(f32), axis=0)
    query_self_low = grad_query_self.astype(bf16)
    context_sent, context_kept = grid.halves(all_low, grad_context_self)
    query_sent, query_kept = grid.halves(rows_low, query_self_low)
    vector_grads = (
        self_query_bias_grad,
        self_value_bias_grad,
        self_output_bias_grad,
        first_gain_grad,
        first_shift_grad,
        cross_query_bias_grad,
        cross_value_bias_grad,
        cross_output_bias_grad,
        second_gain_grad,
        second_shift_grad,
        reduce_bias_grad,
        third_gain_grad,
        third_shift_grad,
    )
    vector_grads = jnp.concatenate(
        [jnp.stack(vector_grads).T, expand_bias_grad.reshape(width, -1)], axis=1
    )
    vector_grads = jnp.pad(vector_grads, ((0, 0), (0, lane - spread)))
    vector_grads = vector_grads.reshape(devices, rows, lane)
    vector_sent, vector_kept = grid.vector_halves(vector_grads)
    query_sent, context_sent, vector_sent = together(query_sent, context_sent, vector_sent)
    query_got, context_got, vector_got = grid.swap((query_sent, context_sent, vector_sent))
    inputs_part, memory_part, query_got, context_got, vector_got, cross_sides = together(
        inputs_part, memory_part, query_got, context_got, vector_got, cross_sides
    )
    cross_chip = grid.chip_sum(cross_group, cross_sides)
    self_group = [
        [query_kept, query_got],
        [context_kept, context_got],
        [vector_kept, vector_got],
    ]
    self_group, cross_chip = together(self_group, cross_chip)

    cross_grad = lax.psum_scatter(cross_chip, "seq", scatter_dimension=0)
    self_sends = grid.corner_sends(self_group)
    (self_sends,) = together(self_sends)
    self_corners = grid.corner_moves(self_sends)
    (self_corners,) = together(self_corners)

    self_sends = grid.side_sends(self_group, self_corners)
    self_sends, query_self_low = together(self_sends, query_self_low)
    self_sides = grid.side_moves(self_sends)
    inputs_base = residual_scale * grad_first + times_transposed(query_self_low, self_query)
    inputs_base, self_sides = together(inputs_base, self_sides)

    self_chip = grid.chip_sum(self_group, self_sides)
    self_sends = grid.depth_sends(self_chip)
    self_depths = grid.depth_moves(self_sends)
    cross_grad = cross_grad.astype(f32)
    cross_out_grad, cross_query_grad = cross_grad[:, :width], cross_grad[:, width : 2 * width]
    cross_context_grad = cross_grad[:, 2 * width : 4 * width]
    self_out_grad = cross_grad[:, 4 * width :]
    reduce_grad = reduce_grad.astype(f32)
    expand_grad = expand_grad.astype(f32)
    memory_grad = memory_grad.astype(f32)
    inputs_grad = inputs_base + inputs_grad.astype(f32)
    self_grad = grid.share(self_chip, self_depths)
    self_inward_grad, share = self_grad[:, : 3 * width], self_grad[:, 3 * width :]
    (
        self_query_bias_grad,
        self_value_bias_grad,
        self_output_bias_grad,
        first_gain_grad,
        first_shift_grad,
        cross_query_bias_grad,
        cross_value_bias_grad,
        cross_output_bias_grad,
        second_gain_grad,
        second_shift_grad,
        reduce_bias_grad,
        third_gain_grad,
        third_shift_grad,
    ) = [line for line in share[:, : len(vectors)].T]
    expand_bias_grad = share[:, len(vectors) : spread].reshape(-1)

    return (
        result.reshape(pair_count, group_len, width),
        inputs_grad.reshape(pair_count, group_len, width),
        memory_grad.reshape(pair_count, group_len, width),
        self_inward_grad,
        self_out_grad,
        self_query_bias_grad,
        self_value_bias_grad,
        self_output_bias_grad,
        first_gain_grad,
        first_shift_grad,
        cross_query_grad,
        cross_context_grad,
        cross_out_grad,
        cross_query_bias_grad,
        cross_value_bias_grad,
        cross_output_bias_grad,
        second_gain_grad,
        second_shift_grad,
        expand_grad,
        expand_bias_grad,
        reduce_grad,
        reduce_bias_grad,
        third_gain_grad,
        third_shift_grad,
    )


def solution(mesh):
    rows = P(("dp", "seq"), None)
    vector = P(("dp", "seq"))
    tokens = P("dp", "seq", None)
    in_specs = (
        (tokens, tokens, P("dp", None), P("dp"), tokens)
        + (rows, rows)
        + (vector,) * 5
        + (rows,) * 3
        + (vector,) * 5
        + (rows, vector, rows)
        + (vector,) * 3
    )
    out_specs = (
        (tokens,) * 3
        + (rows, rows)
        + (vector,) * 5
        + (rows,) * 3
        + (vector,) * 5
        + (rows, vector, rows)
        + (vector,) * 3
    )
    return jax.shard_map(
        functools.partial(local, Grid(mesh)),
        mesh=mesh,
        in_specs=in_specs,
        out_specs=out_specs,
        check_vma=False,
    )
```

```python
import functools

import jax
import jax.numpy as jnp
from jax import lax
from jax.experimental import pallas as pl
from jax.experimental.pallas import tpu as pltpu
from jax.sharding import PartitionSpec as P

HEADS = 16
HEAD_DIM = 64
PAIR = 2 * HEAD_DIM

residual_scale = 4.16
epsilon = 1e-05
score_scale = 0.125
negative_fill = -1e30
bf16 = jnp.bfloat16
f32 = jnp.float32


def norm_layer(values, gain_vector, shift_vector):
    middle = jnp.mean(values, axis=-1, keepdims=True)
    centred = values - middle
    spread = jnp.mean(centred * centred, axis=-1, keepdims=True)
    return centred * lax.rsqrt(spread + epsilon) * gain_vector + shift_vector


def gelu_tanh(values):
    return (
        0.5
        * values
        * (1.0 + jnp.tanh(0.7978845608028654 * (values + 0.044715 * values * values * values)))
    )


def dense(left_side, right_side):
    return jnp.dot(left_side, right_side, preferred_element_type=f32)


def times_transposed(left_side, right_side):
    return lax.dot_general(
        left_side, right_side, (((1,), (1,)), ((), ())), preferred_element_type=f32
    )


def transposed_times(left_side, right_side):
    return lax.dot_general(
        left_side, right_side, (((0,), (0,)), ((), ())), preferred_element_type=f32
    )


def lane_head(shape, head):
    lane = lax.broadcasted_iota(jnp.int32, shape, 1)
    return (lane < HEAD_DIM) if head == 0 else (lane >= HEAD_DIM)


def masked_scores(scores, place_ref, causal, group_len):
    if not causal:
        return scores
    blocks = scores.shape[0] // group_len
    own = place_ref[0, blocks]
    diff = lax.broadcasted_iota(jnp.int32, (group_len, group_len), 0) - lax.broadcasted_iota(
        jnp.int32, (group_len, group_len), 1
    )
    parts = []
    for block in range(blocks):
        reach = (own - place_ref[0, block]) * group_len
        part = scores[block * group_len : (block + 1) * group_len]
        parts.append(jnp.where(diff <= reach, part, negative_fill))
    return jnp.concatenate(parts, axis=0)


def attend_forward_kernel(causal, place_ref, q_ref, k_ref, v_ref, o_ref, total_ref):
    group_len = q_ref.shape[0]
    scaled = q_ref[...] * jnp.asarray(score_scale, bf16)
    keys = k_ref[...]
    values = v_ref[...]
    scores, outs = [], []
    for head in range(2):
        own = jnp.where(lane_head(scaled.shape, head), scaled, jnp.zeros_like(scaled))
        scores.append(times_transposed(keys, own))
    for head in range(2):
        here = masked_scores(scores[head], place_ref, causal, group_len)
        top = jnp.max(here, axis=0, keepdims=True)
        weights = jnp.exp(here - top)
        total = jnp.sum(weights, axis=0, keepdims=True)
        blended = transposed_times(values, weights.astype(bf16)) / total
        outs.append(blended)
        total_ref[0, head : head + 1, :] = top + jnp.log(total)
    row = lax.broadcasted_iota(jnp.int32, outs[0].shape, 0)
    o_ref[...] = jnp.where(row < HEAD_DIM, outs[0], outs[1]).T.astype(bf16)


def attend_backward_kernel(
    causal, place_ref, q_ref, k_ref, v_ref, total_ref, g_ref, dq_ref, dkv_ref, held, sems
):
    group_len = q_ref.shape[0]
    scaled = q_ref[...] * jnp.asarray(score_scale, bf16)
    keys = k_ref[...]
    values = v_ref[...]
    grads = g_ref[...]
    dqs, dks, dvs = [], [], []
    owns, masked, scores, dprobs = [], [], [], []
    for head in range(2):
        mine = lane_head(scaled.shape, head)
        owns.append(jnp.where(mine, scaled, jnp.zeros_like(scaled)))
        masked.append(jnp.where(mine, grads, jnp.zeros_like(grads)))
        scores.append(times_transposed(keys, owns[head]))
        dprobs.append(times_transposed(values, masked[head]))
    for head in range(2):
        here = masked_scores(scores[head], place_ref, causal, group_len)
        weights = jnp.exp(here - total_ref[0, head : head + 1, :])
        dvs.append(dense(weights.astype(bf16), masked[head]))
        dprob = dprobs[head]
        delta = jnp.sum(dprob * weights, axis=0, keepdims=True)
        dscore = (weights * (dprob - delta)).astype(bf16)
        dks.append(dense(dscore, owns[head]))
        dqs.append(transposed_times(keys, dscore))
    row = lax.broadcasted_iota(jnp.int32, dqs[0].shape, 0)
    dq_ref[...] = jnp.where(row < HEAD_DIM, dqs[0], dqs[1]).T * score_scale
    step, steps = pl.program_id(0), pl.num_programs(0)
    slot = lax.rem(step, 2)
    width = dkv_ref.shape[1] // 2

    def moves(at, slot):
        return [
            pltpu.make_async_copy(
                held.at[slot, part],
                dkv_ref.at[:, pl.ds(pl.multiple_of(part * width + at * PAIR, PAIR), PAIR)],
                sems.at[slot, part],
            )
            for part in range(2)
        ]

    @pl.when(step >= 2)
    def _():
        for move in moves(step - 2, slot):
            move.wait()

    held[slot, 0] = (dks[0] + dks[1]).astype(bf16)
    held[slot, 1] = (dvs[0] + dvs[1]).astype(bf16)
    for move in moves(step, slot):
        move.start()

    @pl.when(step == steps - 1)
    def _():
        for move in moves(step - 1, 1 - slot):
            move.wait()
        for move in moves(step, slot):
            move.wait()


def attention_specs(group_len, length, pairs):
    row = pl.BlockSpec((group_len, PAIR), lambda h: (0, h))
    keys = pl.BlockSpec((length, PAIR), lambda h: (0, h))
    values = pl.BlockSpec((length, PAIR), lambda h: (0, h + pairs))
    total = pl.BlockSpec((1, 2, group_len), lambda h: (h, 0, 0))
    place = pl.BlockSpec(memory_space=pltpu.SMEM)
    return place, row, keys, values, total


FREE = pl.CostEstimate(flops=1, bytes_accessed=1, transcendentals=0)
ROOM = pltpu.CompilerParams(vmem_limit_bytes=24 * 1024 * 1024)
WIDE_ROOM = pltpu.CompilerParams(vmem_limit_bytes=48 * 1024 * 1024)


def attend_forward(query_rows, context_rows, places, causal):
    group_len, width = query_rows.shape
    length = context_rows.shape[0]
    pairs = width // PAIR
    place, row, keys, values, total = attention_specs(group_len, length, pairs)
    return pl.pallas_call(
        functools.partial(attend_forward_kernel, causal),
        grid=(pairs,),
        in_specs=[place, row, keys, values],
        out_specs=[row, total],
        out_shape=[
            jax.ShapeDtypeStruct((group_len, width), bf16),
            jax.ShapeDtypeStruct((pairs, 2, group_len), f32),
        ],
        compiler_params=ROOM,
        cost_estimate=FREE,
    )(places, query_rows, context_rows, context_rows)


def attend_backward(query_rows, context_rows, places, totals, grads, causal):
    group_len, width = query_rows.shape
    length = context_rows.shape[0]
    pairs = width // PAIR
    place, row, keys, values, total = attention_specs(group_len, length, pairs)
    return pl.pallas_call(
        functools.partial(attend_backward_kernel, causal),
        grid=(pairs,),
        in_specs=[place, row, keys, values, total, row],
        out_specs=[row, pl.BlockSpec(memory_space=pl.ANY)],
        out_shape=[
            jax.ShapeDtypeStruct((group_len, width), f32),
            jax.ShapeDtypeStruct((length, 2 * width), bf16),
        ],
        scratch_shapes=[
            pltpu.VMEM((2, 2, length, PAIR), bf16),
            pltpu.SemaphoreType.DMA((2, 2)),
        ],
        compiler_params=WIDE_ROOM,
        cost_estimate=FREE,
    )(places, query_rows, context_rows, context_rows, totals, grads)


def context_back_kernel(g_ref, k_ref, v_ref, out_ref):
    width = k_ref.shape[1]
    out_ref[...] = (
        times_transposed(g_ref[:, :width], k_ref[...])
        + times_transposed(g_ref[:, width:], v_ref[...])
    ).astype(bf16)


def context_back(grads, weights, start):
    length, both = grads.shape
    width = both // 2
    each = width // 4
    return pl.pallas_call(
        context_back_kernel,
        grid=(4,),
        in_specs=[
            pl.BlockSpec((length, both), lambda j: (0, 0)),
            pl.BlockSpec((each, width), lambda j: (j, start)),
            pl.BlockSpec((each, width), lambda j: (j, start + 1)),
        ],
        out_specs=pl.BlockSpec((length, each), lambda j: (0, j)),
        out_shape=jax.ShapeDtypeStruct((length, width), bf16),
        compiler_params=WIDE_ROOM,
        cost_estimate=FREE,
    )(grads, weights, weights)


def context_halves_kernel(where_ref, other_ref, own_ref, g_ref, sent_ref, kept_ref):
    rows = sent_ref.shape[0]
    grads = g_ref[...]
    sent_ref[...] = dense(other_ref[...].reshape(rows, -1), grads).astype(bf16)
    kept_ref[...] = dense(own_ref[...].reshape(rows, -1), grads).astype(bf16)


def turn_kernel(x_ref, out_ref):
    out_ref[...] = x_ref[...].T


def turned(values):
    rows, columns = values.shape
    return pl.pallas_call(
        turn_kernel,
        grid=(columns // PAIR,),
        in_specs=[pl.BlockSpec((rows, PAIR), lambda j: (0, j))],
        out_specs=pl.BlockSpec((PAIR, rows), lambda j: (j, 0)),
        out_shape=jax.ShapeDtypeStruct((columns, rows), values.dtype),
        compiler_params=ROOM,
        cost_estimate=FREE,
    )(values)


def feed_forward_kernel(x_ref, e_ref, r_ref, b_ref, expanded_ref, hidden_ref, out_ref):
    step = pl.program_id(0)
    wide = b_ref.shape[-1]
    expanded = dense(x_ref[...], e_ref[...].reshape(-1, wide)) + b_ref[...]
    expanded_ref[0] = expanded
    hidden = gelu_tanh(expanded).astype(bf16)
    hidden_ref[...] = hidden
    part = dense(hidden, r_ref[...].reshape(wide, -1))

    @pl.when(step == 0)
    def _():
        out_ref[...] = part

    @pl.when(step > 0)
    def _():
        out_ref[...] += part


def feed_backward_kernel(g_ref, e_ref, r_ref, expanded_ref, low_ref, bias_ref, out_ref):
    step = pl.program_id(0)
    wide = low_ref.shape[-1]
    grad_hidden = times_transposed(g_ref[...], r_ref[...].reshape(wide, -1))
    u = expanded_ref[0]
    square = u * u
    bent = jnp.tanh(0.7978845608028654 * (u + 0.044715 * square * u))
    slope = 0.5 * (1.0 + bent) + 0.5 * u * (1.0 - bent * bent) * (
        0.7978845608028654 * (1.0 + 3.0 * 0.044715 * square)
    )
    grad = grad_hidden * slope
    bias_ref[...] = jnp.sum(grad, axis=0, keepdims=True)
    low = grad.astype(bf16)
    low_ref[...] = low
    part = times_transposed(low, e_ref[...].reshape(-1, wide))

    @pl.when(step == 0)
    def _():
        out_ref[...] = part

    @pl.when(step > 0)
    def _():
        out_ref[...] += part


def feed_specs(count, width, each):
    return (
        pl.BlockSpec((count, width), lambda j: (0, 0)),
        pl.BlockSpec((1, width, each), lambda j: (j, 0, 0)),
        pl.BlockSpec((each, width), lambda j: (j, 0)),
        pl.BlockSpec((count, each), lambda j: (0, j)),
        pl.BlockSpec((1, each), lambda j: (0, j)),
        pl.BlockSpec((1, count, each), lambda j: (j, 0, 0)),
    )


def feed_forward(rows, expand_all, reduce_all, bias):
    count, width = rows.shape
    wide = reduce_all.shape[0]
    each = expand_all.shape[2]
    whole, first, second, part, line, block = feed_specs(count, width, each)
    return pl.pallas_call(
        feed_forward_kernel,
        grid=(wide // each,),
        in_specs=[whole, first, second, line],
        out_specs=[block, part, whole],
        out_shape=[
            jax.ShapeDtypeStruct((wide // each, count, each), f32),
            jax.ShapeDtypeStruct((count, wide), bf16),
            jax.ShapeDtypeStruct((count, width), f32),
        ],
        compiler_params=WIDE_ROOM,
        cost_estimate=FREE,
    )(rows, expand_all, reduce_all, bias.reshape(1, -1))


def feed_backward(grads, expand_all, reduce_all, expanded):
    count, width = grads.shape
    wide = reduce_all.shape[0]
    each = expand_all.shape[2]
    whole, first, second, part, line, block = feed_specs(count, width, each)
    return pl.pallas_call(
        feed_backward_kernel,
        grid=(wide // each,),
        in_specs=[whole, first, second, block],
        out_specs=[part, line, whole],
        out_shape=[
            jax.ShapeDtypeStruct((count, wide), bf16),
            jax.ShapeDtypeStruct((1, wide), f32),
            jax.ShapeDtypeStruct((count, width), f32),
        ],
        compiler_params=WIDE_ROOM,
        cost_estimate=FREE,
    )(grads, expand_all, reduce_all, expanded)


class Grid:
    def __init__(self, mesh):
        self.dp = mesh.shape["dp"]
        depth = mesh.shape["seq"]
        core = 2 if self.dp % 2 == 0 else 1
        chips = self.dp // core
        outer = 1
        while outer * outer < chips:
            outer *= 2
        inner = chips // outer
        self.sizes = {"outer": outer, "inner": inner, "core": core, "depth": depth}
        self.strides = {"outer": inner * core, "inner": core, "core": 1}

    def index(self, dim):
        if dim == "depth":
            return lax.axis_index("seq")
        return (lax.axis_index("dp") // self.strides[dim]) % self.sizes[dim]

    def shift(self, value, dim, step):
        size = self.sizes[dim]
        if dim == "depth":
            return lax.ppermute(value, "seq", [(i, (i + step) % size) for i in range(size)])
        stride = self.strides[dim]
        pairs = []
        for device in range(self.dp):
            at = (device // stride) % size
            pairs.append((device, device + ((at + step) % size - at) * stride))
        return lax.ppermute(value, "dp", pairs)

    def steps(self, dim):
        return range(1, self.sizes[dim])

    def from_depth(self, shard):
        return [self.shift(shard, "depth", step) for step in self.steps("depth")]

    def depth_block(self, shard, pieces):
        size, me = self.sizes["depth"], self.index("depth")
        return jnp.stack(
            [lax.select_n((me - at) % size, shard, *pieces) for at in range(size)]
        )

    def from_sides(self, block):
        return (
            [self.shift(block, "inner", step) for step in self.steps("inner")],
            [self.shift(block, "outer", step) for step in self.steps("outer")],
        )

    def from_corners(self, sides):
        along_inner, along_outer = sides
        half = along_inner[0].shape[0] // 2
        top = jnp.stack([block[:half] for block in along_inner])
        bottom = jnp.stack([block[half:] for block in along_outer])
        return (
            [self.shift(top, "outer", step) for step in self.steps("outer")],
            [self.shift(bottom, "inner", step) for step in self.steps("inner")],
        )

    def swap(self, pieces):
        return jax.tree.map(lambda piece: self.shift(piece, "core", 1), pieces)

    def whole(self, own, others, blocks=1):
        outer, inner, core = (self.sizes[n] for n in ("outer", "inner", "core"))
        each, total = own[0].shape[-2], own[0].shape[-1]
        columns = total // blocks
        height = self.sizes["depth"] * each
        half = height // 2
        pieces, places = [], []

        def add(piece, back_a, back_b, other, start):
            pieces.append(piece.reshape(-1, total))
            places.append((back_a, back_b, other, start))

        for other, (block, (along_inner, along_outer), (top, bottom)) in enumerate([own, others]):
            add(block, 0, 0, other, 0)
            for j, piece in enumerate(along_inner):
                add(piece, 0, j + 1, other, 0)
            for i, piece in enumerate(along_outer):
                add(piece, i + 1, 0, other, 0)
            for i in range(outer - 1):
                for j in range(inner - 1):
                    add(top[i][j], i + 1, j + 1, other, 0)
                    add(bottom[j][i], i + 1, j + 1, other, half)

        def kernel(*refs):
            out, sems = refs[len(pieces)], refs[len(pieces) + 1]
            device = lax.axis_index("dp")
            a = device // self.strides["outer"]
            b = lax.rem(device // self.strides["inner"], inner)
            c = lax.rem(device, core)
            copies = []
            for at, (ref, (back_a, back_b, other, start)) in enumerate(zip(refs, places)):
                to_a = lax.rem(a + (outer - back_a), outer)
                to_b = lax.rem(b + (inner - back_b), inner)
                to_c = lax.rem(c + other, core)
                index = (to_a * inner + to_b) * core + to_c
                for j in range(blocks):
                    copies.append(
                        pltpu.make_async_copy(
                            ref.at[:, pl.ds(j * columns, columns)],
                            out.at[j, index, pl.ds(start, ref.shape[0])],
                            sems.at[at, j],
                        )
                    )
            for copy in copies:
                copy.start()
            for copy in copies:
                copy.wait()

        anywhere = pl.BlockSpec(memory_space=pltpu.HBM)
        matrix = pl.pallas_call(
            kernel,
            in_specs=[anywhere] * len(pieces),
            out_specs=pl.BlockSpec(memory_space=pltpu.VMEM),
            out_shape=jax.ShapeDtypeStruct((blocks, outer * inner * core, height, columns), bf16),
            scratch_shapes=[pltpu.SemaphoreType.DMA((len(pieces), blocks))],
            compiler_params=WIDE_ROOM,
            cost_estimate=FREE,
        )(*pieces)
        matrix = matrix.reshape(blocks, -1, columns)
        return matrix if blocks > 1 else matrix[0]

    def picked(self, left_side):
        core = self.sizes["core"]
        count = self.sizes["outer"] * self.sizes["inner"]
        block = left_side.shape[1] // (count * core)
        me = self.index("core")
        even, odd = [
            [left_side[:, (core * j + i) * block : (core * j + i + 1) * block] for j in range(count)]
            for i in range(core)
        ]
        return tuple(
            jnp.concatenate(
                [jnp.where(me == 0, *((e, o) if own else (o, e))) for e, o in zip(even, odd)], axis=1
            )
            for own in (False, True)
        )

    def halves(self, picked, right_side):
        outer, inner, depth = self.sizes["outer"], self.sizes["inner"], self.sizes["depth"]
        each = picked[0].shape[1] // (outer * inner * depth)
        shape = (outer, inner, depth, each, right_side.shape[1])
        return tuple(
            transposed_times(chosen, right_side).astype(bf16).reshape(shape) for chosen in picked
        )

    def context_halves(self, turned, grads):
        outer, inner, core, depth = (self.sizes[n] for n in ("outer", "inner", "core", "depth"))
        height, rows = turned.shape
        block = height // (outer * inner * core)
        columns = grads.shape[1]
        each = columns // 4
        me = self.index("core")
        piece = (outer * inner, 1, block, rows)
        sent, kept = pl.pallas_call(
            context_halves_kernel,
            grid_spec=pltpu.PrefetchScalarGridSpec(
                num_scalar_prefetch=1,
                grid=(4,),
                in_specs=[
                    pl.BlockSpec(piece, lambda j, where: (0, where[0], 0, 0)),
                    pl.BlockSpec(piece, lambda j, where: (0, where[1], 0, 0)),
                    pl.BlockSpec((rows, each), lambda j, where: (0, j)),
                ],
                out_specs=[pl.BlockSpec((height // core, each), lambda j, where: (0, j))] * 2,
            ),
            out_shape=[jax.ShapeDtypeStruct((height // core, columns), bf16)] * 2,
            compiler_params=WIDE_ROOM,
            cost_estimate=FREE,
        )(
            jnp.stack([1 - me, me]).astype(jnp.int32),
            *([turned.reshape(outer * inner, core, block, rows)] * 2),
            grads,
        )
        shape = (outer, inner, depth, block // depth, columns)
        return sent.reshape(shape), kept.reshape(shape)

    def vector_halves(self, packed):
        core = self.sizes["core"]
        outer, inner, depth = self.sizes["outer"], self.sizes["inner"], self.sizes["depth"]
        split = packed.reshape((outer, inner, core, depth) + packed.shape[1:])
        me = self.index("core")
        even, odd = split[:, :, 0], split[:, :, 1]
        return jnp.where(me == 0, odd, even).astype(bf16), jnp.where(me == 0, even, odd)

    def sums(self, terms):
        return sum(term.astype(f32) for term in terms)

    def corner_sends(self, group):
        if self.square:
            top, bottom = self.block_sums(group, "corner", [])
            return [top], [bottom]
        outer, inner = self.sizes["outer"], self.sizes["inner"]
        a, b = self.index("outer"), self.index("inner")
        half = group[0][0].shape[2] // 2

        def block(terms, at_a, at_b, low, high):
            cut = [
                lax.dynamic_slice(
                    term,
                    (at_a % outer, at_b % inner, low, 0, 0),
                    (1, 1, high - low) + term.shape[3:],
                )
                for term in terms
            ]
            return self.sums(cut)[0, 0].astype(bf16)

        def joined(blocks):
            return jnp.concatenate(blocks, axis=-1) if len(blocks) > 1 else blocks[0]

        top = [
            jnp.stack(
                [
                    joined([block(terms, a + i, b + j, 0, half) for terms in group])
                    for j in self.steps("inner")
                ]
            )
            for i in self.steps("outer")
        ]
        bottom = [
            jnp.stack(
                [
                    joined([block(terms, a + i, b + j, half, 2 * half) for terms in group])
                    for i in self.steps("outer")
                ]
            )
            for j in self.steps("inner")
        ]
        return top, bottom

    def corner_moves(self, sends):
        top, bottom = sends
        return (
            [self.shift(send, "outer", step) for send, step in zip(top, self.steps("outer"))],
            [self.shift(send, "inner", step) for send, step in zip(bottom, self.steps("inner"))],
        )

    def side_sends(self, group, corners):
        top, bottom = corners
        if self.square:
            to_inner, to_outer = self.block_sums(group, "sides", [top[0], bottom[0]])
            return [to_inner], [to_outer]
        outer, inner = self.sizes["outer"], self.sizes["inner"]
        a, b = self.index("outer"), self.index("inner")
        half = group[0][0].shape[2] // 2

        def block(at_a, at_b, low, high, extra):
            sums, start = [], 0
            for terms in group:
                columns = terms[0].shape[-1]
                cut = [
                    lax.dynamic_slice(
                        term,
                        (at_a % outer, at_b % inner, low, 0, 0),
                        (1, 1, high - low) + term.shape[3:],
                    )[0, 0]
                    for term in terms
                ]
                cut += [piece[..., start : start + columns] for piece in extra]
                sums.append(self.sums(cut).astype(bf16))
                start += columns
            return jnp.concatenate(sums, axis=-1) if len(sums) > 1 else sums[0]

        to_inner = [
            jnp.concatenate(
                [
                    block(a, b + j, 0, half, [piece[j - 1] for piece in top]),
                    block(a, b + j, half, 2 * half, []),
                ]
            )
            for j in self.steps("inner")
        ]
        to_outer = [
            jnp.concatenate(
                [
                    block(a + i, b, 0, half, []),
                    block(a + i, b, half, 2 * half, [piece[i - 1] for piece in bottom]),
                ]
            )
            for i in self.steps("outer")
        ]
        return to_inner, to_outer

    def side_moves(self, sends):
        to_inner, to_outer = sends
        return [self.shift(send, "inner", step) for send, step in zip(to_inner, self.steps("inner"))] + [
            self.shift(send, "outer", step) for send, step in zip(to_outer, self.steps("outer"))
        ]

    def chip_terms(self, group, sides):
        a, b = self.index("outer"), self.index("inner")
        out, start = [], 0
        for terms in group:
            columns = terms[0].shape[-1]
            own = [
                lax.dynamic_slice(term, (a, b, 0, 0, 0), (1, 1) + term.shape[2:])[0, 0]
                for term in terms
            ]
            out.append(own + [piece[..., start : start + columns] for piece in sides])
            start += columns
        return out

    def chip_sum(self, group, sides):
        if self.square:
            total = sum(terms[0].shape[-1] for terms in group)
            return self.block_sums(group, "own", sides).reshape(
                self.sizes["depth"], -1, total
            )
        sums = [self.sums(terms).astype(bf16) for terms in self.chip_terms(group, sides)]
        return jnp.concatenate(sums, axis=-1) if len(sums) > 1 else sums[0]

    @property
    def square(self):
        return self.sizes["outer"] == 2 and self.sizes["inner"] == 2

    def block_sums(self, group, what, received):
        a, b = self.index("outer"), self.index("inner")
        place = {
            "corner": [(1 - a) * 2 + 1 - b],
            "sides": [a * 2 + 1 - b, (1 - a) * 2 + b],
            "own": [a * 2 + b],
        }[what]
        terms = [
            [term.reshape(4, -1, term.shape[-1]) for term in matrix] for matrix in group
        ]
        rows = terms[0][0].shape[1]
        half = rows // 2
        widths = [matrix[0].shape[-1] for matrix in terms]
        counts = [len(matrix) for matrix in terms]
        flat = [term for matrix in terms for term in matrix]
        received = [piece.reshape(-1, sum(widths)) for piece in received]

        def kernel(where_ref, *refs):
            terms_in, rest = refs[: len(flat)], refs[len(flat) :]
            got_in, rest = rest[: len(received)], rest[len(received) :]
            outs, rest = rest[: len(heights)], rest[len(heights) :]
            held, got, sems = rest[: len(flat)], rest[len(flat) : -1], rest[-1]
            copies = [
                pltpu.make_async_copy(
                    ref.at[where_ref[at]], held[i].at[at], sems.at[at * len(flat) + i]
                )
                for at in range(len(place))
                for i, ref in enumerate(terms_in)
            ]
            first_got = len(copies)
            copies += [
                pltpu.make_async_copy(ref, got[i], sems.at[first_got + i])
                for i, ref in enumerate(got_in)
            ]
            for copy in copies:
                copy.start()
            for copy in copies:
                copy.wait()
            for at in range(len(place)):
                first, start = 0, 0
                for count, columns in zip(counts, widths):
                    for low in range(0, columns, 512):
                        high = min(low + 512, columns)
                        here = slice(start + low, start + high)
                        value = sum(
                            ref[at, :, low:high].astype(f32) for ref in held[first : first + count]
                        )
                        if what == "corner":
                            outs[0][:, here] = value[:half].astype(bf16)
                            outs[1][:, here] = value[half:].astype(bf16)
                        elif what == "sides":
                            top, bottom = value[:half], value[half:]
                            if at == 0:
                                top = top + got[0][:, here].astype(f32)
                            else:
                                bottom = bottom + got[1][:, here].astype(f32)
                            outs[at][:half, here] = top.astype(bf16)
                            outs[at][half:, here] = bottom.astype(bf16)
                        else:
                            value = value + sum(ref[:, here].astype(f32) for ref in got)
                            outs[0][:, here] = value.astype(bf16)
                    first += count
                    start += columns

        heights = {"corner": [half, half], "sides": [rows, rows], "own": [rows]}[what]
        in_hbm = pl.BlockSpec(memory_space=pltpu.HBM)
        out = pl.pallas_call(
            kernel,
            in_specs=[pl.BlockSpec(memory_space=pltpu.SMEM)]
            + [in_hbm] * (len(flat) + len(received)),
            out_specs=[pl.BlockSpec(memory_space=pltpu.VMEM)] * len(heights),
            out_shape=[jax.ShapeDtypeStruct((height, sum(widths)), bf16) for height in heights],
            scratch_shapes=[
                pltpu.VMEM((len(place), rows, term.shape[-1]), term.dtype) for term in flat
            ]
            + [pltpu.VMEM(piece.shape, bf16) for piece in received]
            + [pltpu.SemaphoreType.DMA((len(place) * len(flat) + len(received),))],
            compiler_params=WIDE_ROOM,
            cost_estimate=FREE,
        )(jnp.stack(place).astype(jnp.int32), *flat, *received)
        return out[0] if what == "own" else out

    def depth_sends(self, chip):
        size, me = self.sizes["depth"], self.index("depth")
        return [
            lax.dynamic_index_in_dim(chip, (me + step) % size, 0, keepdims=False)
            for step in self.steps("depth")
        ]

    def depth_moves(self, sends):
        return [self.shift(send, "depth", step) for send, step in zip(sends, self.steps("depth"))]

    def share(self, chip, received):
        own = lax.dynamic_index_in_dim(chip, self.index("depth"), 0, keepdims=False)
        return self.sums([own] + received)


def together(*values):
    return lax.optimization_barrier(values)


def local(grid, *args):
    (
        inputs,
        memory,
        group_place,
        pair_mask,
        cotangent,
        self_inward,
        self_outward,
        self_query_bias,
        self_value_bias,
        self_output_bias,
        first_gain,
        first_shift,
        cross_query,
        cross_memory,
        cross_outward,
        cross_query_bias,
        cross_value_bias,
        cross_output_bias,
        second_gain,
        second_shift,
        expand_weight,
        expand_bias,
        reduce_weight,
        reduce_bias,
        third_gain,
        third_shift,
    ) = args
    pair_count, group_len, width = inputs.shape
    rows_in = inputs.reshape(group_len, width)
    rows_low = rows_in.astype(bf16)
    memory_low = memory.reshape(group_len, width).astype(bf16)

    vectors = (
        self_query_bias,
        self_value_bias,
        self_output_bias,
        first_gain,
        first_shift,
        cross_query_bias,
        cross_value_bias,
        cross_output_bias,
        second_gain,
        second_shift,
        reduce_bias,
        third_gain,
        third_shift,
    )
    rows = self_inward.shape[0]
    devices = width // rows
    places = jnp.concatenate(
        [
            group_place.reshape(1, -1),
            lax.dynamic_slice_in_dim(group_place, lax.axis_index("seq"), 1, axis=1),
        ],
        axis=1,
    )

    lane = 128
    one = jnp.concatenate(
        [self_inward, jnp.pad(self_query_bias[:, None], ((0, 0), (0, lane - 1)))], axis=1
    )
    packed = jnp.concatenate(
        [jnp.stack(vectors).T, expand_bias.reshape(rows, -1)], axis=1
    )
    spread = packed.shape[1]
    packed = jnp.pad(packed, ((0, 0), (0, lane - spread)))
    two = jnp.concatenate(
        [self_outward, cross_query, cross_outward, cross_memory, packed], axis=1
    )

    one_depth = grid.from_depth(one)
    one_depth, two, rows_low_sent = together(one_depth, two, rows_low)

    one_block = grid.depth_block(one, one_depth)
    one_sides = grid.from_sides(one_block)
    two_depth = grid.from_depth(two)
    one_sides, two_depth, rows_low_sent = together(one_sides, two_depth, rows_low_sent)

    all_low = lax.all_gather(rows_low_sent, "seq", axis=0, tiled=True)
    one_corners = grid.from_corners(one_sides)
    two_block = grid.depth_block(two, two_depth)
    one_corners, two_block = together(one_corners, two_block)

    two_sides = grid.from_sides(two_block)
    one_block_other, one_sides_other, one_corners_other = grid.swap(
        (one_block, one_sides, one_corners)
    )
    one_all = grid.whole(
        (one_block, one_sides, one_corners),
        (one_block_other, one_sides_other, one_corners_other),
    )
    self_query, self_context = one_all[:, :width], one_all[:, width : 3 * width]
    self_query_bias = one_all[:, 3 * width].astype(f32)
    query_self = (dense(rows_low, self_query) + self_query_bias).astype(bf16)
    two_sides, query_self, all_low, expand_weight = together(
        two_sides, query_self, all_low, expand_weight
    )

    two_corners = grid.from_corners(two_sides)
    expand_depth = grid.from_depth(expand_weight)
    context_self = dense(all_low, self_context).astype(bf16)
    blended_self, total_self = attend_forward(query_self, context_self, places, True)
    blended_self, two_corners, expand_depth, reduce_weight = together(
        blended_self, two_corners, expand_depth, reduce_weight
    )

    expand_block = grid.depth_block(expand_weight, expand_depth)
    two_block_other, two_sides_other, two_corners_other = grid.swap(
        (two_block, two_sides, two_corners)
    )
    two_block_other, two_sides_other, two_corners_other, expand_block = together(
        two_block_other, two_sides_other, two_corners_other, expand_block
    )
    expand_sides = grid.from_sides(expand_block)
    reduce_depth = grid.from_depth(reduce_weight)
    two_all = grid.whole(
        (two_block, two_sides, two_corners),
        (two_block_other, two_sides_other, two_corners_other),
    )
    packed = two_all[:, 5 * width : 5 * width + spread].astype(f32)
    (
        self_query_bias,
        self_value_bias,
        self_output_bias,
        first_gain,
        first_shift,
        cross_query_bias,
        cross_value_bias,
        cross_output_bias,
        second_gain,
        second_shift,
        reduce_bias,
        third_gain,
        third_shift,
    ) = [line for line in packed[:, : len(vectors)].T]
    expand_bias = packed[:, len(vectors) :].reshape(-1)
    self_outward, cross_query, cross_outward = [
        two_all[:, i * width : (i + 1) * width] for i in range(3)
    ]
    cross_context = two_all[:, 3 * width : 5 * width]
    blended_self = (blended_self + self_value_bias).astype(bf16)
    pre_first = residual_scale * rows_in + dense(blended_self, self_outward) + self_output_bias
    after_self = norm_layer(pre_first, first_gain, first_shift)
    after_self_low = after_self.astype(bf16)
    query_cross = (dense(after_self_low, cross_query) + cross_query_bias).astype(bf16)
    query_cross, expand_sides, reduce_depth, memory_low = together(
        query_cross, expand_sides, reduce_depth, memory_low
    )

    all_memory = lax.all_gather(memory_low, "seq", axis=0, tiled=True)
    reduce_block = grid.depth_block(reduce_weight, reduce_depth)
    expand_corners = grid.from_corners(expand_sides)
    reduce_sides = grid.from_sides(reduce_block)
    (expand_corners,) = together(expand_corners)
    expand_block_other, expand_sides_other, expand_corners_other = grid.swap(
        (expand_block, expand_sides, expand_corners)
    )
    expand_all = grid.whole(
        (expand_block, expand_sides, expand_corners),
        (expand_block_other, expand_sides_other, expand_corners_other),
        expand_weight.shape[1] // width,
    )
    picks = [
        grid.picked(left) for left in (rows_low, blended_self, after_self_low)
    ] + [turned(all_low)]
    expand_all, reduce_sides, all_memory, picks = together(
        expand_all, reduce_sides, all_memory, picks
    )

    reduce_corners = grid.from_corners(reduce_sides)
    reduce_block_other = grid.swap(reduce_block)
    reduce_sides_other = grid.swap(reduce_sides)
    context_cross = dense(all_memory, cross_context).astype(bf16)
    blended_cross, total_cross = attend_forward(query_cross, context_cross, places, False)
    memory_turned = turned(all_memory)
    (
        reduce_corners,
        blended_cross,
        reduce_block_other,
        reduce_sides_other,
        memory_turned,
    ) = together(
        reduce_corners, blended_cross, reduce_block_other, reduce_sides_other, memory_turned
    )

    reduce_corners_other = grid.swap(reduce_corners)
    blended_cross = (blended_cross + cross_value_bias).astype(bf16)
    pre_second = (
        residual_scale * after_self + dense(blended_cross, cross_outward) + cross_output_bias
    )
    after_cross = norm_layer(pre_second, second_gain, second_shift)
    cross_low = after_cross.astype(bf16)
    reduce_all = grid.whole(
        (reduce_block, reduce_sides, reduce_corners),
        (reduce_block_other, reduce_sides_other, reduce_corners_other),
    )
    expanded, hidden, reduced = feed_forward(cross_low, expand_all, reduce_all, expand_bias)
    pre_third = residual_scale * after_cross + reduced + reduce_bias
    result = norm_layer(pre_third, third_gain, third_shift)

    grad_out = cotangent.reshape(group_len, width) * pair_mask.astype(f32)[0]
    norm_back = jax.vjp(norm_layer, pre_third, third_gain, third_shift)[1]
    grad_third, third_gain_grad, third_shift_grad = norm_back(grad_out)
    reduce_bias_grad = jnp.sum(grad_third, axis=0)
    low_third = grad_third.astype(bf16)
    expanded_low, expand_bias_grad, grad_cross = feed_backward(
        low_third, expand_all, reduce_all, expanded
    )
    hidden_other, hidden_own = grid.picked(hidden)
    (reduce_sent,) = grid.halves((hidden_other,), low_third)
    reduce_sent, expanded_low, grad_cross, low_third = together(
        reduce_sent, expanded_low, grad_cross, low_third
    )

    reduce_got = grid.swap(reduce_sent)
    expand_sent, expand_kept = grid.halves(grid.picked(cross_low), expanded_low)
    grad_cross = residual_scale * grad_third + grad_cross
    norm_back = jax.vjp(norm_layer, pre_second, second_gain, second_shift)[1]
    grad_second, second_gain_grad, second_shift_grad = norm_back(grad_cross)
    cross_output_bias_grad = jnp.sum(grad_second, axis=0)
    second_low = grad_second.astype(bf16)
    grad_blended = times_transposed(second_low, cross_outward).astype(bf16)
    out_sent, out_kept = grid.halves(grid.picked(blended_cross), second_low)
    (reduce_kept,) = grid.halves((hidden_own,), low_third)
    (
        grad_blended,
        reduce_got,
        reduce_kept,
        expand_sent,
        expand_kept,
        out_sent,
        out_kept,
    ) = together(
        grad_blended, reduce_got, reduce_kept, expand_sent, expand_kept, out_sent, out_kept
    )

    reduce_group = [[reduce_kept, reduce_got]]
    reduce_sends = grid.corner_sends(reduce_group)
    reduce_sends, grad_blended, expand_sent, out_sent = together(
        reduce_sends, grad_blended, expand_sent, out_sent
    )
    reduce_corners = grid.corner_moves(reduce_sends)
    expand_got, out_got = grid.swap((expand_sent, out_sent))
    grad_query_cross, grad_context_cross = attend_backward(
        query_cross, context_cross, places, total_cross, grad_blended, False
    )
    grad_query_cross, grad_context_cross, reduce_corners, expand_got, out_got = together(
        grad_query_cross, grad_context_cross, reduce_corners, expand_got, out_got
    )

    reduce_sends = grid.side_sends(reduce_group, reduce_corners)
    reduce_sends, grad_query_cross, grad_context_cross = together(
        reduce_sends, grad_query_cross, grad_context_cross
    )
    reduce_sides = grid.side_moves(reduce_sends)
    memory_part = context_back(grad_context_cross, two_all, 3)
    context_sent, context_kept = grid.context_halves(memory_turned, grad_context_cross)
    grad_query_cross, memory_part, reduce_sides, context_sent, context_kept = together(
        grad_query_cross, memory_part, reduce_sides, context_sent, context_kept
    )

    expand_group = [[expand_kept, expand_got], [out_kept, out_got]]
    expand_sends = grid.corner_sends(expand_group)
    reduce_chip = grid.chip_sum(reduce_group, reduce_sides)
    expand_sends, reduce_chip, grad_query_cross, memory_part = together(
        expand_sends, reduce_chip, grad_query_cross, memory_part
    )
    expand_corners = grid.corner_moves(expand_sends)
    reduce_grad = lax.psum_scatter(reduce_chip, "seq", scatter_dimension=0)
    memory_grad = lax.psum_scatter(memory_part, "seq", scatter_dimension=0, tiled=True)
    cross_query_bias_grad = jnp.sum(grad_query_cross, axis=0)
    query_cross_low = grad_query_cross.astype(bf16)
    grad_self = residual_scale * grad_second + times_transposed(query_cross_low, cross_query)
    norm_back = jax.vjp(norm_layer, pre_first, first_gain, first_shift)[1]
    grad_first, first_gain_grad, first_shift_grad = norm_back(grad_self)
    self_output_bias_grad = jnp.sum(grad_first, axis=0)
    first_low = grad_first.astype(bf16)
    outward_sent, outward_kept = grid.halves(picks[1], first_low)
    grad_blended = times_transposed(first_low, self_outward).astype(bf16)
    query_sent, query_kept = grid.halves(picks[2], query_cross_low)
    grad_blended, expand_corners, outward_sent, outward_kept, query_sent, query_kept = together(
        grad_blended, expand_corners, outward_sent, outward_kept, query_sent, query_kept
    )

    expand_sends = grid.side_sends(expand_group, expand_corners)
    expand_sends, grad_blended, context_sent, query_sent, outward_sent = together(
        expand_sends, grad_blended, context_sent, query_sent, outward_sent
    )
    expand_sides = grid.side_moves(expand_sends)
    context_got, query_got, outward_got = grid.swap((context_sent, query_sent, outward_sent))
    cross_group = [
        [query_kept, query_got],
        [context_kept, context_got],
        [outward_kept, outward_got],
    ]
    grad_query_self, grad_context_self = attend_backward(
        query_self, context_self, places, total_self, grad_blended, True
    )
    inputs_part = context_back(grad_context_self, one_all, 1)
    context_sent, context_kept = grid.context_halves(picks[3], grad_context_self)
    query_self_low = grad_query_self.astype(bf16)
    query_sent, query_kept = grid.halves(picks[0], query_self_low)
    (
        cross_group,
        expand_sides,
        inputs_part,
        grad_query_self,
        grad_context_self,
        query_self_low,
        query_sent,
        context_sent,
        query_kept,
        context_kept,
        reduce_grad,
    ) = together(
        cross_group,
        expand_sides,
        inputs_part,
        grad_query_self,
        grad_context_self,
        query_self_low,
        query_sent,
        context_sent,
        query_kept,
        context_kept,
        reduce_grad,
    )

    inputs_grad = lax.psum_scatter(inputs_part, "seq", scatter_dimension=0, tiled=True)
    cross_sends = grid.corner_sends(cross_group)
    lines = (
        self_output_bias_grad,
        first_gain_grad,
        first_shift_grad,
        cross_query_bias_grad,
        cross_output_bias_grad,
        second_gain_grad,
        second_shift_grad,
        reduce_bias_grad,
        third_gain_grad,
        third_shift_grad,
        expand_bias_grad,
    )
    cross_sends, grad_query_self, grad_context_self, grad_context_cross, lines = together(
        cross_sends, grad_query_self, grad_context_self, grad_context_cross, lines
    )
    cross_corners = grid.corner_moves(cross_sends)
    expand_chip = grid.chip_sum(expand_group, expand_sides)
    expand_grad = lax.psum_scatter(expand_chip, "seq", scatter_dimension=0)
    self_query_bias_grad = jnp.sum(grad_query_self, axis=0)
    self_value_bias_grad = jnp.sum(grad_context_self[:, width:].astype(f32), axis=0)
    cross_value_bias_grad = jnp.sum(grad_context_cross[:, width:].astype(f32), axis=0)
    vector_grads = jnp.concatenate(
        [
            jnp.stack(
                (self_query_bias_grad, self_value_bias_grad)
                + tuple(lines[:4])
                + (cross_value_bias_grad,)
                + tuple(lines[4:10])
            ).T,
            lines[10].reshape(width, -1),
        ],
        axis=1,
    )
    vector_grads = jnp.pad(vector_grads, ((0, 0), (0, lane - spread)))
    vector_grads = vector_grads.reshape(devices, rows, lane)
    vector_sent, vector_kept = grid.vector_halves(vector_grads)
    cross_corners, vector_sent, vector_kept, expand_chip = together(
        cross_corners, vector_sent, vector_kept, expand_chip
    )

    cross_sends = grid.side_sends(cross_group, cross_corners)
    cross_sends, query_sent, context_sent, vector_sent = together(
        cross_sends, query_sent, context_sent, vector_sent
    )
    cross_sides = grid.side_moves(cross_sends)
    query_got, context_got, vector_got = grid.swap((query_sent, context_sent, vector_sent))
    cross_sides, query_got, context_got, vector_got, memory_grad = together(
        cross_sides, query_got, context_got, vector_got, memory_grad
    )

    self_group = [
        [query_kept, query_got],
        [context_kept, context_got],
        [vector_kept, vector_got],
    ]
    self_sends = grid.corner_sends(self_group)
    cross_chip = grid.chip_sum(cross_group, cross_sides)
    self_sends, cross_chip, query_self_low = together(self_sends, cross_chip, query_self_low)
    self_corners = grid.corner_moves(self_sends)
    cross_grad = lax.psum_scatter(cross_chip, "seq", scatter_dimension=0)
    inputs_base = residual_scale * grad_first + times_transposed(query_self_low, self_query)
    inputs_base, self_corners, inputs_grad = together(inputs_base, self_corners, inputs_grad)

    self_sends = grid.side_sends(self_group, self_corners)
    self_sides = grid.side_moves(self_sends)
    reduce_grad = reduce_grad.astype(f32)
    expand_grad = expand_grad.astype(f32)
    expand_grad, cross_out_grad = expand_grad[:, :-width], expand_grad[:, -width:]
    memory_grad = memory_grad.astype(f32)
    inputs_grad = inputs_base + inputs_grad.astype(f32)
    self_sides, reduce_grad, expand_grad, cross_out_grad, memory_grad, inputs_grad = together(
        self_sides, reduce_grad, expand_grad, cross_out_grad, memory_grad, inputs_grad
    )

    self_chip = grid.chip_sum(self_group, self_sides)
    self_sends = grid.depth_sends(self_chip)
    self_depths = grid.depth_moves(self_sends)
    self_depths, cross_grad = together(self_depths, cross_grad)
    cross_grad = cross_grad.astype(f32)
    cross_query_grad = cross_grad[:, :width]
    cross_context_grad = cross_grad[:, width : 3 * width]
    self_out_grad = cross_grad[:, 3 * width :]
    self_grad = grid.share(self_chip, self_depths)
    self_inward_grad, share = self_grad[:, : 3 * width], self_grad[:, 3 * width :]
    (
        self_query_bias_grad,
        self_value_bias_grad,
        self_output_bias_grad,
        first_gain_grad,
        first_shift_grad,
        cross_query_bias_grad,
        cross_value_bias_grad,
        cross_output_bias_grad,
        second_gain_grad,
        second_shift_grad,
        reduce_bias_grad,
        third_gain_grad,
        third_shift_grad,
    ) = [line for line in share[:, : len(vectors)].T]
    expand_bias_grad = share[:, len(vectors) : spread].reshape(-1)

    return (
        result.reshape(pair_count, group_len, width),
        inputs_grad.reshape(pair_count, group_len, width),
        memory_grad.reshape(pair_count, group_len, width),
        self_inward_grad,
        self_out_grad,
        self_query_bias_grad,
        self_value_bias_grad,
        self_output_bias_grad,
        first_gain_grad,
        first_shift_grad,
        cross_query_grad,
        cross_context_grad,
        cross_out_grad,
        cross_query_bias_grad,
        cross_value_bias_grad,
        cross_output_bias_grad,
        second_gain_grad,
        second_shift_grad,
        expand_grad,
        expand_bias_grad,
        reduce_grad,
        reduce_bias_grad,
        third_gain_grad,
        third_shift_grad,
    )


def solution(mesh):
    rows = P(("dp", "seq"), None)
    vector = P(("dp", "seq"))
    tokens = P("dp", "seq", None)
    in_specs = (
        (tokens, tokens, P("dp", None), P("dp"), tokens)
        + (rows, rows)
        + (vector,) * 5
        + (rows,) * 3
        + (vector,) * 5
        + (rows, vector, rows)
        + (vector,) * 3
    )
    out_specs = (
        (tokens,) * 3
        + (rows, rows)
        + (vector,) * 5
        + (rows,) * 3
        + (vector,) * 5
        + (rows, vector, rows)
        + (vector,) * 3
    )
    return jax.shard_map(
        functools.partial(local, Grid(mesh)),
        mesh=mesh,
        in_specs=in_specs,
        out_specs=out_specs,
        check_vma=False,
    )
```

```python
import functools

import jax
import jax.numpy as jnp
from jax import lax
from jax.experimental import pallas as pl
from jax.experimental.pallas import tpu as pltpu
from jax.sharding import PartitionSpec as P

HEADS = 16
HEAD_DIM = 64
PAIR = 2 * HEAD_DIM

residual_scale = 4.16
epsilon = 1e-05
score_scale = 0.125
negative_fill = -1e30
bf16 = jnp.bfloat16
f32 = jnp.float32


def norm_layer(values, gain_vector, shift_vector):
    middle = jnp.mean(values, axis=-1, keepdims=True)
    centred = values - middle
    spread = jnp.mean(centred * centred, axis=-1, keepdims=True)
    return centred * lax.rsqrt(spread + epsilon) * gain_vector + shift_vector


def gelu_tanh(values):
    return (
        0.5
        * values
        * (1.0 + jnp.tanh(0.7978845608028654 * (values + 0.044715 * values * values * values)))
    )


def dense(left_side, right_side):
    return jnp.dot(left_side, right_side, preferred_element_type=f32)


def times_transposed(left_side, right_side):
    return lax.dot_general(
        left_side, right_side, (((1,), (1,)), ((), ())), preferred_element_type=f32
    )


def transposed_times(left_side, right_side):
    return lax.dot_general(
        left_side, right_side, (((0,), (0,)), ((), ())), preferred_element_type=f32
    )


def lane_head(shape, head):
    lane = lax.broadcasted_iota(jnp.int32, shape, 1)
    return (lane < HEAD_DIM) if head == 0 else (lane >= HEAD_DIM)


def masked_scores(scores, place_ref, causal, group_len):
    if not causal:
        return scores
    blocks = scores.shape[0] // group_len
    own = place_ref[0, blocks]
    diff = lax.broadcasted_iota(jnp.int32, (group_len, group_len), 0) - lax.broadcasted_iota(
        jnp.int32, (group_len, group_len), 1
    )
    parts = []
    for block in range(blocks):
        reach = (own - place_ref[0, block]) * group_len
        part = scores[block * group_len : (block + 1) * group_len]
        parts.append(jnp.where(diff <= reach, part, negative_fill))
    return jnp.concatenate(parts, axis=0)


def attend_forward_kernel(causal, place_ref, q_ref, k_ref, v_ref, o_ref, total_ref):
    group_len = q_ref.shape[0]
    heads = [(part, head) for part in range(q_ref.shape[1] // PAIR) for head in range(2)]

    def lanes(part):
        return slice(part * PAIR, (part + 1) * PAIR)

    def scores_of(part, head):
        scaled = q_ref[:, lanes(part)] * jnp.asarray(score_scale, bf16)
        own = jnp.where(lane_head(scaled.shape, head), scaled, jnp.zeros_like(scaled))
        return times_transposed(k_ref[:, lanes(part)], own)

    ahead = [scores_of(*at) for at in heads[:2]]
    outs = []
    for i, (part, head) in enumerate(heads):
        if i + 2 < len(heads):
            ahead.append(scores_of(*heads[i + 2]))
        here = masked_scores(ahead[i], place_ref, causal, group_len)
        top = jnp.max(here, axis=0, keepdims=True)
        weights = jnp.exp(here - top)
        total = jnp.sum(weights, axis=0, keepdims=True)
        blended = transposed_times(v_ref[:, lanes(part)], weights.astype(bf16)) / total
        outs.append(blended)
        total_ref[part, head : head + 1, :] = top + jnp.log(total)
        if head == 1:
            row = lax.broadcasted_iota(jnp.int32, blended.shape, 0)
            o_ref[:, lanes(part)] = (
                jnp.where(row < HEAD_DIM, outs[-2], outs[-1]).T.astype(bf16)
            )


def attend_backward_kernel(
    causal, place_ref, q_ref, k_ref, v_ref, total_ref, g_ref, dq_ref, dkv_ref, held, sems
):
    group_len = q_ref.shape[0]
    both = q_ref.shape[1]
    heads = [(part, head) for part in range(both // PAIR) for head in range(2)]
    step, steps = pl.program_id(0), pl.num_programs(0)
    slot = lax.rem(step, 2)
    width = dkv_ref.shape[1] // 2

    def moves(at, slot):
        return [
            pltpu.make_async_copy(
                held.at[slot, part],
                dkv_ref.at[:, pl.ds(pl.multiple_of(part * width + at * both, both), both)],
                sems.at[slot, part],
            )
            for part in range(2)
        ]

    @pl.when(step >= 2)
    def _():
        for move in moves(step - 2, slot):
            move.wait()

    def lanes(part):
        return slice(part * PAIR, (part + 1) * PAIR)

    def start_of(part, head):
        scaled = q_ref[:, lanes(part)] * jnp.asarray(score_scale, bf16)
        grads = g_ref[:, lanes(part)]
        mine = lane_head(scaled.shape, head)
        own = jnp.where(mine, scaled, jnp.zeros_like(scaled))
        grad = jnp.where(mine, grads, jnp.zeros_like(grads))
        return (
            own,
            grad,
            times_transposed(k_ref[:, lanes(part)], own),
            times_transposed(v_ref[:, lanes(part)], grad),
        )

    ahead = [start_of(*at) for at in heads[:2]]
    dqs, dks, dvs = [], [], []
    for i, (part, head) in enumerate(heads):
        if i + 2 < len(heads):
            ahead.append(start_of(*heads[i + 2]))
        own, grad, scores, dprob = ahead[i]
        here = masked_scores(scores, place_ref, causal, group_len)
        weights = jnp.exp(here - total_ref[part, head : head + 1, :])
        dvs.append(dense(weights.astype(bf16), grad))
        delta = jnp.sum(dprob * weights, axis=0, keepdims=True)
        dscore = (weights * (dprob - delta)).astype(bf16)
        dks.append(dense(dscore, own))
        dqs.append(transposed_times(k_ref[:, lanes(part)], dscore))
        if head == 1:
            row = lax.broadcasted_iota(jnp.int32, dqs[0].shape, 0)
            dq_ref[:, lanes(part)] = (
                jnp.where(row < HEAD_DIM, dqs[-2], dqs[-1]).T * score_scale
            )
            held[slot, 0, :, lanes(part)] = (dks[-2] + dks[-1]).astype(bf16)
            held[slot, 1, :, lanes(part)] = (dvs[-2] + dvs[-1]).astype(bf16)
    for move in moves(step, slot):
        move.start()

    @pl.when(step == steps - 1)
    def _():
        for move in moves(step - 1, 1 - slot):
            move.wait()
        for move in moves(step, slot):
            move.wait()


def attention_specs(group_len, length, pairs):
    row = pl.BlockSpec((group_len, 2 * PAIR), lambda h: (0, h))
    keys = pl.BlockSpec((length, 2 * PAIR), lambda h: (0, h))
    values = pl.BlockSpec((length, 2 * PAIR), lambda h: (0, h + pairs // 2))
    total = pl.BlockSpec((2, 2, group_len), lambda h: (h, 0, 0))
    place = pl.BlockSpec(memory_space=pltpu.SMEM)
    return place, row, keys, values, total


FREE = pl.CostEstimate(flops=1, bytes_accessed=1, transcendentals=0)
ROOM = pltpu.CompilerParams(vmem_limit_bytes=24 * 1024 * 1024)
WIDE_ROOM = pltpu.CompilerParams(vmem_limit_bytes=48 * 1024 * 1024)


def attend_forward(query_rows, context_rows, places, causal):
    group_len, width = query_rows.shape
    length = context_rows.shape[0]
    pairs = width // PAIR
    place, row, keys, values, total = attention_specs(group_len, length, pairs)
    return pl.pallas_call(
        functools.partial(attend_forward_kernel, causal),
        grid=(pairs // 2,),
        in_specs=[place, row, keys, values],
        out_specs=[row, total],
        out_shape=[
            jax.ShapeDtypeStruct((group_len, width), bf16),
            jax.ShapeDtypeStruct((pairs, 2, group_len), f32),
        ],
        compiler_params=WIDE_ROOM,
        cost_estimate=FREE,
    )(places, query_rows, context_rows, context_rows)


def attend_backward(query_rows, context_rows, places, totals, grads, causal):
    group_len, width = query_rows.shape
    length = context_rows.shape[0]
    pairs = width // PAIR
    place, row, keys, values, total = attention_specs(group_len, length, pairs)
    return pl.pallas_call(
        functools.partial(attend_backward_kernel, causal),
        grid=(pairs // 2,),
        in_specs=[place, row, keys, values, total, row],
        out_specs=[row, pl.BlockSpec(memory_space=pl.ANY)],
        out_shape=[
            jax.ShapeDtypeStruct((group_len, width), f32),
            jax.ShapeDtypeStruct((length, 2 * width), bf16),
        ],
        scratch_shapes=[
            pltpu.VMEM((2, 2, length, 2 * PAIR), bf16),
            pltpu.SemaphoreType.DMA((2, 2)),
        ],
        compiler_params=WIDE_ROOM,
        cost_estimate=FREE,
    )(places, query_rows, context_rows, context_rows, totals, grads)


def context_back_kernel(g_ref, k_ref, v_ref, out_ref):
    width = k_ref.shape[1]
    out_ref[...] = (
        times_transposed(g_ref[:, :width], k_ref[...])
        + times_transposed(g_ref[:, width:], v_ref[...])
    ).astype(bf16)


def context_back(grads, weights, start):
    length, both = grads.shape
    width = both // 2
    each = width // 4
    return pl.pallas_call(
        context_back_kernel,
        grid=(4,),
        in_specs=[
            pl.BlockSpec((length, both), lambda j: (0, 0)),
            pl.BlockSpec((each, width), lambda j: (j, start)),
            pl.BlockSpec((each, width), lambda j: (j, start + 1)),
        ],
        out_specs=pl.BlockSpec((length, each), lambda j: (0, j)),
        out_shape=jax.ShapeDtypeStruct((length, width), bf16),
        compiler_params=WIDE_ROOM,
        cost_estimate=FREE,
    )(grads, weights, weights)


def context_halves_kernel(where_ref, other_ref, own_ref, g_ref, sent_ref, kept_ref):
    rows = sent_ref.shape[0]
    grads = g_ref[...]
    sent_ref[...] = dense(other_ref[...].reshape(rows, -1), grads).astype(bf16)
    kept_ref[...] = dense(own_ref[...].reshape(rows, -1), grads).astype(bf16)


def turn_kernel(x_ref, out_ref):
    out_ref[...] = x_ref[...].T


def turned(values):
    rows, columns = values.shape
    return pl.pallas_call(
        turn_kernel,
        grid=(columns // PAIR,),
        in_specs=[pl.BlockSpec((rows, PAIR), lambda j: (0, j))],
        out_specs=pl.BlockSpec((PAIR, rows), lambda j: (j, 0)),
        out_shape=jax.ShapeDtypeStruct((columns, rows), values.dtype),
        compiler_params=ROOM,
        cost_estimate=FREE,
    )(values)


def feed_forward_kernel(x_ref, e_ref, r_ref, b_ref, expanded_ref, hidden_ref, out_ref):
    step = pl.program_id(0)
    wide = b_ref.shape[-1]
    expanded = dense(x_ref[...], e_ref[...].reshape(-1, wide)) + b_ref[...]
    expanded_ref[0] = expanded
    hidden = gelu_tanh(expanded).astype(bf16)
    hidden_ref[...] = hidden
    part = dense(hidden, r_ref[...].reshape(wide, -1))

    @pl.when(step == 0)
    def _():
        out_ref[...] = part

    @pl.when(step > 0)
    def _():
        out_ref[...] += part


def feed_backward_kernel(g_ref, e_ref, r_ref, expanded_ref, low_ref, bias_ref, out_ref):
    step = pl.program_id(0)
    wide = low_ref.shape[-1]
    grad_hidden = times_transposed(g_ref[...], r_ref[...].reshape(wide, -1))
    u = expanded_ref[0]
    square = u * u
    bent = jnp.tanh(0.7978845608028654 * (u + 0.044715 * square * u))
    slope = 0.5 * (1.0 + bent) + 0.5 * u * (1.0 - bent * bent) * (
        0.7978845608028654 * (1.0 + 3.0 * 0.044715 * square)
    )
    grad = grad_hidden * slope
    bias_ref[...] = jnp.sum(grad, axis=0, keepdims=True)
    low = grad.astype(bf16)
    low_ref[...] = low
    part = times_transposed(low, e_ref[...].reshape(-1, wide))

    @pl.when(step == 0)
    def _():
        out_ref[...] = part

    @pl.when(step > 0)
    def _():
        out_ref[...] += part


def feed_specs(count, width, each):
    return (
        pl.BlockSpec((count, width), lambda j: (0, 0)),
        pl.BlockSpec((1, width, each), lambda j: (j, 0, 0)),
        pl.BlockSpec((each, width), lambda j: (j, 0)),
        pl.BlockSpec((count, each), lambda j: (0, j)),
        pl.BlockSpec((1, each), lambda j: (0, j)),
        pl.BlockSpec((1, count, each), lambda j: (j, 0, 0)),
    )


def feed_forward(rows, expand_all, reduce_all, bias):
    count, width = rows.shape
    wide = reduce_all.shape[0]
    each = expand_all.shape[2]
    whole, first, second, part, line, block = feed_specs(count, width, each)
    return pl.pallas_call(
        feed_forward_kernel,
        grid=(wide // each,),
        in_specs=[whole, first, second, line],
        out_specs=[block, part, whole],
        out_shape=[
            jax.ShapeDtypeStruct((wide // each, count, each), f32),
            jax.ShapeDtypeStruct((count, wide), bf16),
            jax.ShapeDtypeStruct((count, width), f32),
        ],
        compiler_params=WIDE_ROOM,
        cost_estimate=FREE,
    )(rows, expand_all, reduce_all, bias.reshape(1, -1))


def feed_backward(grads, expand_all, reduce_all, expanded):
    count, width = grads.shape
    wide = reduce_all.shape[0]
    each = expand_all.shape[2]
    whole, first, second, part, line, block = feed_specs(count, width, each)
    return pl.pallas_call(
        feed_backward_kernel,
        grid=(wide // each,),
        in_specs=[whole, first, second, block],
        out_specs=[part, line, whole],
        out_shape=[
            jax.ShapeDtypeStruct((count, wide), bf16),
            jax.ShapeDtypeStruct((1, wide), f32),
            jax.ShapeDtypeStruct((count, width), f32),
        ],
        compiler_params=WIDE_ROOM,
        cost_estimate=FREE,
    )(grads, expand_all, reduce_all, expanded)


class Grid:
    def __init__(self, mesh):
        self.dp = mesh.shape["dp"]
        depth = mesh.shape["seq"]
        core = 2 if self.dp % 2 == 0 else 1
        chips = self.dp // core
        outer = 1
        while outer * outer < chips:
            outer *= 2
        inner = chips // outer
        self.sizes = {"outer": outer, "inner": inner, "core": core, "depth": depth}
        self.strides = {"outer": inner * core, "inner": core, "core": 1}

    def index(self, dim):
        if dim == "depth":
            return lax.axis_index("seq")
        return (lax.axis_index("dp") // self.strides[dim]) % self.sizes[dim]

    def shift(self, value, dim, step):
        size = self.sizes[dim]
        if dim == "depth":
            return lax.ppermute(value, "seq", [(i, (i + step) % size) for i in range(size)])
        stride = self.strides[dim]
        pairs = []
        for device in range(self.dp):
            at = (device // stride) % size
            pairs.append((device, device + ((at + step) % size - at) * stride))
        return lax.ppermute(value, "dp", pairs)

    def steps(self, dim):
        return range(1, self.sizes[dim])

    def from_depth(self, shard):
        return [self.shift(shard, "depth", step) for step in self.steps("depth")]

    def depth_block(self, shard, pieces):
        size, me = self.sizes["depth"], self.index("depth")
        return jnp.stack(
            [lax.select_n((me - at) % size, shard, *pieces) for at in range(size)]
        )

    def from_sides(self, block):
        return (
            [self.shift(block, "inner", step) for step in self.steps("inner")],
            [self.shift(block, "outer", step) for step in self.steps("outer")],
        )

    def from_corners(self, sides):
        along_inner, along_outer = sides
        half = along_inner[0].shape[0] // 2
        top = jnp.stack([block[:half] for block in along_inner])
        bottom = jnp.stack([block[half:] for block in along_outer])
        return (
            [self.shift(top, "outer", step) for step in self.steps("outer")],
            [self.shift(bottom, "inner", step) for step in self.steps("inner")],
        )

    def swap(self, pieces):
        return jax.tree.map(lambda piece: self.shift(piece, "core", 1), pieces)

    def whole(self, own, others, blocks=1):
        outer, inner, core = (self.sizes[n] for n in ("outer", "inner", "core"))
        each, total = own[0].shape[-2], own[0].shape[-1]
        columns = total // blocks
        height = self.sizes["depth"] * each
        half = height // 2
        pieces, places = [], []

        def add(piece, back_a, back_b, other, start):
            pieces.append(piece.reshape(-1, total))
            places.append((back_a, back_b, other, start))

        for other, (block, (along_inner, along_outer), (top, bottom)) in enumerate([own, others]):
            add(block, 0, 0, other, 0)
            for j, piece in enumerate(along_inner):
                add(piece, 0, j + 1, other, 0)
            for i, piece in enumerate(along_outer):
                add(piece, i + 1, 0, other, 0)
            for i in range(outer - 1):
                for j in range(inner - 1):
                    add(top[i][j], i + 1, j + 1, other, 0)
                    add(bottom[j][i], i + 1, j + 1, other, half)

        def kernel(*refs):
            out, sems = refs[len(pieces)], refs[len(pieces) + 1]
            device = lax.axis_index("dp")
            a = device // self.strides["outer"]
            b = lax.rem(device // self.strides["inner"], inner)
            c = lax.rem(device, core)
            copies = []
            for at, (ref, (back_a, back_b, other, start)) in enumerate(zip(refs, places)):
                to_a = lax.rem(a + (outer - back_a), outer)
                to_b = lax.rem(b + (inner - back_b), inner)
                to_c = lax.rem(c + other, core)
                index = (to_a * inner + to_b) * core + to_c
                for j in range(blocks):
                    copies.append(
                        pltpu.make_async_copy(
                            ref.at[:, pl.ds(j * columns, columns)],
                            out.at[j, index, pl.ds(start, ref.shape[0])],
                            sems.at[at, j],
                        )
                    )
            for copy in copies:
                copy.start()
            for copy in copies:
                copy.wait()

        anywhere = pl.BlockSpec(memory_space=pltpu.HBM)
        matrix = pl.pallas_call(
            kernel,
            in_specs=[anywhere] * len(pieces),
            out_specs=pl.BlockSpec(memory_space=pltpu.VMEM),
            out_shape=jax.ShapeDtypeStruct((blocks, outer * inner * core, height, columns), bf16),
            scratch_shapes=[pltpu.SemaphoreType.DMA((len(pieces), blocks))],
            compiler_params=WIDE_ROOM,
            cost_estimate=FREE,
        )(*pieces)
        matrix = matrix.reshape(blocks, -1, columns)
        return matrix if blocks > 1 else matrix[0]

    def picked(self, left_side):
        core = self.sizes["core"]
        count = self.sizes["outer"] * self.sizes["inner"]
        block = left_side.shape[1] // (count * core)
        me = self.index("core")
        even, odd = [
            [left_side[:, (core * j + i) * block : (core * j + i + 1) * block] for j in range(count)]
            for i in range(core)
        ]
        return tuple(
            jnp.concatenate(
                [jnp.where(me == 0, *((e, o) if own else (o, e))) for e, o in zip(even, odd)], axis=1
            )
            for own in (False, True)
        )

    def halves(self, picked, right_side):
        outer, inner, depth = self.sizes["outer"], self.sizes["inner"], self.sizes["depth"]
        each = picked[0].shape[1] // (outer * inner * depth)
        shape = (outer, inner, depth, each, right_side.shape[1])
        return tuple(
            transposed_times(chosen, right_side).astype(bf16).reshape(shape) for chosen in picked
        )

    def context_halves(self, turned, grads):
        outer, inner, core, depth = (self.sizes[n] for n in ("outer", "inner", "core", "depth"))
        height, rows = turned.shape
        block = height // (outer * inner * core)
        columns = grads.shape[1]
        each = columns // 4
        me = self.index("core")
        piece = (outer * inner, 1, block, rows)
        sent, kept = pl.pallas_call(
            context_halves_kernel,
            grid_spec=pltpu.PrefetchScalarGridSpec(
                num_scalar_prefetch=1,
                grid=(4,),
                in_specs=[
                    pl.BlockSpec(piece, lambda j, where: (0, where[0], 0, 0)),
                    pl.BlockSpec(piece, lambda j, where: (0, where[1], 0, 0)),
                    pl.BlockSpec((rows, each), lambda j, where: (0, j)),
                ],
                out_specs=[pl.BlockSpec((height // core, each), lambda j, where: (0, j))] * 2,
            ),
            out_shape=[jax.ShapeDtypeStruct((height // core, columns), bf16)] * 2,
            compiler_params=WIDE_ROOM,
            cost_estimate=FREE,
        )(
            jnp.stack([1 - me, me]).astype(jnp.int32),
            *([turned.reshape(outer * inner, core, block, rows)] * 2),
            grads,
        )
        shape = (outer, inner, depth, block // depth, columns)
        return sent.reshape(shape), kept.reshape(shape)

    def vector_halves(self, packed):
        core = self.sizes["core"]
        outer, inner, depth = self.sizes["outer"], self.sizes["inner"], self.sizes["depth"]
        split = packed.reshape((outer, inner, core, depth) + packed.shape[1:])
        me = self.index("core")
        even, odd = split[:, :, 0], split[:, :, 1]
        return jnp.where(me == 0, odd, even).astype(bf16), jnp.where(me == 0, even, odd)

    def sums(self, terms):
        return sum(term.astype(f32) for term in terms)

    def corner_sends(self, group):
        if self.square:
            top, bottom = self.block_sums(group, "corner", [])
            return [top], [bottom]
        outer, inner = self.sizes["outer"], self.sizes["inner"]
        a, b = self.index("outer"), self.index("inner")
        half = group[0][0].shape[2] // 2

        def block(terms, at_a, at_b, low, high):
            cut = [
                lax.dynamic_slice(
                    term,
                    (at_a % outer, at_b % inner, low, 0, 0),
                    (1, 1, high - low) + term.shape[3:],
                )
                for term in terms
            ]
            return self.sums(cut)[0, 0].astype(bf16)

        def joined(blocks):
            return jnp.concatenate(blocks, axis=-1) if len(blocks) > 1 else blocks[0]

        top = [
            jnp.stack(
                [
                    joined([block(terms, a + i, b + j, 0, half) for terms in group])
                    for j in self.steps("inner")
                ]
            )
            for i in self.steps("outer")
        ]
        bottom = [
            jnp.stack(
                [
                    joined([block(terms, a + i, b + j, half, 2 * half) for terms in group])
                    for i in self.steps("outer")
                ]
            )
            for j in self.steps("inner")
        ]
        return top, bottom

    def corner_moves(self, sends):
        top, bottom = sends
        return (
            [self.shift(send, "outer", step) for send, step in zip(top, self.steps("outer"))],
            [self.shift(send, "inner", step) for send, step in zip(bottom, self.steps("inner"))],
        )

    def side_sends(self, group, corners):
        top, bottom = corners
        if self.square:
            to_inner, to_outer = self.block_sums(group, "sides", [top[0], bottom[0]])
            return [to_inner], [to_outer]
        outer, inner = self.sizes["outer"], self.sizes["inner"]
        a, b = self.index("outer"), self.index("inner")
        half = group[0][0].shape[2] // 2

        def block(at_a, at_b, low, high, extra):
            sums, start = [], 0
            for terms in group:
                columns = terms[0].shape[-1]
                cut = [
                    lax.dynamic_slice(
                        term,
                        (at_a % outer, at_b % inner, low, 0, 0),
                        (1, 1, high - low) + term.shape[3:],
                    )[0, 0]
                    for term in terms
                ]
                cut += [piece[..., start : start + columns] for piece in extra]
                sums.append(self.sums(cut).astype(bf16))
                start += columns
            return jnp.concatenate(sums, axis=-1) if len(sums) > 1 else sums[0]

        to_inner = [
            jnp.concatenate(
                [
                    block(a, b + j, 0, half, [piece[j - 1] for piece in top]),
                    block(a, b + j, half, 2 * half, []),
                ]
            )
            for j in self.steps("inner")
        ]
        to_outer = [
            jnp.concatenate(
                [
                    block(a + i, b, 0, half, []),
                    block(a + i, b, half, 2 * half, [piece[i - 1] for piece in bottom]),
                ]
            )
            for i in self.steps("outer")
        ]
        return to_inner, to_outer

    def side_moves(self, sends):
        to_inner, to_outer = sends
        return [self.shift(send, "inner", step) for send, step in zip(to_inner, self.steps("inner"))] + [
            self.shift(send, "outer", step) for send, step in zip(to_outer, self.steps("outer"))
        ]

    def chip_terms(self, group, sides):
        a, b = self.index("outer"), self.index("inner")
        out, start = [], 0
        for terms in group:
            columns = terms[0].shape[-1]
            own = [
                lax.dynamic_slice(term, (a, b, 0, 0, 0), (1, 1) + term.shape[2:])[0, 0]
                for term in terms
            ]
            out.append(own + [piece[..., start : start + columns] for piece in sides])
            start += columns
        return out

    def chip_sum(self, group, sides):
        if self.square:
            total = sum(terms[0].shape[-1] for terms in group)
            return self.block_sums(group, "own", sides).reshape(
                self.sizes["depth"], -1, total
            )
        sums = [self.sums(terms).astype(bf16) for terms in self.chip_terms(group, sides)]
        return jnp.concatenate(sums, axis=-1) if len(sums) > 1 else sums[0]

    @property
    def square(self):
        return self.sizes["outer"] == 2 and self.sizes["inner"] == 2

    def block_sums(self, group, what, received):
        a, b = self.index("outer"), self.index("inner")
        place = {
            "corner": [(1 - a) * 2 + 1 - b],
            "sides": [a * 2 + 1 - b, (1 - a) * 2 + b],
            "own": [a * 2 + b],
        }[what]
        terms = [
            [term.reshape(4, -1, term.shape[-1]) for term in matrix] for matrix in group
        ]
        rows = terms[0][0].shape[1]
        half = rows // 2
        widths = [matrix[0].shape[-1] for matrix in terms]
        counts = [len(matrix) for matrix in terms]
        flat = [term for matrix in terms for term in matrix]
        received = [piece.reshape(-1, sum(widths)) for piece in received]

        def kernel(where_ref, *refs):
            terms_in, rest = refs[: len(flat)], refs[len(flat) :]
            got_in, rest = rest[: len(received)], rest[len(received) :]
            outs, rest = rest[: len(heights)], rest[len(heights) :]
            held, got, sems = rest[: len(flat)], rest[len(flat) : -1], rest[-1]
            copies = [
                pltpu.make_async_copy(
                    ref.at[where_ref[at]], held[i].at[at], sems.at[at * len(flat) + i]
                )
                for at in range(len(place))
                for i, ref in enumerate(terms_in)
            ]
            first_got = len(copies)
            copies += [
                pltpu.make_async_copy(ref, got[i], sems.at[first_got + i])
                for i, ref in enumerate(got_in)
            ]
            for copy in copies[first_got:] + copies[:first_got]:
                copy.start()
            for copy in copies[first_got:]:
                copy.wait()
            for at in range(len(place)):
                first, start = 0, 0
                for count, columns in zip(counts, widths):
                    for i in range(first, first + count):
                        copies[at * len(flat) + i].wait()
                    for low in range(0, columns, 512):
                        high = min(low + 512, columns)
                        here = slice(start + low, start + high)
                        value = sum(
                            ref[at, :, low:high].astype(f32) for ref in held[first : first + count]
                        )
                        if what == "corner":
                            outs[0][:, here] = value[:half].astype(bf16)
                            outs[1][:, here] = value[half:].astype(bf16)
                        elif what == "sides":
                            top, bottom = value[:half], value[half:]
                            if at == 0:
                                top = top + got[0][:, here].astype(f32)
                            else:
                                bottom = bottom + got[1][:, here].astype(f32)
                            outs[at][:half, here] = top.astype(bf16)
                            outs[at][half:, here] = bottom.astype(bf16)
                        else:
                            value = value + sum(ref[:, here].astype(f32) for ref in got)
                            outs[0][:, here] = value.astype(bf16)
                    first += count
                    start += columns

        heights = {"corner": [half, half], "sides": [rows, rows], "own": [rows]}[what]
        in_hbm = pl.BlockSpec(memory_space=pltpu.HBM)
        out = pl.pallas_call(
            kernel,
            in_specs=[pl.BlockSpec(memory_space=pltpu.SMEM)]
            + [in_hbm] * (len(flat) + len(received)),
            out_specs=[pl.BlockSpec(memory_space=pltpu.VMEM)] * len(heights),
            out_shape=[jax.ShapeDtypeStruct((height, sum(widths)), bf16) for height in heights],
            scratch_shapes=[
                pltpu.VMEM((len(place), rows, term.shape[-1]), term.dtype) for term in flat
            ]
            + [pltpu.VMEM(piece.shape, bf16) for piece in received]
            + [pltpu.SemaphoreType.DMA((len(place) * len(flat) + len(received),))],
            compiler_params=WIDE_ROOM,
            cost_estimate=FREE,
        )(jnp.stack(place).astype(jnp.int32), *flat, *received)
        return out[0] if what == "own" else out

    def depth_sends(self, chip):
        size, me = self.sizes["depth"], self.index("depth")
        return [
            lax.dynamic_index_in_dim(chip, (me + step) % size, 0, keepdims=False)
            for step in self.steps("depth")
        ]

    def depth_moves(self, sends):
        return [self.shift(send, "depth", step) for send, step in zip(sends, self.steps("depth"))]

    def share(self, chip, received):
        own = lax.dynamic_index_in_dim(chip, self.index("depth"), 0, keepdims=False)
        return self.sums([own] + received)


def together(*values):
    return lax.optimization_barrier(values)


def local(grid, *args):
    (
        inputs,
        memory,
        group_place,
        pair_mask,
        cotangent,
        self_inward,
        self_outward,
        self_query_bias,
        self_value_bias,
        self_output_bias,
        first_gain,
        first_shift,
        cross_query,
        cross_memory,
        cross_outward,
        cross_query_bias,
        cross_value_bias,
        cross_output_bias,
        second_gain,
        second_shift,
        expand_weight,
        expand_bias,
        reduce_weight,
        reduce_bias,
        third_gain,
        third_shift,
    ) = args
    pair_count, group_len, width = inputs.shape
    rows_in = inputs.reshape(group_len, width)
    rows_low = rows_in.astype(bf16)
    memory_low = memory.reshape(group_len, width).astype(bf16)

    vectors = (
        self_query_bias,
        self_value_bias,
        self_output_bias,
        first_gain,
        first_shift,
        cross_query_bias,
        cross_value_bias,
        cross_output_bias,
        second_gain,
        second_shift,
        reduce_bias,
        third_gain,
        third_shift,
    )
    rows = self_inward.shape[0]
    devices = width // rows
    places = jnp.concatenate(
        [
            group_place.reshape(1, -1),
            lax.dynamic_slice_in_dim(group_place, lax.axis_index("seq"), 1, axis=1),
        ],
        axis=1,
    )

    lane = 128
    one = jnp.concatenate(
        [self_inward, jnp.pad(self_query_bias[:, None], ((0, 0), (0, lane - 1)))], axis=1
    )
    packed = jnp.concatenate(
        [jnp.stack(vectors).T, expand_bias.reshape(rows, -1)], axis=1
    )
    spread = packed.shape[1]
    packed = jnp.pad(packed, ((0, 0), (0, lane - spread)))
    two = jnp.concatenate(
        [self_outward, cross_query, cross_outward, cross_memory, packed], axis=1
    )

    one_depth = grid.from_depth(one)
    one_depth, two, rows_low_sent = together(one_depth, two, rows_low)

    one_block = grid.depth_block(one, one_depth)
    one_sides = grid.from_sides(one_block)
    two_depth = grid.from_depth(two)
    one_sides, two_depth, rows_low_sent = together(one_sides, two_depth, rows_low_sent)

    all_low = lax.all_gather(rows_low_sent, "seq", axis=0, tiled=True)
    one_corners = grid.from_corners(one_sides)
    two_block = grid.depth_block(two, two_depth)
    one_corners, two_block = together(one_corners, two_block)

    two_sides = grid.from_sides(two_block)
    one_block_other, one_sides_other, one_corners_other = grid.swap(
        (one_block, one_sides, one_corners)
    )
    one_all = grid.whole(
        (one_block, one_sides, one_corners),
        (one_block_other, one_sides_other, one_corners_other),
    )
    self_query, self_context = one_all[:, :width], one_all[:, width : 3 * width]
    self_query_bias = one_all[:, 3 * width].astype(f32)
    query_self = (dense(rows_low, self_query) + self_query_bias).astype(bf16)
    two_sides, query_self, all_low, expand_weight = together(
        two_sides, query_self, all_low, expand_weight
    )

    two_corners = grid.from_corners(two_sides)
    expand_depth = grid.from_depth(expand_weight)
    context_self = dense(all_low, self_context).astype(bf16)
    blended_self, total_self = attend_forward(query_self, context_self, places, True)
    blended_self, two_corners, expand_depth, reduce_weight = together(
        blended_self, two_corners, expand_depth, reduce_weight
    )

    expand_block = grid.depth_block(expand_weight, expand_depth)
    two_block_other, two_sides_other, two_corners_other = grid.swap(
        (two_block, two_sides, two_corners)
    )
    two_block_other, two_sides_other, two_corners_other, expand_block = together(
        two_block_other, two_sides_other, two_corners_other, expand_block
    )
    expand_sides = grid.from_sides(expand_block)
    reduce_depth = grid.from_depth(reduce_weight)
    two_all = grid.whole(
        (two_block, two_sides, two_corners),
        (two_block_other, two_sides_other, two_corners_other),
    )
    packed = two_all[:, 5 * width : 5 * width + spread].astype(f32)
    (
        self_query_bias,
        self_value_bias,
        self_output_bias,
        first_gain,
        first_shift,
        cross_query_bias,
        cross_value_bias,
        cross_output_bias,
        second_gain,
        second_shift,
        reduce_bias,
        third_gain,
        third_shift,
    ) = [line for line in packed[:, : len(vectors)].T]
    expand_bias = packed[:, len(vectors) :].reshape(-1)
    self_outward, cross_query, cross_outward = [
        two_all[:, i * width : (i + 1) * width] for i in range(3)
    ]
    cross_context = two_all[:, 3 * width : 5 * width]
    blended_self = (blended_self + self_value_bias).astype(bf16)
    pre_first = residual_scale * rows_in + dense(blended_self, self_outward) + self_output_bias
    after_self = norm_layer(pre_first, first_gain, first_shift)
    after_self_low = after_self.astype(bf16)
    query_cross = (dense(after_self_low, cross_query) + cross_query_bias).astype(bf16)
    query_cross, expand_sides, reduce_depth, memory_low = together(
        query_cross, expand_sides, reduce_depth, memory_low
    )

    all_memory = lax.all_gather(memory_low, "seq", axis=0, tiled=True)
    reduce_block = grid.depth_block(reduce_weight, reduce_depth)
    expand_corners = grid.from_corners(expand_sides)
    reduce_sides = grid.from_sides(reduce_block)
    (expand_corners,) = together(expand_corners)
    expand_block_other, expand_sides_other, expand_corners_other = grid.swap(
        (expand_block, expand_sides, expand_corners)
    )
    expand_all = grid.whole(
        (expand_block, expand_sides, expand_corners),
        (expand_block_other, expand_sides_other, expand_corners_other),
        expand_weight.shape[1] // width,
    )
    picks = [
        grid.picked(left) for left in (rows_low, blended_self, after_self_low)
    ] + [turned(all_low)]
    expand_all, reduce_sides, all_memory, picks = together(
        expand_all, reduce_sides, all_memory, picks
    )

    reduce_corners = grid.from_corners(reduce_sides)
    reduce_block_other = grid.swap(reduce_block)
    reduce_sides_other = grid.swap(reduce_sides)
    context_cross = dense(all_memory, cross_context).astype(bf16)
    blended_cross, total_cross = attend_forward(query_cross, context_cross, places, False)
    reduce_corners, blended_cross, reduce_block_other, reduce_sides_other = together(
        reduce_corners, blended_cross, reduce_block_other, reduce_sides_other
    )

    reduce_corners_other = grid.swap(reduce_corners)
    blended_cross = (blended_cross + cross_value_bias).astype(bf16)
    pre_second = (
        residual_scale * after_self + dense(blended_cross, cross_outward) + cross_output_bias
    )
    after_cross = norm_layer(pre_second, second_gain, second_shift)
    cross_low = after_cross.astype(bf16)
    reduce_all = grid.whole(
        (reduce_block, reduce_sides, reduce_corners),
        (reduce_block_other, reduce_sides_other, reduce_corners_other),
    )
    expanded, hidden, reduced = feed_forward(cross_low, expand_all, reduce_all, expand_bias)
    pre_third = residual_scale * after_cross + reduced + reduce_bias
    result = norm_layer(pre_third, third_gain, third_shift)

    grad_out = cotangent.reshape(group_len, width) * pair_mask.astype(f32)[0]
    norm_back = jax.vjp(norm_layer, pre_third, third_gain, third_shift)[1]
    grad_third, third_gain_grad, third_shift_grad = norm_back(grad_out)
    reduce_bias_grad = jnp.sum(grad_third, axis=0)
    low_third = grad_third.astype(bf16)
    expanded_low, expand_bias_grad, grad_cross = feed_backward(
        low_third, expand_all, reduce_all, expanded
    )
    hidden_other, hidden_own = grid.picked(hidden)
    (reduce_sent,) = grid.halves((hidden_other,), low_third)
    reduce_sent, expanded_low, grad_cross, low_third = together(
        reduce_sent, expanded_low, grad_cross, low_third
    )

    reduce_got = grid.swap(reduce_sent)
    expand_sent, expand_kept = grid.halves(grid.picked(cross_low), expanded_low)
    grad_cross = residual_scale * grad_third + grad_cross
    norm_back = jax.vjp(norm_layer, pre_second, second_gain, second_shift)[1]
    grad_second, second_gain_grad, second_shift_grad = norm_back(grad_cross)
    cross_output_bias_grad = jnp.sum(grad_second, axis=0)
    second_low = grad_second.astype(bf16)
    grad_blended = times_transposed(second_low, cross_outward).astype(bf16)
    out_sent, out_kept = grid.halves(grid.picked(blended_cross), second_low)
    (reduce_kept,) = grid.halves((hidden_own,), low_third)
    (
        grad_blended,
        reduce_got,
        reduce_kept,
        expand_sent,
        expand_kept,
        out_sent,
        out_kept,
    ) = together(
        grad_blended, reduce_got, reduce_kept, expand_sent, expand_kept, out_sent, out_kept
    )

    reduce_group = [[reduce_kept, reduce_got]]
    reduce_sends = grid.corner_sends(reduce_group)
    reduce_sends, grad_blended, expand_sent, out_sent = together(
        reduce_sends, grad_blended, expand_sent, out_sent
    )
    reduce_corners = grid.corner_moves(reduce_sends)
    expand_got, out_got = grid.swap((expand_sent, out_sent))
    grad_query_cross, grad_context_cross = attend_backward(
        query_cross, context_cross, places, total_cross, grad_blended, False
    )
    grad_query_cross, grad_context_cross, reduce_corners, expand_got, out_got = together(
        grad_query_cross, grad_context_cross, reduce_corners, expand_got, out_got
    )

    reduce_sends = grid.side_sends(reduce_group, reduce_corners)
    reduce_sends, grad_query_cross, grad_context_cross = together(
        reduce_sends, grad_query_cross, grad_context_cross
    )
    reduce_sides = grid.side_moves(reduce_sends)
    memory_part = context_back(grad_context_cross, two_all, 3)
    context_sent, context_kept = grid.context_halves(
        turned(all_memory), grad_context_cross
    )
    grad_query_cross, memory_part, reduce_sides, context_sent, context_kept = together(
        grad_query_cross, memory_part, reduce_sides, context_sent, context_kept
    )

    expand_group = [[expand_kept, expand_got], [out_kept, out_got]]
    expand_sends = grid.corner_sends(expand_group)
    reduce_chip = grid.chip_sum(reduce_group, reduce_sides)
    expand_sends, reduce_chip, grad_query_cross, memory_part = together(
        expand_sends, reduce_chip, grad_query_cross, memory_part
    )
    expand_corners = grid.corner_moves(expand_sends)
    reduce_grad = lax.psum_scatter(reduce_chip, "seq", scatter_dimension=0)
    memory_grad = lax.psum_scatter(memory_part, "seq", scatter_dimension=0, tiled=True)
    cross_query_bias_grad = jnp.sum(grad_query_cross, axis=0)
    query_cross_low = grad_query_cross.astype(bf16)
    grad_self = residual_scale * grad_second + times_transposed(query_cross_low, cross_query)
    norm_back = jax.vjp(norm_layer, pre_first, first_gain, first_shift)[1]
    grad_first, first_gain_grad, first_shift_grad = norm_back(grad_self)
    self_output_bias_grad = jnp.sum(grad_first, axis=0)
    first_low = grad_first.astype(bf16)
    outward_sent, outward_kept = grid.halves(picks[1], first_low)
    grad_blended = times_transposed(first_low, self_outward).astype(bf16)
    query_sent, query_kept = grid.halves(picks[2], query_cross_low)
    grad_blended, expand_corners, outward_sent, outward_kept, query_sent, query_kept = together(
        grad_blended, expand_corners, outward_sent, outward_kept, query_sent, query_kept
    )

    expand_sends = grid.side_sends(expand_group, expand_corners)
    expand_sends, grad_blended, context_sent, query_sent, outward_sent = together(
        expand_sends, grad_blended, context_sent, query_sent, outward_sent
    )
    expand_sides = grid.side_moves(expand_sends)
    context_got, query_got, outward_got = grid.swap((context_sent, query_sent, outward_sent))
    cross_group = [
        [query_kept, query_got],
        [context_kept, context_got],
        [outward_kept, outward_got],
    ]
    grad_query_self, grad_context_self = attend_backward(
        query_self, context_self, places, total_self, grad_blended, True
    )
    context_sent, context_kept = grid.context_halves(picks[3], grad_context_self)
    query_self_low = grad_query_self.astype(bf16)
    query_sent, query_kept = grid.halves(picks[0], query_self_low)
    (
        cross_group,
        expand_sides,
        grad_query_self,
        grad_context_self,
        query_self_low,
        query_sent,
        context_sent,
        query_kept,
        context_kept,
        reduce_grad,
    ) = together(
        cross_group,
        expand_sides,
        grad_query_self,
        grad_context_self,
        query_self_low,
        query_sent,
        context_sent,
        query_kept,
        context_kept,
        reduce_grad,
    )

    cross_sends = grid.corner_sends(cross_group)
    lines = (
        self_output_bias_grad,
        first_gain_grad,
        first_shift_grad,
        cross_query_bias_grad,
        cross_output_bias_grad,
        second_gain_grad,
        second_shift_grad,
        reduce_bias_grad,
        third_gain_grad,
        third_shift_grad,
        expand_bias_grad,
    )
    cross_sends, grad_query_self, grad_context_self, grad_context_cross, lines = together(
        cross_sends, grad_query_self, grad_context_self, grad_context_cross, lines
    )
    cross_corners = grid.corner_moves(cross_sends)
    expand_chip = grid.chip_sum(expand_group, expand_sides)
    expand_grad = lax.psum_scatter(expand_chip, "seq", scatter_dimension=0)
    inputs_part = context_back(grad_context_self, one_all, 1)
    inputs_grad = lax.psum_scatter(inputs_part, "seq", scatter_dimension=0, tiled=True)
    self_query_bias_grad = jnp.sum(grad_query_self, axis=0)
    self_value_bias_grad = jnp.sum(grad_context_self[:, width:].astype(f32), axis=0)
    cross_value_bias_grad = jnp.sum(grad_context_cross[:, width:].astype(f32), axis=0)
    vector_grads = jnp.concatenate(
        [
            jnp.stack(
                (self_query_bias_grad, self_value_bias_grad)
                + tuple(lines[:4])
                + (cross_value_bias_grad,)
                + tuple(lines[4:10])
            ).T,
            lines[10].reshape(width, -1),
        ],
        axis=1,
    )
    vector_grads = jnp.pad(vector_grads, ((0, 0), (0, lane - spread)))
    vector_grads = vector_grads.reshape(devices, rows, lane)
    vector_sent, vector_kept = grid.vector_halves(vector_grads)
    cross_corners, vector_sent, vector_kept, expand_chip, inputs_part = together(
        cross_corners, vector_sent, vector_kept, expand_chip, inputs_part
    )

    cross_sends = grid.side_sends(cross_group, cross_corners)
    cross_sends, query_sent, context_sent, vector_sent = together(
        cross_sends, query_sent, context_sent, vector_sent
    )
    cross_sides = grid.side_moves(cross_sends)
    query_got, context_got, vector_got = grid.swap((query_sent, context_sent, vector_sent))
    cross_sides, query_got, context_got, vector_got, memory_grad = together(
        cross_sides, query_got, context_got, vector_got, memory_grad
    )

    self_group = [
        [query_kept, query_got],
        [context_kept, context_got],
        [vector_kept, vector_got],
    ]
    self_sends = grid.corner_sends(self_group)
    cross_chip = grid.chip_sum(cross_group, cross_sides)
    self_sends, cross_chip, query_self_low = together(self_sends, cross_chip, query_self_low)
    self_corners = grid.corner_moves(self_sends)
    cross_grad = lax.psum_scatter(cross_chip, "seq", scatter_dimension=0)
    inputs_base = residual_scale * grad_first + times_transposed(query_self_low, self_query)
    inputs_base, self_corners, inputs_grad = together(inputs_base, self_corners, inputs_grad)

    self_sends = grid.side_sends(self_group, self_corners)
    self_sides = grid.side_moves(self_sends)
    reduce_grad = reduce_grad.astype(f32)
    expand_grad = expand_grad.astype(f32)
    expand_grad, cross_out_grad = expand_grad[:, :-width], expand_grad[:, -width:]
    memory_grad = memory_grad.astype(f32)
    inputs_grad = inputs_base + inputs_grad.astype(f32)
    self_sides, reduce_grad, expand_grad, cross_out_grad, memory_grad, inputs_grad = together(
        self_sides, reduce_grad, expand_grad, cross_out_grad, memory_grad, inputs_grad
    )

    self_chip = grid.chip_sum(self_group, self_sides)
    self_sends = grid.depth_sends(self_chip)
    self_depths = grid.depth_moves(self_sends)
    self_depths, cross_grad = together(self_depths, cross_grad)
    cross_grad = cross_grad.astype(f32)
    cross_query_grad = cross_grad[:, :width]
    cross_context_grad = cross_grad[:, width : 3 * width]
    self_out_grad = cross_grad[:, 3 * width :]
    self_grad = grid.share(self_chip, self_depths)
    self_inward_grad, share = self_grad[:, : 3 * width], self_grad[:, 3 * width :]
    (
        self_query_bias_grad,
        self_value_bias_grad,
        self_output_bias_grad,
        first_gain_grad,
        first_shift_grad,
        cross_query_bias_grad,
        cross_value_bias_grad,
        cross_output_bias_grad,
        second_gain_grad,
        second_shift_grad,
        reduce_bias_grad,
        third_gain_grad,
        third_shift_grad,
    ) = [line for line in share[:, : len(vectors)].T]
    expand_bias_grad = share[:, len(vectors) : spread].reshape(-1)

    return (
        result.reshape(pair_count, group_len, width),
        inputs_grad.reshape(pair_count, group_len, width),
        memory_grad.reshape(pair_count, group_len, width),
        self_inward_grad,
        self_out_grad,
        self_query_bias_grad,
        self_value_bias_grad,
        self_output_bias_grad,
        first_gain_grad,
        first_shift_grad,
        cross_query_grad,
        cross_context_grad,
        cross_out_grad,
        cross_query_bias_grad,
        cross_value_bias_grad,
        cross_output_bias_grad,
        second_gain_grad,
        second_shift_grad,
        expand_grad,
        expand_bias_grad,
        reduce_grad,
        reduce_bias_grad,
        third_gain_grad,
        third_shift_grad,
    )


def solution(mesh):
    rows = P(("dp", "seq"), None)
    vector = P(("dp", "seq"))
    tokens = P("dp", "seq", None)
    in_specs = (
        (tokens, tokens, P("dp", None), P("dp"), tokens)
        + (rows, rows)
        + (vector,) * 5
        + (rows,) * 3
        + (vector,) * 5
        + (rows, vector, rows)
        + (vector,) * 3
    )
    out_specs = (
        (tokens,) * 3
        + (rows, rows)
        + (vector,) * 5
        + (rows,) * 3
        + (vector,) * 5
        + (rows, vector, rows)
        + (vector,) * 3
    )
    return jax.shard_map(
        functools.partial(local, Grid(mesh)),
        mesh=mesh,
        in_specs=in_specs,
        out_specs=out_specs,
        check_vma=False,
    )
```

```python
import functools

import jax
import jax.numpy as jnp
from jax import lax
from jax.experimental import pallas as pl
from jax.experimental.pallas import tpu as pltpu
from jax.sharding import PartitionSpec as P

HEADS = 16
HEAD_DIM = 64
PAIR = 2 * HEAD_DIM

residual_scale = 4.16
epsilon = 1e-05
score_scale = 0.125
negative_fill = -1e30
bf16 = jnp.bfloat16
f32 = jnp.float32


def norm_layer(values, gain_vector, shift_vector):
    middle = jnp.mean(values, axis=-1, keepdims=True)
    centred = values - middle
    spread = jnp.mean(centred * centred, axis=-1, keepdims=True)
    return centred * lax.rsqrt(spread + epsilon) * gain_vector + shift_vector


def gelu_tanh(values):
    return (
        0.5
        * values
        * (1.0 + jnp.tanh(0.7978845608028654 * (values + 0.044715 * values * values * values)))
    )


def dense(left_side, right_side):
    return jnp.dot(left_side, right_side, preferred_element_type=f32)


def times_transposed(left_side, right_side):
    return lax.dot_general(
        left_side, right_side, (((1,), (1,)), ((), ())), preferred_element_type=f32
    )


def transposed_times(left_side, right_side):
    return lax.dot_general(
        left_side, right_side, (((0,), (0,)), ((), ())), preferred_element_type=f32
    )


def lane_head(shape, head):
    lane = lax.broadcasted_iota(jnp.int32, shape, 1)
    return (lane < HEAD_DIM) if head == 0 else (lane >= HEAD_DIM)


def masked_scores(scores, place_ref, causal, group_len):
    if not causal:
        return scores
    blocks = scores.shape[0] // group_len
    own = place_ref[0, blocks]
    diff = lax.broadcasted_iota(jnp.int32, (group_len, group_len), 0) - lax.broadcasted_iota(
        jnp.int32, (group_len, group_len), 1
    )
    parts = []
    for block in range(blocks):
        reach = (own - place_ref[0, block]) * group_len
        part = scores[block * group_len : (block + 1) * group_len]
        parts.append(jnp.where(diff <= reach, part, negative_fill))
    return jnp.concatenate(parts, axis=0)


def attend_forward_kernel(causal, place_ref, q_ref, k_ref, v_ref, o_ref, total_ref):
    group_len = q_ref.shape[0]
    heads = [(part, head) for part in range(q_ref.shape[1] // PAIR) for head in range(2)]

    def lanes(part):
        return slice(part * PAIR, (part + 1) * PAIR)

    def scores_of(part, head):
        scaled = q_ref[:, lanes(part)] * jnp.asarray(score_scale, bf16)
        own = jnp.where(lane_head(scaled.shape, head), scaled, jnp.zeros_like(scaled))
        return times_transposed(k_ref[:, lanes(part)], own)

    ahead = [scores_of(*at) for at in heads[:2]]
    outs = []
    for i, (part, head) in enumerate(heads):
        if i + 2 < len(heads):
            ahead.append(scores_of(*heads[i + 2]))
        here = masked_scores(ahead[i], place_ref, causal, group_len)
        top = jnp.max(here, axis=0, keepdims=True)
        weights = jnp.exp(here - top)
        total = jnp.sum(weights, axis=0, keepdims=True)
        blended = transposed_times(v_ref[:, lanes(part)], weights.astype(bf16)) / total
        outs.append(blended)
        total_ref[part, head : head + 1, :] = top + jnp.log(total)
        if head == 1:
            row = lax.broadcasted_iota(jnp.int32, blended.shape, 0)
            o_ref[:, lanes(part)] = (
                jnp.where(row < HEAD_DIM, outs[-2], outs[-1]).T.astype(bf16)
            )


def attend_backward_kernel(
    causal, place_ref, q_ref, k_ref, v_ref, total_ref, g_ref, dq_ref, dkv_ref, held, sems
):
    group_len = q_ref.shape[0]
    both = q_ref.shape[1]
    heads = [(part, head) for part in range(both // PAIR) for head in range(2)]
    step, steps = pl.program_id(0), pl.num_programs(0)
    slot = lax.rem(step, 2)
    width = dkv_ref.shape[1] // 2

    def moves(at, slot):
        return [
            pltpu.make_async_copy(
                held.at[slot, part],
                dkv_ref.at[:, pl.ds(pl.multiple_of(part * width + at * both, both), both)],
                sems.at[slot, part],
            )
            for part in range(2)
        ]

    @pl.when(step >= 2)
    def _():
        for move in moves(step - 2, slot):
            move.wait()

    def lanes(part):
        return slice(part * PAIR, (part + 1) * PAIR)

    def start_of(part, head):
        scaled = q_ref[:, lanes(part)] * jnp.asarray(score_scale, bf16)
        grads = g_ref[:, lanes(part)]
        mine = lane_head(scaled.shape, head)
        own = jnp.where(mine, scaled, jnp.zeros_like(scaled))
        grad = jnp.where(mine, grads, jnp.zeros_like(grads))
        return (
            own,
            grad,
            times_transposed(k_ref[:, lanes(part)], own),
            times_transposed(v_ref[:, lanes(part)], grad),
        )

    ahead = [start_of(*at) for at in heads[:2]]
    dqs, dks, dvs = [], [], []
    for i, (part, head) in enumerate(heads):
        if i + 2 < len(heads):
            ahead.append(start_of(*heads[i + 2]))
        own, grad, scores, dprob = ahead[i]
        here = masked_scores(scores, place_ref, causal, group_len)
        weights = jnp.exp(here - total_ref[part, head : head + 1, :])
        dvs.append(dense(weights.astype(bf16), grad))
        delta = jnp.sum(dprob * weights, axis=0, keepdims=True)
        dscore = (weights * (dprob - delta)).astype(bf16)
        dks.append(dense(dscore, own))
        dqs.append(transposed_times(k_ref[:, lanes(part)], dscore))
        if head == 1:
            row = lax.broadcasted_iota(jnp.int32, dqs[0].shape, 0)
            dq_ref[:, lanes(part)] = (
                jnp.where(row < HEAD_DIM, dqs[-2], dqs[-1]).T * score_scale
            )
            held[slot, 0, :, lanes(part)] = (dks[-2] + dks[-1]).astype(bf16)
            held[slot, 1, :, lanes(part)] = (dvs[-2] + dvs[-1]).astype(bf16)
    for move in moves(step, slot):
        move.start()

    @pl.when(step == steps - 1)
    def _():
        for move in moves(step - 1, 1 - slot):
            move.wait()
        for move in moves(step, slot):
            move.wait()


def attention_specs(group_len, length, pairs):
    row = pl.BlockSpec((group_len, 2 * PAIR), lambda h: (0, h))
    keys = pl.BlockSpec((length, 2 * PAIR), lambda h: (0, h))
    values = pl.BlockSpec((length, 2 * PAIR), lambda h: (0, h + pairs // 2))
    total = pl.BlockSpec((2, 2, group_len), lambda h: (h, 0, 0))
    place = pl.BlockSpec(memory_space=pltpu.SMEM)
    return place, row, keys, values, total


FREE = pl.CostEstimate(flops=1, bytes_accessed=1, transcendentals=0)
ROOM = pltpu.CompilerParams(vmem_limit_bytes=24 * 1024 * 1024)
WIDE_ROOM = pltpu.CompilerParams(vmem_limit_bytes=48 * 1024 * 1024)


def attend_forward(query_rows, context_rows, places, causal):
    group_len, width = query_rows.shape
    length = context_rows.shape[0]
    pairs = width // PAIR
    place, row, keys, values, total = attention_specs(group_len, length, pairs)
    return pl.pallas_call(
        functools.partial(attend_forward_kernel, causal),
        grid=(pairs // 2,),
        in_specs=[place, row, keys, values],
        out_specs=[row, total],
        out_shape=[
            jax.ShapeDtypeStruct((group_len, width), bf16),
            jax.ShapeDtypeStruct((pairs, 2, group_len), f32),
        ],
        compiler_params=WIDE_ROOM,
        cost_estimate=FREE,
    )(places, query_rows, context_rows, context_rows)


def attend_backward(query_rows, context_rows, places, totals, grads, causal):
    group_len, width = query_rows.shape
    length = context_rows.shape[0]
    pairs = width // PAIR
    place, row, keys, values, total = attention_specs(group_len, length, pairs)
    return pl.pallas_call(
        functools.partial(attend_backward_kernel, causal),
        grid=(pairs // 2,),
        in_specs=[place, row, keys, values, total, row],
        out_specs=[row, pl.BlockSpec(memory_space=pl.ANY)],
        out_shape=[
            jax.ShapeDtypeStruct((group_len, width), f32),
            jax.ShapeDtypeStruct((length, 2 * width), bf16),
        ],
        scratch_shapes=[
            pltpu.VMEM((2, 2, length, 2 * PAIR), bf16),
            pltpu.SemaphoreType.DMA((2, 2)),
        ],
        compiler_params=WIDE_ROOM,
        cost_estimate=FREE,
    )(places, query_rows, context_rows, context_rows, totals, grads)


def context_back_kernel(g_ref, k_ref, v_ref, out_ref):
    width = k_ref.shape[1]
    out_ref[...] = (
        times_transposed(g_ref[:, :width], k_ref[...])
        + times_transposed(g_ref[:, width:], v_ref[...])
    ).astype(bf16)


def context_back(grads, weights, start):
    length, both = grads.shape
    width = both // 2
    each = width // 4
    return pl.pallas_call(
        context_back_kernel,
        grid=(4,),
        in_specs=[
            pl.BlockSpec((length, both), lambda j: (0, 0)),
            pl.BlockSpec((each, width), lambda j: (j, start)),
            pl.BlockSpec((each, width), lambda j: (j, start + 1)),
        ],
        out_specs=pl.BlockSpec((length, each), lambda j: (0, j)),
        out_shape=jax.ShapeDtypeStruct((length, width), bf16),
        compiler_params=WIDE_ROOM,
        cost_estimate=FREE,
    )(grads, weights, weights)


def context_halves_kernel(where_ref, other_ref, own_ref, g_ref, sent_ref, kept_ref):
    rows = sent_ref.shape[0]
    grads = g_ref[...]
    sent_ref[...] = dense(other_ref[...].reshape(rows, -1), grads).astype(bf16)
    kept_ref[...] = dense(own_ref[...].reshape(rows, -1), grads).astype(bf16)


def turn_kernel(x_ref, out_ref):
    out_ref[...] = x_ref[...].T


def turned(values):
    rows, columns = values.shape
    return pl.pallas_call(
        turn_kernel,
        grid=(columns // PAIR,),
        in_specs=[pl.BlockSpec((rows, PAIR), lambda j: (0, j))],
        out_specs=pl.BlockSpec((PAIR, rows), lambda j: (j, 0)),
        out_shape=jax.ShapeDtypeStruct((columns, rows), values.dtype),
        compiler_params=ROOM,
        cost_estimate=FREE,
    )(values)


def feed_forward_kernel(x_ref, e_ref, r_ref, b_ref, expanded_ref, hidden_ref, out_ref):
    step = pl.program_id(0)
    wide = b_ref.shape[-1]
    expanded = dense(x_ref[...], e_ref[...].reshape(-1, wide)) + b_ref[...]
    expanded_ref[0] = expanded
    hidden = gelu_tanh(expanded).astype(bf16)
    hidden_ref[...] = hidden
    part = dense(hidden, r_ref[...].reshape(wide, -1))

    @pl.when(step == 0)
    def _():
        out_ref[...] = part

    @pl.when(step > 0)
    def _():
        out_ref[...] += part


def feed_backward_kernel(g_ref, e_ref, r_ref, expanded_ref, low_ref, bias_ref, out_ref):
    step = pl.program_id(0)
    wide = low_ref.shape[-1]
    grad_hidden = times_transposed(g_ref[...], r_ref[...].reshape(wide, -1))
    u = expanded_ref[0]
    square = u * u
    bent = jnp.tanh(0.7978845608028654 * (u + 0.044715 * square * u))
    slope = 0.5 * (1.0 + bent) + 0.5 * u * (1.0 - bent * bent) * (
        0.7978845608028654 * (1.0 + 3.0 * 0.044715 * square)
    )
    grad = grad_hidden * slope
    bias_ref[...] = jnp.sum(grad, axis=0, keepdims=True)
    low = grad.astype(bf16)
    low_ref[...] = low
    part = times_transposed(low, e_ref[...].reshape(-1, wide))

    @pl.when(step == 0)
    def _():
        out_ref[...] = part

    @pl.when(step > 0)
    def _():
        out_ref[...] += part


def feed_specs(count, width, each):
    return (
        pl.BlockSpec((count, width), lambda j: (0, 0)),
        pl.BlockSpec((1, width, each), lambda j: (j, 0, 0)),
        pl.BlockSpec((each, width), lambda j: (j, 0)),
        pl.BlockSpec((count, each), lambda j: (0, j)),
        pl.BlockSpec((1, each), lambda j: (0, j)),
        pl.BlockSpec((1, count, each), lambda j: (j, 0, 0)),
    )


def feed_forward(rows, expand_all, reduce_all, bias):
    count, width = rows.shape
    wide = reduce_all.shape[0]
    each = expand_all.shape[2]
    whole, first, second, part, line, block = feed_specs(count, width, each)
    return pl.pallas_call(
        feed_forward_kernel,
        grid=(wide // each,),
        in_specs=[whole, first, second, line],
        out_specs=[block, part, whole],
        out_shape=[
            jax.ShapeDtypeStruct((wide // each, count, each), f32),
            jax.ShapeDtypeStruct((count, wide), bf16),
            jax.ShapeDtypeStruct((count, width), f32),
        ],
        compiler_params=WIDE_ROOM,
        cost_estimate=FREE,
    )(rows, expand_all, reduce_all, bias.reshape(1, -1))


def feed_backward(grads, expand_all, reduce_all, expanded):
    count, width = grads.shape
    wide = reduce_all.shape[0]
    each = expand_all.shape[2]
    whole, first, second, part, line, block = feed_specs(count, width, each)
    return pl.pallas_call(
        feed_backward_kernel,
        grid=(wide // each,),
        in_specs=[whole, first, second, block],
        out_specs=[part, line, whole],
        out_shape=[
            jax.ShapeDtypeStruct((count, wide), bf16),
            jax.ShapeDtypeStruct((1, wide), f32),
            jax.ShapeDtypeStruct((count, width), f32),
        ],
        compiler_params=WIDE_ROOM,
        cost_estimate=FREE,
    )(grads, expand_all, reduce_all, expanded)


class Grid:
    def __init__(self, mesh):
        self.dp = mesh.shape["dp"]
        depth = mesh.shape["seq"]
        core = 2 if self.dp % 2 == 0 else 1
        chips = self.dp // core
        outer = 1
        while outer * outer < chips:
            outer *= 2
        inner = chips // outer
        self.sizes = {"outer": outer, "inner": inner, "core": core, "depth": depth}
        self.strides = {"outer": inner * core, "inner": core, "core": 1}

    def index(self, dim):
        if dim == "depth":
            return lax.axis_index("seq")
        return (lax.axis_index("dp") // self.strides[dim]) % self.sizes[dim]

    def shift(self, value, dim, step):
        size = self.sizes[dim]
        if dim == "depth":
            return lax.ppermute(value, "seq", [(i, (i + step) % size) for i in range(size)])
        stride = self.strides[dim]
        pairs = []
        for device in range(self.dp):
            at = (device // stride) % size
            pairs.append((device, device + ((at + step) % size - at) * stride))
        return lax.ppermute(value, "dp", pairs)

    def steps(self, dim):
        return range(1, self.sizes[dim])

    def from_depth(self, shard):
        return [self.shift(shard, "depth", step) for step in self.steps("depth")]

    def depth_block(self, shard, pieces):
        size, me = self.sizes["depth"], self.index("depth")
        return jnp.stack(
            [lax.select_n((me - at) % size, shard, *pieces) for at in range(size)]
        )

    def from_sides(self, block):
        return (
            [self.shift(block, "inner", step) for step in self.steps("inner")],
            [self.shift(block, "outer", step) for step in self.steps("outer")],
        )

    def from_corners(self, sides):
        along_inner, along_outer = sides
        half = along_inner[0].shape[0] // 2
        top = jnp.stack([block[:half] for block in along_inner])
        bottom = jnp.stack([block[half:] for block in along_outer])
        return (
            [self.shift(top, "outer", step) for step in self.steps("outer")],
            [self.shift(bottom, "inner", step) for step in self.steps("inner")],
        )

    def swap(self, pieces):
        return jax.tree.map(lambda piece: self.shift(piece, "core", 1), pieces)

    def whole(self, own, others, blocks=1):
        outer, inner, core = (self.sizes[n] for n in ("outer", "inner", "core"))
        each, total = own[0].shape[-2], own[0].shape[-1]
        columns = total // blocks
        height = self.sizes["depth"] * each
        half = height // 2
        pieces, places = [], []

        def add(piece, back_a, back_b, other, start):
            pieces.append(piece.reshape(-1, total))
            places.append((back_a, back_b, other, start))

        for other, (block, (along_inner, along_outer), (top, bottom)) in enumerate([own, others]):
            add(block, 0, 0, other, 0)
            for j, piece in enumerate(along_inner):
                add(piece, 0, j + 1, other, 0)
            for i, piece in enumerate(along_outer):
                add(piece, i + 1, 0, other, 0)
            for i in range(outer - 1):
                for j in range(inner - 1):
                    add(top[i][j], i + 1, j + 1, other, 0)
                    add(bottom[j][i], i + 1, j + 1, other, half)

        def kernel(*refs):
            out, sems = refs[len(pieces)], refs[len(pieces) + 1]
            device = lax.axis_index("dp")
            a = device // self.strides["outer"]
            b = lax.rem(device // self.strides["inner"], inner)
            c = lax.rem(device, core)
            copies = []
            for at, (ref, (back_a, back_b, other, start)) in enumerate(zip(refs, places)):
                to_a = lax.rem(a + (outer - back_a), outer)
                to_b = lax.rem(b + (inner - back_b), inner)
                to_c = lax.rem(c + other, core)
                index = (to_a * inner + to_b) * core + to_c
                for j in range(blocks):
                    copies.append(
                        pltpu.make_async_copy(
                            ref.at[:, pl.ds(j * columns, columns)],
                            out.at[j, index, pl.ds(start, ref.shape[0])],
                            sems.at[at, j],
                        )
                    )
            for copy in copies:
                copy.start()
            for copy in copies:
                copy.wait()

        anywhere = pl.BlockSpec(memory_space=pltpu.HBM)
        matrix = pl.pallas_call(
            kernel,
            in_specs=[anywhere] * len(pieces),
            out_specs=pl.BlockSpec(memory_space=pltpu.VMEM),
            out_shape=jax.ShapeDtypeStruct((blocks, outer * inner * core, height, columns), bf16),
            scratch_shapes=[pltpu.SemaphoreType.DMA((len(pieces), blocks))],
            compiler_params=WIDE_ROOM,
            cost_estimate=FREE,
        )(*pieces)
        matrix = matrix.reshape(blocks, -1, columns)
        return matrix if blocks > 1 else matrix[0]

    def picked(self, left_side):
        core = self.sizes["core"]
        count = self.sizes["outer"] * self.sizes["inner"]
        block = left_side.shape[1] // (count * core)
        me = self.index("core")
        even, odd = [
            [left_side[:, (core * j + i) * block : (core * j + i + 1) * block] for j in range(count)]
            for i in range(core)
        ]
        return tuple(
            jnp.concatenate(
                [jnp.where(me == 0, *((e, o) if own else (o, e))) for e, o in zip(even, odd)], axis=1
            )
            for own in (False, True)
        )

    def halves(self, picked, right_side):
        outer, inner, depth = self.sizes["outer"], self.sizes["inner"], self.sizes["depth"]
        each = picked[0].shape[1] // (outer * inner * depth)
        shape = (outer, inner, depth, each, right_side.shape[1])
        return tuple(
            transposed_times(chosen, right_side).astype(bf16).reshape(shape) for chosen in picked
        )

    def context_halves(self, turned, grads):
        outer, inner, core, depth = (self.sizes[n] for n in ("outer", "inner", "core", "depth"))
        height, rows = turned.shape
        block = height // (outer * inner * core)
        columns = grads.shape[1]
        each = columns // 4
        me = self.index("core")
        piece = (outer * inner, 1, block, rows)
        sent, kept = pl.pallas_call(
            context_halves_kernel,
            grid_spec=pltpu.PrefetchScalarGridSpec(
                num_scalar_prefetch=1,
                grid=(4,),
                in_specs=[
                    pl.BlockSpec(piece, lambda j, where: (0, where[0], 0, 0)),
                    pl.BlockSpec(piece, lambda j, where: (0, where[1], 0, 0)),
                    pl.BlockSpec((rows, each), lambda j, where: (0, j)),
                ],
                out_specs=[pl.BlockSpec((height // core, each), lambda j, where: (0, j))] * 2,
            ),
            out_shape=[jax.ShapeDtypeStruct((height // core, columns), bf16)] * 2,
            compiler_params=WIDE_ROOM,
            cost_estimate=FREE,
        )(
            jnp.stack([1 - me, me]).astype(jnp.int32),
            *([turned.reshape(outer * inner, core, block, rows)] * 2),
            grads,
        )
        shape = (outer, inner, depth, block // depth, columns)
        return sent.reshape(shape), kept.reshape(shape)

    def vector_halves(self, packed):
        core = self.sizes["core"]
        outer, inner, depth = self.sizes["outer"], self.sizes["inner"], self.sizes["depth"]
        split = packed.reshape((outer, inner, core, depth) + packed.shape[1:])
        me = self.index("core")
        even, odd = split[:, :, 0], split[:, :, 1]
        return jnp.where(me == 0, odd, even).astype(bf16), jnp.where(me == 0, even, odd)

    def sums(self, terms):
        return sum(term.astype(f32) for term in terms)

    def corner_sends(self, group):
        if self.square:
            top, bottom = self.block_sums(group, "corner", [])
            return [top], [bottom]
        outer, inner = self.sizes["outer"], self.sizes["inner"]
        a, b = self.index("outer"), self.index("inner")
        half = group[0][0].shape[2] // 2

        def block(terms, at_a, at_b, low, high):
            cut = [
                lax.dynamic_slice(
                    term,
                    (at_a % outer, at_b % inner, low, 0, 0),
                    (1, 1, high - low) + term.shape[3:],
                )
                for term in terms
            ]
            return self.sums(cut)[0, 0].astype(bf16)

        def joined(blocks):
            return jnp.concatenate(blocks, axis=-1) if len(blocks) > 1 else blocks[0]

        top = [
            jnp.stack(
                [
                    joined([block(terms, a + i, b + j, 0, half) for terms in group])
                    for j in self.steps("inner")
                ]
            )
            for i in self.steps("outer")
        ]
        bottom = [
            jnp.stack(
                [
                    joined([block(terms, a + i, b + j, half, 2 * half) for terms in group])
                    for i in self.steps("outer")
                ]
            )
            for j in self.steps("inner")
        ]
        return top, bottom

    def corner_moves(self, sends):
        top, bottom = sends
        return (
            [self.shift(send, "outer", step) for send, step in zip(top, self.steps("outer"))],
            [self.shift(send, "inner", step) for send, step in zip(bottom, self.steps("inner"))],
        )

    def side_sends(self, group, corners):
        top, bottom = corners
        if self.square:
            to_inner, to_outer = self.block_sums(group, "sides", [top[0], bottom[0]])
            return [to_inner], [to_outer]
        outer, inner = self.sizes["outer"], self.sizes["inner"]
        a, b = self.index("outer"), self.index("inner")
        half = group[0][0].shape[2] // 2

        def block(at_a, at_b, low, high, extra):
            sums, start = [], 0
            for terms in group:
                columns = terms[0].shape[-1]
                cut = [
                    lax.dynamic_slice(
                        term,
                        (at_a % outer, at_b % inner, low, 0, 0),
                        (1, 1, high - low) + term.shape[3:],
                    )[0, 0]
                    for term in terms
                ]
                cut += [piece[..., start : start + columns] for piece in extra]
                sums.append(self.sums(cut).astype(bf16))
                start += columns
            return jnp.concatenate(sums, axis=-1) if len(sums) > 1 else sums[0]

        to_inner = [
            jnp.concatenate(
                [
                    block(a, b + j, 0, half, [piece[j - 1] for piece in top]),
                    block(a, b + j, half, 2 * half, []),
                ]
            )
            for j in self.steps("inner")
        ]
        to_outer = [
            jnp.concatenate(
                [
                    block(a + i, b, 0, half, []),
                    block(a + i, b, half, 2 * half, [piece[i - 1] for piece in bottom]),
                ]
            )
            for i in self.steps("outer")
        ]
        return to_inner, to_outer

    def side_moves(self, sends):
        to_inner, to_outer = sends
        return [self.shift(send, "inner", step) for send, step in zip(to_inner, self.steps("inner"))] + [
            self.shift(send, "outer", step) for send, step in zip(to_outer, self.steps("outer"))
        ]

    def chip_terms(self, group, sides):
        a, b = self.index("outer"), self.index("inner")
        out, start = [], 0
        for terms in group:
            columns = terms[0].shape[-1]
            own = [
                lax.dynamic_slice(term, (a, b, 0, 0, 0), (1, 1) + term.shape[2:])[0, 0]
                for term in terms
            ]
            out.append(own + [piece[..., start : start + columns] for piece in sides])
            start += columns
        return out

    def chip_sum(self, group, sides):
        if self.square:
            total = sum(terms[0].shape[-1] for terms in group)
            return self.block_sums(group, "own", sides).reshape(
                self.sizes["depth"], -1, total
            )
        sums = [self.sums(terms).astype(bf16) for terms in self.chip_terms(group, sides)]
        return jnp.concatenate(sums, axis=-1) if len(sums) > 1 else sums[0]

    @property
    def square(self):
        return self.sizes["outer"] == 2 and self.sizes["inner"] == 2

    def block_sums(self, group, what, received):
        a, b = self.index("outer"), self.index("inner")
        place = {
            "corner": [(1 - a) * 2 + 1 - b],
            "sides": [a * 2 + 1 - b, (1 - a) * 2 + b],
            "own": [a * 2 + b],
        }[what]
        terms = [
            [term.reshape(4, -1, term.shape[-1]) for term in matrix] for matrix in group
        ]
        rows = terms[0][0].shape[1]
        half = rows // 2
        widths = [matrix[0].shape[-1] for matrix in terms]
        counts = [len(matrix) for matrix in terms]
        flat = [term for matrix in terms for term in matrix]
        received = [piece.reshape(-1, sum(widths)) for piece in received]

        def kernel(where_ref, *refs):
            terms_in, rest = refs[: len(flat)], refs[len(flat) :]
            got_in, rest = rest[: len(received)], rest[len(received) :]
            outs, rest = rest[: len(heights)], rest[len(heights) :]
            held, got, sems = rest[: len(flat)], rest[len(flat) : -1], rest[-1]
            copies = [
                pltpu.make_async_copy(
                    ref.at[where_ref[at]], held[i].at[at], sems.at[at * len(flat) + i]
                )
                for at in range(len(place))
                for i, ref in enumerate(terms_in)
            ]
            first_got = len(copies)
            copies += [
                pltpu.make_async_copy(ref, got[i], sems.at[first_got + i])
                for i, ref in enumerate(got_in)
            ]
            for copy in copies[first_got:] + copies[:first_got]:
                copy.start()
            for copy in copies[first_got:]:
                copy.wait()
            for at in range(len(place)):
                first, start = 0, 0
                for count, columns in zip(counts, widths):
                    for i in range(first, first + count):
                        copies[at * len(flat) + i].wait()
                    for low in range(0, columns, 512):
                        high = min(low + 512, columns)
                        here = slice(start + low, start + high)
                        value = sum(
                            ref[at, :, low:high].astype(f32) for ref in held[first : first + count]
                        )
                        if what == "corner":
                            outs[0][:, here] = value[:half].astype(bf16)
                            outs[1][:, here] = value[half:].astype(bf16)
                        elif what == "sides":
                            top, bottom = value[:half], value[half:]
                            if at == 0:
                                top = top + got[0][:, here].astype(f32)
                            else:
                                bottom = bottom + got[1][:, here].astype(f32)
                            outs[at][:half, here] = top.astype(bf16)
                            outs[at][half:, here] = bottom.astype(bf16)
                        else:
                            value = value + sum(ref[:, here].astype(f32) for ref in got)
                            outs[0][:, here] = value.astype(bf16)
                    first += count
                    start += columns

        heights = {"corner": [half, half], "sides": [rows, rows], "own": [rows]}[what]
        in_hbm = pl.BlockSpec(memory_space=pltpu.HBM)
        out = pl.pallas_call(
            kernel,
            in_specs=[pl.BlockSpec(memory_space=pltpu.SMEM)]
            + [in_hbm] * (len(flat) + len(received)),
            out_specs=[pl.BlockSpec(memory_space=pltpu.VMEM)] * len(heights),
            out_shape=[jax.ShapeDtypeStruct((height, sum(widths)), bf16) for height in heights],
            scratch_shapes=[
                pltpu.VMEM((len(place), rows, term.shape[-1]), term.dtype) for term in flat
            ]
            + [pltpu.VMEM(piece.shape, bf16) for piece in received]
            + [pltpu.SemaphoreType.DMA((len(place) * len(flat) + len(received),))],
            compiler_params=WIDE_ROOM,
            cost_estimate=FREE,
        )(jnp.stack(place).astype(jnp.int32), *flat, *received)
        return out[0] if what == "own" else out

    def depth_sends(self, chip):
        size, me = self.sizes["depth"], self.index("depth")
        return [
            lax.dynamic_index_in_dim(chip, (me + step) % size, 0, keepdims=False)
            for step in self.steps("depth")
        ]

    def depth_moves(self, sends):
        return [self.shift(send, "depth", step) for send, step in zip(sends, self.steps("depth"))]

    def share(self, chip, received):
        own = lax.dynamic_index_in_dim(chip, self.index("depth"), 0, keepdims=False)
        return self.sums([own] + received)


def together(*values):
    return lax.optimization_barrier(values)


def local(grid, *args):
    (
        inputs,
        memory,
        group_place,
        pair_mask,
        cotangent,
        self_inward,
        self_outward,
        self_query_bias,
        self_value_bias,
        self_output_bias,
        first_gain,
        first_shift,
        cross_query,
        cross_memory,
        cross_outward,
        cross_query_bias,
        cross_value_bias,
        cross_output_bias,
        second_gain,
        second_shift,
        expand_weight,
        expand_bias,
        reduce_weight,
        reduce_bias,
        third_gain,
        third_shift,
    ) = args
    pair_count, group_len, width = inputs.shape
    rows_in = inputs.reshape(group_len, width)
    rows_low = rows_in.astype(bf16)
    memory_low = memory.reshape(group_len, width).astype(bf16)

    vectors = (
        self_query_bias,
        self_value_bias,
        self_output_bias,
        first_gain,
        first_shift,
        cross_query_bias,
        cross_value_bias,
        cross_output_bias,
        second_gain,
        second_shift,
        reduce_bias,
        third_gain,
        third_shift,
    )
    rows = self_inward.shape[0]
    devices = width // rows
    places = jnp.concatenate(
        [
            group_place.reshape(1, -1),
            lax.dynamic_slice_in_dim(group_place, lax.axis_index("seq"), 1, axis=1),
        ],
        axis=1,
    )

    lane = 128
    one = jnp.concatenate(
        [self_inward, jnp.pad(self_query_bias[:, None], ((0, 0), (0, lane - 1)))], axis=1
    )
    packed = jnp.concatenate(
        [jnp.stack(vectors).T, expand_bias.reshape(rows, -1)], axis=1
    )
    spread = packed.shape[1]
    packed = jnp.pad(packed, ((0, 0), (0, lane - spread)))
    two = jnp.concatenate(
        [self_outward, cross_query, cross_outward, cross_memory, packed], axis=1
    )

    one_depth = grid.from_depth(one)
    one_depth, two, rows_low_sent = together(one_depth, two, rows_low)

    one_block = grid.depth_block(one, one_depth)
    one_sides = grid.from_sides(one_block)
    two_depth = grid.from_depth(two)
    one_sides, two_depth, rows_low_sent = together(one_sides, two_depth, rows_low_sent)

    all_low = lax.all_gather(rows_low_sent, "seq", axis=0, tiled=True)
    one_corners = grid.from_corners(one_sides)
    two_block = grid.depth_block(two, two_depth)
    one_corners, two_block = together(one_corners, two_block)

    two_sides = grid.from_sides(two_block)
    one_block_other, one_sides_other, one_corners_other = grid.swap(
        (one_block, one_sides, one_corners)
    )
    one_all = grid.whole(
        (one_block, one_sides, one_corners),
        (one_block_other, one_sides_other, one_corners_other),
    )
    self_query, self_context = one_all[:, :width], one_all[:, width : 3 * width]
    self_query_bias = one_all[:, 3 * width].astype(f32)
    query_self = (dense(rows_low, self_query) + self_query_bias).astype(bf16)
    two_sides, query_self, all_low, expand_weight = together(
        two_sides, query_self, all_low, expand_weight
    )

    two_corners = grid.from_corners(two_sides)
    expand_depth = grid.from_depth(expand_weight)
    context_self = dense(all_low, self_context).astype(bf16)
    blended_self, total_self = attend_forward(query_self, context_self, places, True)
    blended_self, two_corners, expand_depth, reduce_weight = together(
        blended_self, two_corners, expand_depth, reduce_weight
    )

    expand_block = grid.depth_block(expand_weight, expand_depth)
    two_block_other, two_sides_other, two_corners_other = grid.swap(
        (two_block, two_sides, two_corners)
    )
    two_block_other, two_sides_other, two_corners_other, expand_block = together(
        two_block_other, two_sides_other, two_corners_other, expand_block
    )
    expand_sides = grid.from_sides(expand_block)
    reduce_depth = grid.from_depth(reduce_weight)
    two_all = grid.whole(
        (two_block, two_sides, two_corners),
        (two_block_other, two_sides_other, two_corners_other),
    )
    packed = two_all[:, 5 * width : 5 * width + spread].astype(f32)
    (
        self_query_bias,
        self_value_bias,
        self_output_bias,
        first_gain,
        first_shift,
        cross_query_bias,
        cross_value_bias,
        cross_output_bias,
        second_gain,
        second_shift,
        reduce_bias,
        third_gain,
        third_shift,
    ) = [line for line in packed[:, : len(vectors)].T]
    expand_bias = packed[:, len(vectors) :].reshape(-1)
    self_outward, cross_query, cross_outward = [
        two_all[:, i * width : (i + 1) * width] for i in range(3)
    ]
    cross_context = two_all[:, 3 * width : 5 * width]
    blended_self = (blended_self + self_value_bias).astype(bf16)
    pre_first = residual_scale * rows_in + dense(blended_self, self_outward) + self_output_bias
    after_self = norm_layer(pre_first, first_gain, first_shift)
    after_self_low = after_self.astype(bf16)
    query_cross = (dense(after_self_low, cross_query) + cross_query_bias).astype(bf16)
    query_cross, expand_sides, reduce_depth, memory_low = together(
        query_cross, expand_sides, reduce_depth, memory_low
    )

    all_memory = lax.all_gather(memory_low, "seq", axis=0, tiled=True)
    reduce_block = grid.depth_block(reduce_weight, reduce_depth)
    expand_corners = grid.from_corners(expand_sides)
    reduce_sides = grid.from_sides(reduce_block)
    (expand_corners,) = together(expand_corners)
    expand_block_other, expand_sides_other, expand_corners_other = grid.swap(
        (expand_block, expand_sides, expand_corners)
    )
    expand_all = grid.whole(
        (expand_block, expand_sides, expand_corners),
        (expand_block_other, expand_sides_other, expand_corners_other),
        expand_weight.shape[1] // width,
    )
    picks = [
        grid.picked(left) for left in (rows_low, blended_self, after_self_low)
    ] + [turned(all_low)]
    expand_all, reduce_sides, all_memory, picks = together(
        expand_all, reduce_sides, all_memory, picks
    )

    reduce_corners = grid.from_corners(reduce_sides)
    reduce_block_other = grid.swap(reduce_block)
    reduce_sides_other = grid.swap(reduce_sides)
    context_cross = dense(all_memory, cross_context).astype(bf16)
    blended_cross, total_cross = attend_forward(query_cross, context_cross, places, False)
    reduce_corners, blended_cross, reduce_block_other, reduce_sides_other = together(
        reduce_corners, blended_cross, reduce_block_other, reduce_sides_other
    )

    reduce_corners_other = grid.swap(reduce_corners)
    blended_cross = (blended_cross + cross_value_bias).astype(bf16)
    pre_second = (
        residual_scale * after_self + dense(blended_cross, cross_outward) + cross_output_bias
    )
    after_cross = norm_layer(pre_second, second_gain, second_shift)
    cross_low = after_cross.astype(bf16)
    reduce_all = grid.whole(
        (reduce_block, reduce_sides, reduce_corners),
        (reduce_block_other, reduce_sides_other, reduce_corners_other),
    )
    expanded, hidden, reduced = feed_forward(cross_low, expand_all, reduce_all, expand_bias)
    pre_third = residual_scale * after_cross + reduced + reduce_bias
    result = norm_layer(pre_third, third_gain, third_shift)

    grad_out = cotangent.reshape(group_len, width) * pair_mask.astype(f32)[0]
    norm_back = jax.vjp(norm_layer, pre_third, third_gain, third_shift)[1]
    grad_third, third_gain_grad, third_shift_grad = norm_back(grad_out)
    reduce_bias_grad = jnp.sum(grad_third, axis=0)
    low_third = grad_third.astype(bf16)
    expanded_low, expand_bias_grad, grad_cross = feed_backward(
        low_third, expand_all, reduce_all, expanded
    )
    hidden_other, hidden_own = grid.picked(hidden)
    (reduce_sent,) = grid.halves((hidden_other,), low_third)
    reduce_sent, expanded_low, grad_cross, low_third = together(
        reduce_sent, expanded_low, grad_cross, low_third
    )

    reduce_got = grid.swap(reduce_sent)
    expand_sent, expand_kept = grid.halves(grid.picked(cross_low), expanded_low)
    grad_cross = residual_scale * grad_third + grad_cross
    norm_back = jax.vjp(norm_layer, pre_second, second_gain, second_shift)[1]
    grad_second, second_gain_grad, second_shift_grad = norm_back(grad_cross)
    cross_output_bias_grad = jnp.sum(grad_second, axis=0)
    second_low = grad_second.astype(bf16)
    grad_blended = times_transposed(second_low, cross_outward).astype(bf16)
    out_sent, out_kept = grid.halves(grid.picked(blended_cross), second_low)
    (reduce_kept,) = grid.halves((hidden_own,), low_third)
    (
        grad_blended,
        reduce_got,
        reduce_kept,
        expand_sent,
        expand_kept,
        out_sent,
        out_kept,
    ) = together(
        grad_blended, reduce_got, reduce_kept, expand_sent, expand_kept, out_sent, out_kept
    )

    reduce_group = [[reduce_kept, reduce_got]]
    reduce_sends = grid.corner_sends(reduce_group)
    reduce_sends, grad_blended, expand_sent, out_sent = together(
        reduce_sends, grad_blended, expand_sent, out_sent
    )
    reduce_corners = grid.corner_moves(reduce_sends)
    expand_got, out_got = grid.swap((expand_sent, out_sent))
    grad_query_cross, grad_context_cross = attend_backward(
        query_cross, context_cross, places, total_cross, grad_blended, False
    )
    grad_query_cross, grad_context_cross, reduce_corners, expand_got, out_got = together(
        grad_query_cross, grad_context_cross, reduce_corners, expand_got, out_got
    )

    reduce_sends = grid.side_sends(reduce_group, reduce_corners)
    reduce_sends, grad_query_cross, grad_context_cross = together(
        reduce_sends, grad_query_cross, grad_context_cross
    )
    reduce_sides = grid.side_moves(reduce_sends)
    memory_part = context_back(grad_context_cross, two_all, 3)
    context_sent, context_kept = grid.context_halves(
        turned(all_memory), grad_context_cross
    )
    grad_query_cross, memory_part, reduce_sides, context_sent, context_kept = together(
        grad_query_cross, memory_part, reduce_sides, context_sent, context_kept
    )

    expand_group = [[expand_kept, expand_got], [out_kept, out_got]]
    expand_sends = grid.corner_sends(expand_group)
    reduce_chip = grid.chip_sum(reduce_group, reduce_sides)
    expand_sends, reduce_chip, grad_query_cross, memory_part = together(
        expand_sends, reduce_chip, grad_query_cross, memory_part
    )
    expand_corners = grid.corner_moves(expand_sends)
    joined = lax.psum_scatter(
        jnp.concatenate([reduce_chip, memory_part.reshape(-1, group_len, width)], axis=1),
        "seq",
        scatter_dimension=0,
    )
    cross_query_bias_grad = jnp.sum(grad_query_cross, axis=0)
    query_cross_low = grad_query_cross.astype(bf16)
    grad_self = residual_scale * grad_second + times_transposed(query_cross_low, cross_query)
    norm_back = jax.vjp(norm_layer, pre_first, first_gain, first_shift)[1]
    grad_first, first_gain_grad, first_shift_grad = norm_back(grad_self)
    self_output_bias_grad = jnp.sum(grad_first, axis=0)
    first_low = grad_first.astype(bf16)
    outward_sent, outward_kept = grid.halves(picks[1], first_low)
    grad_blended = times_transposed(first_low, self_outward).astype(bf16)
    query_sent, query_kept = grid.halves(picks[2], query_cross_low)
    grad_blended, expand_corners, outward_sent, outward_kept, query_sent, query_kept = together(
        grad_blended, expand_corners, outward_sent, outward_kept, query_sent, query_kept
    )

    expand_sends = grid.side_sends(expand_group, expand_corners)
    expand_sends, grad_blended, context_sent, query_sent, outward_sent = together(
        expand_sends, grad_blended, context_sent, query_sent, outward_sent
    )
    expand_sides = grid.side_moves(expand_sends)
    context_got, query_got, outward_got = grid.swap((context_sent, query_sent, outward_sent))
    cross_group = [
        [query_kept, query_got],
        [context_kept, context_got],
        [outward_kept, outward_got],
    ]
    grad_query_self, grad_context_self = attend_backward(
        query_self, context_self, places, total_self, grad_blended, True
    )
    inputs_part = context_back(grad_context_self, one_all, 1)
    context_sent, context_kept = grid.context_halves(picks[3], grad_context_self)
    query_self_low = grad_query_self.astype(bf16)
    query_sent, query_kept = grid.halves(picks[0], query_self_low)
    (
        cross_group,
        expand_sides,
        grad_query_self,
        grad_context_self,
        query_self_low,
        query_sent,
        context_sent,
        query_kept,
        context_kept,
        inputs_part,
    ) = together(
        cross_group,
        expand_sides,
        grad_query_self,
        grad_context_self,
        query_self_low,
        query_sent,
        context_sent,
        query_kept,
        context_kept,
        inputs_part,
    )

    inputs_grad = lax.psum_scatter(inputs_part, "seq", scatter_dimension=0, tiled=True)
    cross_sends = grid.corner_sends(cross_group)
    lines = (
        self_output_bias_grad,
        first_gain_grad,
        first_shift_grad,
        cross_query_bias_grad,
        cross_output_bias_grad,
        second_gain_grad,
        second_shift_grad,
        reduce_bias_grad,
        third_gain_grad,
        third_shift_grad,
        expand_bias_grad,
    )
    cross_sends, grad_query_self, grad_context_self, grad_context_cross, lines = together(
        cross_sends, grad_query_self, grad_context_self, grad_context_cross, lines
    )
    cross_corners = grid.corner_moves(cross_sends)
    expand_chip = grid.chip_sum(expand_group, expand_sides)
    expand_grad = lax.psum_scatter(expand_chip, "seq", scatter_dimension=0)
    self_query_bias_grad = jnp.sum(grad_query_self, axis=0)
    self_value_bias_grad = jnp.sum(grad_context_self[:, width:].astype(f32), axis=0)
    cross_value_bias_grad = jnp.sum(grad_context_cross[:, width:].astype(f32), axis=0)
    vector_grads = jnp.concatenate(
        [
            jnp.stack(
                (self_query_bias_grad, self_value_bias_grad)
                + tuple(lines[:4])
                + (cross_value_bias_grad,)
                + tuple(lines[4:10])
            ).T,
            lines[10].reshape(width, -1),
        ],
        axis=1,
    )
    vector_grads = jnp.pad(vector_grads, ((0, 0), (0, lane - spread)))
    vector_grads = vector_grads.reshape(devices, rows, lane)
    vector_sent, vector_kept = grid.vector_halves(vector_grads)
    cross_corners, vector_sent, vector_kept, expand_chip, joined = together(
        cross_corners, vector_sent, vector_kept, expand_chip, joined
    )
    reduce_grad, memory_grad = joined[:-group_len], joined[-group_len:]

    cross_sends = grid.side_sends(cross_group, cross_corners)
    cross_sends, query_sent, context_sent, vector_sent = together(
        cross_sends, query_sent, context_sent, vector_sent
    )
    cross_sides = grid.side_moves(cross_sends)
    query_got, context_got, vector_got = grid.swap((query_sent, context_sent, vector_sent))
    cross_sides, query_got, context_got, vector_got = together(
        cross_sides, query_got, context_got, vector_got
    )

    self_group = [
        [query_kept, query_got],
        [context_kept, context_got],
        [vector_kept, vector_got],
    ]
    self_sends = grid.corner_sends(self_group)
    cross_chip = grid.chip_sum(cross_group, cross_sides)
    self_sends, cross_chip, query_self_low = together(self_sends, cross_chip, query_self_low)
    self_corners = grid.corner_moves(self_sends)
    cross_grad = lax.psum_scatter(cross_chip, "seq", scatter_dimension=0)
    inputs_base = residual_scale * grad_first + times_transposed(query_self_low, self_query)
    inputs_base, self_corners, inputs_grad = together(inputs_base, self_corners, inputs_grad)

    self_sends = grid.side_sends(self_group, self_corners)
    self_sides = grid.side_moves(self_sends)
    reduce_grad = reduce_grad.astype(f32)
    expand_grad = expand_grad.astype(f32)
    expand_grad, cross_out_grad = expand_grad[:, :-width], expand_grad[:, -width:]
    memory_grad = memory_grad.astype(f32)
    inputs_grad = inputs_base + inputs_grad.astype(f32)
    self_sides, reduce_grad, expand_grad, cross_out_grad, memory_grad, inputs_grad = together(
        self_sides, reduce_grad, expand_grad, cross_out_grad, memory_grad, inputs_grad
    )

    self_chip = grid.chip_sum(self_group, self_sides)
    self_sends = grid.depth_sends(self_chip)
    self_depths = grid.depth_moves(self_sends)
    self_depths, cross_grad = together(self_depths, cross_grad)
    cross_grad = cross_grad.astype(f32)
    cross_query_grad = cross_grad[:, :width]
    cross_context_grad = cross_grad[:, width : 3 * width]
    self_out_grad = cross_grad[:, 3 * width :]
    self_grad = grid.share(self_chip, self_depths)
    self_inward_grad, share = self_grad[:, : 3 * width], self_grad[:, 3 * width :]
    (
        self_query_bias_grad,
        self_value_bias_grad,
        self_output_bias_grad,
        first_gain_grad,
        first_shift_grad,
        cross_query_bias_grad,
        cross_value_bias_grad,
        cross_output_bias_grad,
        second_gain_grad,
        second_shift_grad,
        reduce_bias_grad,
        third_gain_grad,
        third_shift_grad,
    ) = [line for line in share[:, : len(vectors)].T]
    expand_bias_grad = share[:, len(vectors) : spread].reshape(-1)

    return (
        result.reshape(pair_count, group_len, width),
        inputs_grad.reshape(pair_count, group_len, width),
        memory_grad.reshape(pair_count, group_len, width),
        self_inward_grad,
        self_out_grad,
        self_query_bias_grad,
        self_value_bias_grad,
        self_output_bias_grad,
        first_gain_grad,
        first_shift_grad,
        cross_query_grad,
        cross_context_grad,
        cross_out_grad,
        cross_query_bias_grad,
        cross_value_bias_grad,
        cross_output_bias_grad,
        second_gain_grad,
        second_shift_grad,
        expand_grad,
        expand_bias_grad,
        reduce_grad,
        reduce_bias_grad,
        third_gain_grad,
        third_shift_grad,
    )


def solution(mesh):
    rows = P(("dp", "seq"), None)
    vector = P(("dp", "seq"))
    tokens = P("dp", "seq", None)
    in_specs = (
        (tokens, tokens, P("dp", None), P("dp"), tokens)
        + (rows, rows)
        + (vector,) * 5
        + (rows,) * 3
        + (vector,) * 5
        + (rows, vector, rows)
        + (vector,) * 3
    )
    out_specs = (
        (tokens,) * 3
        + (rows, rows)
        + (vector,) * 5
        + (rows,) * 3
        + (vector,) * 5
        + (rows, vector, rows)
        + (vector,) * 3
    )
    return jax.shard_map(
        functools.partial(local, Grid(mesh)),
        mesh=mesh,
        in_specs=in_specs,
        out_specs=out_specs,
        check_vma=False,
    )
```

```python
import functools

import jax
import jax.numpy as jnp
from jax import lax
from jax.experimental import pallas as pl
from jax.experimental.pallas import tpu as pltpu
from jax.sharding import PartitionSpec as P

HEADS = 16
HEAD_DIM = 64
PAIR = 2 * HEAD_DIM

residual_scale = 4.16
epsilon = 1e-05
score_scale = 0.125
negative_fill = -1e30
bf16 = jnp.bfloat16
f32 = jnp.float32


def norm_layer(values, gain_vector, shift_vector):
    middle = jnp.mean(values, axis=-1, keepdims=True)
    centred = values - middle
    spread = jnp.mean(centred * centred, axis=-1, keepdims=True)
    return centred * lax.rsqrt(spread + epsilon) * gain_vector + shift_vector


def gelu_tanh(values):
    return (
        0.5
        * values
        * (1.0 + jnp.tanh(0.7978845608028654 * (values + 0.044715 * values * values * values)))
    )


def dense(left_side, right_side):
    return jnp.dot(left_side, right_side, preferred_element_type=f32)


def times_transposed(left_side, right_side):
    return lax.dot_general(
        left_side, right_side, (((1,), (1,)), ((), ())), preferred_element_type=f32
    )


def transposed_times(left_side, right_side):
    return lax.dot_general(
        left_side, right_side, (((0,), (0,)), ((), ())), preferred_element_type=f32
    )


def lane_head(shape, head):
    lane = lax.broadcasted_iota(jnp.int32, shape, 1)
    return (lane < HEAD_DIM) if head == 0 else (lane >= HEAD_DIM)


def masked_scores(scores, place_ref, causal, group_len):
    if not causal:
        return scores
    blocks = scores.shape[0] // group_len
    own = place_ref[0, blocks]
    diff = lax.broadcasted_iota(jnp.int32, (group_len, group_len), 0) - lax.broadcasted_iota(
        jnp.int32, (group_len, group_len), 1
    )
    parts = []
    for block in range(blocks):
        reach = (own - place_ref[0, block]) * group_len
        part = scores[block * group_len : (block + 1) * group_len]
        parts.append(jnp.where(diff <= reach, part, negative_fill))
    return jnp.concatenate(parts, axis=0)


def attend_forward_kernel(causal, place_ref, q_ref, k_ref, v_ref, o_ref, total_ref):
    group_len = q_ref.shape[0]
    heads = [(part, head) for part in range(q_ref.shape[1] // PAIR) for head in range(2)]

    def lanes(part):
        return slice(part * PAIR, (part + 1) * PAIR)

    def scores_of(part, head):
        scaled = q_ref[:, lanes(part)] * jnp.asarray(score_scale, bf16)
        own = jnp.where(lane_head(scaled.shape, head), scaled, jnp.zeros_like(scaled))
        return times_transposed(k_ref[:, lanes(part)], own)

    ahead = [scores_of(*at) for at in heads[:2]]
    outs = []
    for i, (part, head) in enumerate(heads):
        if i + 2 < len(heads):
            ahead.append(scores_of(*heads[i + 2]))
        here = masked_scores(ahead[i], place_ref, causal, group_len)
        top = jnp.max(here, axis=0, keepdims=True)
        weights = jnp.exp(here - top)
        total = jnp.sum(weights, axis=0, keepdims=True)
        blended = transposed_times(v_ref[:, lanes(part)], weights.astype(bf16)) / total
        outs.append(blended)
        total_ref[part, head : head + 1, :] = top + jnp.log(total)
        if head == 1:
            row = lax.broadcasted_iota(jnp.int32, blended.shape, 0)
            o_ref[:, lanes(part)] = (
                jnp.where(row < HEAD_DIM, outs[-2], outs[-1]).T.astype(bf16)
            )


def attend_backward_kernel(
    causal, place_ref, q_ref, k_ref, v_ref, total_ref, g_ref, dq_ref, dkv_ref, held, sems
):
    group_len = q_ref.shape[0]
    both = q_ref.shape[1]
    heads = [(part, head) for part in range(both // PAIR) for head in range(2)]
    step, steps = pl.program_id(0), pl.num_programs(0)
    slot = lax.rem(step, 2)
    width = dkv_ref.shape[1] // 2

    def moves(at, slot):
        return [
            pltpu.make_async_copy(
                held.at[slot, part],
                dkv_ref.at[:, pl.ds(pl.multiple_of(part * width + at * both, both), both)],
                sems.at[slot, part],
            )
            for part in range(2)
        ]

    @pl.when(step >= 2)
    def _():
        for move in moves(step - 2, slot):
            move.wait()

    def lanes(part):
        return slice(part * PAIR, (part + 1) * PAIR)

    def start_of(part, head):
        scaled = q_ref[:, lanes(part)] * jnp.asarray(score_scale, bf16)
        grads = g_ref[:, lanes(part)]
        mine = lane_head(scaled.shape, head)
        own = jnp.where(mine, scaled, jnp.zeros_like(scaled))
        grad = jnp.where(mine, grads, jnp.zeros_like(grads))
        return (
            own,
            grad,
            times_transposed(k_ref[:, lanes(part)], own),
            times_transposed(v_ref[:, lanes(part)], grad),
        )

    ahead = [start_of(*at) for at in heads[:2]]
    dqs, dks, dvs = [], [], []
    for i, (part, head) in enumerate(heads):
        if i + 2 < len(heads):
            ahead.append(start_of(*heads[i + 2]))
        own, grad, scores, dprob = ahead[i]
        here = masked_scores(scores, place_ref, causal, group_len)
        weights = jnp.exp(here - total_ref[part, head : head + 1, :])
        dvs.append(dense(weights.astype(bf16), grad))
        delta = jnp.sum(dprob * weights, axis=0, keepdims=True)
        dscore = (weights * (dprob - delta)).astype(bf16)
        dks.append(dense(dscore, own))
        dqs.append(transposed_times(k_ref[:, lanes(part)], dscore))
        if head == 1:
            row = lax.broadcasted_iota(jnp.int32, dqs[0].shape, 0)
            dq_ref[:, lanes(part)] = (
                jnp.where(row < HEAD_DIM, dqs[-2], dqs[-1]).T * score_scale
            )
            held[slot, 0, :, lanes(part)] = (dks[-2] + dks[-1]).astype(bf16)
            held[slot, 1, :, lanes(part)] = (dvs[-2] + dvs[-1]).astype(bf16)
    for move in moves(step, slot):
        move.start()

    @pl.when(step == steps - 1)
    def _():
        for move in moves(step - 1, 1 - slot):
            move.wait()
        for move in moves(step, slot):
            move.wait()


def attention_specs(group_len, length, pairs):
    row = pl.BlockSpec((group_len, 2 * PAIR), lambda h: (0, h))
    keys = pl.BlockSpec((length, 2 * PAIR), lambda h: (0, h))
    values = pl.BlockSpec((length, 2 * PAIR), lambda h: (0, h + pairs // 2))
    total = pl.BlockSpec((2, 2, group_len), lambda h: (h, 0, 0))
    place = pl.BlockSpec(memory_space=pltpu.SMEM)
    return place, row, keys, values, total


FREE = pl.CostEstimate(flops=1, bytes_accessed=1, transcendentals=0)
ROOM = pltpu.CompilerParams(vmem_limit_bytes=24 * 1024 * 1024)
WIDE_ROOM = pltpu.CompilerParams(vmem_limit_bytes=48 * 1024 * 1024)


def attend_forward(query_rows, context_rows, places, causal):
    group_len, width = query_rows.shape
    length = context_rows.shape[0]
    pairs = width // PAIR
    place, row, keys, values, total = attention_specs(group_len, length, pairs)
    return pl.pallas_call(
        functools.partial(attend_forward_kernel, causal),
        grid=(pairs // 2,),
        in_specs=[place, row, keys, values],
        out_specs=[row, total],
        out_shape=[
            jax.ShapeDtypeStruct((group_len, width), bf16),
            jax.ShapeDtypeStruct((pairs, 2, group_len), f32),
        ],
        compiler_params=WIDE_ROOM,
        cost_estimate=FREE,
    )(places, query_rows, context_rows, context_rows)


def attend_backward(query_rows, context_rows, places, totals, grads, causal):
    group_len, width = query_rows.shape
    length = context_rows.shape[0]
    pairs = width // PAIR
    place, row, keys, values, total = attention_specs(group_len, length, pairs)
    return pl.pallas_call(
        functools.partial(attend_backward_kernel, causal),
        grid=(pairs // 2,),
        in_specs=[place, row, keys, values, total, row],
        out_specs=[row, pl.BlockSpec(memory_space=pl.ANY)],
        out_shape=[
            jax.ShapeDtypeStruct((group_len, width), f32),
            jax.ShapeDtypeStruct((length, 2 * width), bf16),
        ],
        scratch_shapes=[
            pltpu.VMEM((2, 2, length, 2 * PAIR), bf16),
            pltpu.SemaphoreType.DMA((2, 2)),
        ],
        compiler_params=WIDE_ROOM,
        cost_estimate=FREE,
    )(places, query_rows, context_rows, context_rows, totals, grads)


def context_back_kernel(g_ref, k_ref, v_ref, out_ref):
    width = k_ref.shape[1]
    out_ref[...] = (
        times_transposed(g_ref[:, :width], k_ref[...])
        + times_transposed(g_ref[:, width:], v_ref[...])
    ).astype(bf16)


def context_back(grads, weights, start):
    length, both = grads.shape
    width = both // 2
    each = width // 4
    return pl.pallas_call(
        context_back_kernel,
        grid=(4,),
        in_specs=[
            pl.BlockSpec((length, both), lambda j: (0, 0)),
            pl.BlockSpec((each, width), lambda j: (j, start)),
            pl.BlockSpec((each, width), lambda j: (j, start + 1)),
        ],
        out_specs=pl.BlockSpec((length, each), lambda j: (0, j)),
        out_shape=jax.ShapeDtypeStruct((length, width), bf16),
        compiler_params=WIDE_ROOM,
        cost_estimate=FREE,
    )(grads, weights, weights)


def context_halves_kernel(where_ref, other_ref, own_ref, g_ref, sent_ref, kept_ref):
    rows = sent_ref.shape[0]
    grads = g_ref[...]
    sent_ref[...] = dense(other_ref[...].reshape(rows, -1), grads).astype(bf16)
    kept_ref[...] = dense(own_ref[...].reshape(rows, -1), grads).astype(bf16)


def turn_kernel(x_ref, out_ref):
    out_ref[...] = x_ref[...].T


def turned(values):
    rows, columns = values.shape
    return pl.pallas_call(
        turn_kernel,
        grid=(columns // PAIR,),
        in_specs=[pl.BlockSpec((rows, PAIR), lambda j: (0, j))],
        out_specs=pl.BlockSpec((PAIR, rows), lambda j: (j, 0)),
        out_shape=jax.ShapeDtypeStruct((columns, rows), values.dtype),
        compiler_params=ROOM,
        cost_estimate=FREE,
    )(values)


def feed_forward_kernel(x_ref, e_ref, r_ref, b_ref, expanded_ref, hidden_ref, out_ref):
    step = pl.program_id(0)
    wide = b_ref.shape[-1]
    expanded = dense(x_ref[...], e_ref[...].reshape(-1, wide)) + b_ref[...]
    expanded_ref[0] = expanded
    hidden = gelu_tanh(expanded).astype(bf16)
    hidden_ref[...] = hidden
    part = dense(hidden, r_ref[...].reshape(wide, -1))

    @pl.when(step == 0)
    def _():
        out_ref[...] = part

    @pl.when(step > 0)
    def _():
        out_ref[...] += part


def feed_backward_kernel(g_ref, e_ref, r_ref, expanded_ref, low_ref, bias_ref, out_ref):
    step = pl.program_id(0)
    wide = low_ref.shape[-1]
    grad_hidden = times_transposed(g_ref[...], r_ref[...].reshape(wide, -1))
    u = expanded_ref[0]
    square = u * u
    bent = jnp.tanh(0.7978845608028654 * (u + 0.044715 * square * u))
    slope = 0.5 * (1.0 + bent) + 0.5 * u * (1.0 - bent * bent) * (
        0.7978845608028654 * (1.0 + 3.0 * 0.044715 * square)
    )
    grad = grad_hidden * slope
    bias_ref[...] = jnp.sum(grad, axis=0, keepdims=True)
    low = grad.astype(bf16)
    low_ref[...] = low
    part = times_transposed(low, e_ref[...].reshape(-1, wide))

    @pl.when(step == 0)
    def _():
        out_ref[...] = part

    @pl.when(step > 0)
    def _():
        out_ref[...] += part


def feed_specs(count, width, each):
    return (
        pl.BlockSpec((count, width), lambda j: (0, 0)),
        pl.BlockSpec((1, width, each), lambda j: (j, 0, 0)),
        pl.BlockSpec((each, width), lambda j: (j, 0)),
        pl.BlockSpec((count, each), lambda j: (0, j)),
        pl.BlockSpec((1, each), lambda j: (0, j)),
        pl.BlockSpec((1, count, each), lambda j: (j, 0, 0)),
    )


def feed_forward(rows, expand_all, reduce_all, bias):
    count, width = rows.shape
    wide = reduce_all.shape[0]
    each = expand_all.shape[2]
    whole, first, second, part, line, block = feed_specs(count, width, each)
    return pl.pallas_call(
        feed_forward_kernel,
        grid=(wide // each,),
        in_specs=[whole, first, second, line],
        out_specs=[block, part, whole],
        out_shape=[
            jax.ShapeDtypeStruct((wide // each, count, each), f32),
            jax.ShapeDtypeStruct((count, wide), bf16),
            jax.ShapeDtypeStruct((count, width), f32),
        ],
        compiler_params=WIDE_ROOM,
        cost_estimate=FREE,
    )(rows, expand_all, reduce_all, bias.reshape(1, -1))


def feed_backward(grads, expand_all, reduce_all, expanded):
    count, width = grads.shape
    wide = reduce_all.shape[0]
    each = expand_all.shape[2]
    whole, first, second, part, line, block = feed_specs(count, width, each)
    return pl.pallas_call(
        feed_backward_kernel,
        grid=(wide // each,),
        in_specs=[whole, first, second, block],
        out_specs=[part, line, whole],
        out_shape=[
            jax.ShapeDtypeStruct((count, wide), bf16),
            jax.ShapeDtypeStruct((1, wide), f32),
            jax.ShapeDtypeStruct((count, width), f32),
        ],
        compiler_params=WIDE_ROOM,
        cost_estimate=FREE,
    )(grads, expand_all, reduce_all, expanded)


class Grid:
    def __init__(self, mesh):
        self.dp = mesh.shape["dp"]
        depth = mesh.shape["seq"]
        core = 2 if self.dp % 2 == 0 else 1
        chips = self.dp // core
        outer = 1
        while outer * outer < chips:
            outer *= 2
        inner = chips // outer
        self.sizes = {"outer": outer, "inner": inner, "core": core, "depth": depth}
        self.strides = {"outer": inner * core, "inner": core, "core": 1}

    def index(self, dim):
        if dim == "depth":
            return lax.axis_index("seq")
        return (lax.axis_index("dp") // self.strides[dim]) % self.sizes[dim]

    def shift(self, value, dim, step):
        size = self.sizes[dim]
        if dim == "depth":
            return lax.ppermute(value, "seq", [(i, (i + step) % size) for i in range(size)])
        stride = self.strides[dim]
        pairs = []
        for device in range(self.dp):
            at = (device // stride) % size
            pairs.append((device, device + ((at + step) % size - at) * stride))
        return lax.ppermute(value, "dp", pairs)

    def steps(self, dim):
        return range(1, self.sizes[dim])

    def from_depth(self, shard):
        return [self.shift(shard, "depth", step) for step in self.steps("depth")]

    def depth_block(self, shard, pieces):
        size, me = self.sizes["depth"], self.index("depth")
        return jnp.stack(
            [lax.select_n((me - at) % size, shard, *pieces) for at in range(size)]
        )

    def from_sides(self, block):
        return (
            [self.shift(block, "inner", step) for step in self.steps("inner")],
            [self.shift(block, "outer", step) for step in self.steps("outer")],
        )

    def from_corners(self, sides):
        along_inner, along_outer = sides
        half = along_inner[0].shape[0] // 2
        top = jnp.stack([block[:half] for block in along_inner])
        bottom = jnp.stack([block[half:] for block in along_outer])
        return (
            [self.shift(top, "outer", step) for step in self.steps("outer")],
            [self.shift(bottom, "inner", step) for step in self.steps("inner")],
        )

    def swap(self, pieces):
        return jax.tree.map(lambda piece: self.shift(piece, "core", 1), pieces)

    def whole(self, own, others, blocks=1):
        outer, inner, core = (self.sizes[n] for n in ("outer", "inner", "core"))
        each, total = own[0].shape[-2], own[0].shape[-1]
        columns = total // blocks
        height = self.sizes["depth"] * each
        half = height // 2
        pieces, places = [], []

        def add(piece, back_a, back_b, other, start):
            pieces.append(piece.reshape(-1, total))
            places.append((back_a, back_b, other, start))

        for other, (block, (along_inner, along_outer), (top, bottom)) in enumerate([own, others]):
            add(block, 0, 0, other, 0)
            for j, piece in enumerate(along_inner):
                add(piece, 0, j + 1, other, 0)
            for i, piece in enumerate(along_outer):
                add(piece, i + 1, 0, other, 0)
            for i in range(outer - 1):
                for j in range(inner - 1):
                    add(top[i][j], i + 1, j + 1, other, 0)
                    add(bottom[j][i], i + 1, j + 1, other, half)

        def kernel(*refs):
            out, sems = refs[len(pieces)], refs[len(pieces) + 1]
            device = lax.axis_index("dp")
            a = device // self.strides["outer"]
            b = lax.rem(device // self.strides["inner"], inner)
            c = lax.rem(device, core)
            copies = []
            for at, (ref, (back_a, back_b, other, start)) in enumerate(zip(refs, places)):
                to_a = lax.rem(a + (outer - back_a), outer)
                to_b = lax.rem(b + (inner - back_b), inner)
                to_c = lax.rem(c + other, core)
                index = (to_a * inner + to_b) * core + to_c
                for j in range(blocks):
                    copies.append(
                        pltpu.make_async_copy(
                            ref.at[:, pl.ds(j * columns, columns)],
                            out.at[j, index, pl.ds(start, ref.shape[0])],
                            sems.at[at, j],
                        )
                    )
            for copy in copies:
                copy.start()
            for copy in copies:
                copy.wait()

        anywhere = pl.BlockSpec(memory_space=pltpu.HBM)
        matrix = pl.pallas_call(
            kernel,
            in_specs=[anywhere] * len(pieces),
            out_specs=pl.BlockSpec(memory_space=pltpu.VMEM),
            out_shape=jax.ShapeDtypeStruct((blocks, outer * inner * core, height, columns), bf16),
            scratch_shapes=[pltpu.SemaphoreType.DMA((len(pieces), blocks))],
            compiler_params=WIDE_ROOM,
            cost_estimate=FREE,
        )(*pieces)
        matrix = matrix.reshape(blocks, -1, columns)
        return matrix if blocks > 1 else matrix[0]

    def picked(self, left_side):
        core = self.sizes["core"]
        count = self.sizes["outer"] * self.sizes["inner"]
        block = left_side.shape[1] // (count * core)
        me = self.index("core")
        even, odd = [
            [left_side[:, (core * j + i) * block : (core * j + i + 1) * block] for j in range(count)]
            for i in range(core)
        ]
        return tuple(
            jnp.concatenate(
                [jnp.where(me == 0, *((e, o) if own else (o, e))) for e, o in zip(even, odd)], axis=1
            )
            for own in (False, True)
        )

    def halves(self, picked, right_side):
        outer, inner, depth = self.sizes["outer"], self.sizes["inner"], self.sizes["depth"]
        each = picked[0].shape[1] // (outer * inner * depth)
        shape = (outer, inner, depth, each, right_side.shape[1])
        return tuple(
            transposed_times(chosen, right_side).astype(bf16).reshape(shape) for chosen in picked
        )

    def context_halves(self, turned, grads):
        outer, inner, core, depth = (self.sizes[n] for n in ("outer", "inner", "core", "depth"))
        height, rows = turned.shape
        block = height // (outer * inner * core)
        columns = grads.shape[1]
        each = columns // 4
        me = self.index("core")
        piece = (outer * inner, 1, block, rows)
        sent, kept = pl.pallas_call(
            context_halves_kernel,
            grid_spec=pltpu.PrefetchScalarGridSpec(
                num_scalar_prefetch=1,
                grid=(4,),
                in_specs=[
                    pl.BlockSpec(piece, lambda j, where: (0, where[0], 0, 0)),
                    pl.BlockSpec(piece, lambda j, where: (0, where[1], 0, 0)),
                    pl.BlockSpec((rows, each), lambda j, where: (0, j)),
                ],
                out_specs=[pl.BlockSpec((height // core, each), lambda j, where: (0, j))] * 2,
            ),
            out_shape=[jax.ShapeDtypeStruct((height // core, columns), bf16)] * 2,
            compiler_params=WIDE_ROOM,
            cost_estimate=FREE,
        )(
            jnp.stack([1 - me, me]).astype(jnp.int32),
            *([turned.reshape(outer * inner, core, block, rows)] * 2),
            grads,
        )
        shape = (outer, inner, depth, block // depth, columns)
        return sent.reshape(shape), kept.reshape(shape)

    def vector_halves(self, packed):
        core = self.sizes["core"]
        outer, inner, depth = self.sizes["outer"], self.sizes["inner"], self.sizes["depth"]
        split = packed.reshape((outer, inner, core, depth) + packed.shape[1:])
        me = self.index("core")
        even, odd = split[:, :, 0], split[:, :, 1]
        return jnp.where(me == 0, odd, even).astype(bf16), jnp.where(me == 0, even, odd)

    def sums(self, terms):
        return sum(term.astype(f32) for term in terms)

    def corner_sends(self, group):
        if self.square:
            top, bottom = self.block_sums(group, "corner", [])
            return [top], [bottom]
        outer, inner = self.sizes["outer"], self.sizes["inner"]
        a, b = self.index("outer"), self.index("inner")
        half = group[0][0].shape[2] // 2

        def block(terms, at_a, at_b, low, high):
            cut = [
                lax.dynamic_slice(
                    term,
                    (at_a % outer, at_b % inner, low, 0, 0),
                    (1, 1, high - low) + term.shape[3:],
                )
                for term in terms
            ]
            return self.sums(cut)[0, 0].astype(bf16)

        def joined(blocks):
            return jnp.concatenate(blocks, axis=-1) if len(blocks) > 1 else blocks[0]

        top = [
            jnp.stack(
                [
                    joined([block(terms, a + i, b + j, 0, half) for terms in group])
                    for j in self.steps("inner")
                ]
            )
            for i in self.steps("outer")
        ]
        bottom = [
            jnp.stack(
                [
                    joined([block(terms, a + i, b + j, half, 2 * half) for terms in group])
                    for i in self.steps("outer")
                ]
            )
            for j in self.steps("inner")
        ]
        return top, bottom

    def corner_moves(self, sends):
        top, bottom = sends
        return (
            [self.shift(send, "outer", step) for send, step in zip(top, self.steps("outer"))],
            [self.shift(send, "inner", step) for send, step in zip(bottom, self.steps("inner"))],
        )

    def side_sends(self, group, corners):
        top, bottom = corners
        if self.square:
            to_inner, to_outer = self.block_sums(group, "sides", [top[0], bottom[0]])
            return [to_inner], [to_outer]
        outer, inner = self.sizes["outer"], self.sizes["inner"]
        a, b = self.index("outer"), self.index("inner")
        half = group[0][0].shape[2] // 2

        def block(at_a, at_b, low, high, extra):
            sums, start = [], 0
            for terms in group:
                columns = terms[0].shape[-1]
                cut = [
                    lax.dynamic_slice(
                        term,
                        (at_a % outer, at_b % inner, low, 0, 0),
                        (1, 1, high - low) + term.shape[3:],
                    )[0, 0]
                    for term in terms
                ]
                cut += [piece[..., start : start + columns] for piece in extra]
                sums.append(self.sums(cut).astype(bf16))
                start += columns
            return jnp.concatenate(sums, axis=-1) if len(sums) > 1 else sums[0]

        to_inner = [
            jnp.concatenate(
                [
                    block(a, b + j, 0, half, [piece[j - 1] for piece in top]),
                    block(a, b + j, half, 2 * half, []),
                ]
            )
            for j in self.steps("inner")
        ]
        to_outer = [
            jnp.concatenate(
                [
                    block(a + i, b, 0, half, []),
                    block(a + i, b, half, 2 * half, [piece[i - 1] for piece in bottom]),
                ]
            )
            for i in self.steps("outer")
        ]
        return to_inner, to_outer

    def side_moves(self, sends):
        to_inner, to_outer = sends
        return [self.shift(send, "inner", step) for send, step in zip(to_inner, self.steps("inner"))] + [
            self.shift(send, "outer", step) for send, step in zip(to_outer, self.steps("outer"))
        ]

    def chip_terms(self, group, sides):
        a, b = self.index("outer"), self.index("inner")
        out, start = [], 0
        for terms in group:
            columns = terms[0].shape[-1]
            own = [
                lax.dynamic_slice(term, (a, b, 0, 0, 0), (1, 1) + term.shape[2:])[0, 0]
                for term in terms
            ]
            out.append(own + [piece[..., start : start + columns] for piece in sides])
            start += columns
        return out

    def chip_sum(self, group, sides):
        if self.square:
            total = sum(terms[0].shape[-1] for terms in group)
            return self.block_sums(group, "own", sides).reshape(
                self.sizes["depth"], -1, total
            )
        sums = [self.sums(terms).astype(bf16) for terms in self.chip_terms(group, sides)]
        return jnp.concatenate(sums, axis=-1) if len(sums) > 1 else sums[0]

    @property
    def square(self):
        return self.sizes["outer"] == 2 and self.sizes["inner"] == 2

    def block_sums(self, group, what, received):
        a, b = self.index("outer"), self.index("inner")
        place = {
            "corner": [(1 - a) * 2 + 1 - b],
            "sides": [a * 2 + 1 - b, (1 - a) * 2 + b],
            "own": [a * 2 + b],
        }[what]
        terms = [
            [term.reshape(4, -1, term.shape[-1]) for term in matrix] for matrix in group
        ]
        rows = terms[0][0].shape[1]
        half = rows // 2
        widths = [matrix[0].shape[-1] for matrix in terms]
        counts = [len(matrix) for matrix in terms]
        flat = [term for matrix in terms for term in matrix]
        received = [piece.reshape(-1, sum(widths)) for piece in received]

        def kernel(where_ref, *refs):
            terms_in, rest = refs[: len(flat)], refs[len(flat) :]
            got_in, rest = rest[: len(received)], rest[len(received) :]
            outs, rest = rest[: len(heights)], rest[len(heights) :]
            held, got, sems = rest[: len(flat)], rest[len(flat) : -1], rest[-1]
            copies = [
                pltpu.make_async_copy(
                    ref.at[where_ref[at]], held[i].at[at], sems.at[at * len(flat) + i]
                )
                for at in range(len(place))
                for i, ref in enumerate(terms_in)
            ]
            first_got = len(copies)
            copies += [
                pltpu.make_async_copy(ref, got[i], sems.at[first_got + i])
                for i, ref in enumerate(got_in)
            ]
            for copy in copies[first_got:] + copies[:first_got]:
                copy.start()
            for copy in copies[first_got:]:
                copy.wait()
            for at in range(len(place)):
                first, start = 0, 0
                for count, columns in zip(counts, widths):
                    for i in range(first, first + count):
                        copies[at * len(flat) + i].wait()
                    for low in range(0, columns, 512):
                        high = min(low + 512, columns)
                        here = slice(start + low, start + high)
                        value = sum(
                            ref[at, :, low:high].astype(f32) for ref in held[first : first + count]
                        )
                        if what == "corner":
                            outs[0][:, here] = value[:half].astype(bf16)
                            outs[1][:, here] = value[half:].astype(bf16)
                        elif what == "sides":
                            top, bottom = value[:half], value[half:]
                            if at == 0:
                                top = top + got[0][:, here].astype(f32)
                            else:
                                bottom = bottom + got[1][:, here].astype(f32)
                            outs[at][:half, here] = top.astype(bf16)
                            outs[at][half:, here] = bottom.astype(bf16)
                        else:
                            value = value + sum(ref[:, here].astype(f32) for ref in got)
                            outs[0][:, here] = value.astype(bf16)
                    first += count
                    start += columns

        heights = {"corner": [half, half], "sides": [rows, rows], "own": [rows]}[what]
        in_hbm = pl.BlockSpec(memory_space=pltpu.HBM)
        out = pl.pallas_call(
            kernel,
            in_specs=[pl.BlockSpec(memory_space=pltpu.SMEM)]
            + [in_hbm] * (len(flat) + len(received)),
            out_specs=[pl.BlockSpec(memory_space=pltpu.VMEM)] * len(heights),
            out_shape=[jax.ShapeDtypeStruct((height, sum(widths)), bf16) for height in heights],
            scratch_shapes=[
                pltpu.VMEM((len(place), rows, term.shape[-1]), term.dtype) for term in flat
            ]
            + [pltpu.VMEM(piece.shape, bf16) for piece in received]
            + [pltpu.SemaphoreType.DMA((len(place) * len(flat) + len(received),))],
            compiler_params=WIDE_ROOM,
            cost_estimate=FREE,
        )(jnp.stack(place).astype(jnp.int32), *flat, *received)
        return out[0] if what == "own" else out

    def depth_sends(self, chip):
        size, me = self.sizes["depth"], self.index("depth")
        return [
            lax.dynamic_index_in_dim(chip, (me + step) % size, 0, keepdims=False)
            for step in self.steps("depth")
        ]

    def depth_moves(self, sends):
        return [self.shift(send, "depth", step) for send, step in zip(sends, self.steps("depth"))]

    def share(self, chip, received):
        own = lax.dynamic_index_in_dim(chip, self.index("depth"), 0, keepdims=False)
        return self.sums([own] + received)


def together(*values):
    return lax.optimization_barrier(values)


def local(grid, *args):
    (
        inputs,
        memory,
        group_place,
        pair_mask,
        cotangent,
        self_inward,
        self_outward,
        self_query_bias,
        self_value_bias,
        self_output_bias,
        first_gain,
        first_shift,
        cross_query,
        cross_memory,
        cross_outward,
        cross_query_bias,
        cross_value_bias,
        cross_output_bias,
        second_gain,
        second_shift,
        expand_weight,
        expand_bias,
        reduce_weight,
        reduce_bias,
        third_gain,
        third_shift,
    ) = args
    pair_count, group_len, width = inputs.shape
    rows_in = inputs.reshape(group_len, width)
    rows_low = rows_in.astype(bf16)
    memory_low = memory.reshape(group_len, width).astype(bf16)

    vectors = (
        self_query_bias,
        self_value_bias,
        self_output_bias,
        first_gain,
        first_shift,
        cross_query_bias,
        cross_value_bias,
        cross_output_bias,
        second_gain,
        second_shift,
        reduce_bias,
        third_gain,
        third_shift,
    )
    rows = self_inward.shape[0]
    devices = width // rows
    places = jnp.concatenate(
        [
            group_place.reshape(1, -1),
            lax.dynamic_slice_in_dim(group_place, lax.axis_index("seq"), 1, axis=1),
        ],
        axis=1,
    )

    lane = 128
    one = jnp.concatenate(
        [self_inward, jnp.pad(self_query_bias[:, None], ((0, 0), (0, lane - 1)))], axis=1
    )
    packed = jnp.concatenate(
        [jnp.stack(vectors).T, expand_bias.reshape(rows, -1)], axis=1
    )
    spread = packed.shape[1]
    packed = jnp.pad(packed, ((0, 0), (0, lane - spread)))
    two = jnp.concatenate(
        [self_outward, cross_query, cross_outward, cross_memory, packed], axis=1
    )

    one_depth = grid.from_depth(one)
    one_depth, two, rows_low_sent = together(one_depth, two, rows_low)

    one_block = grid.depth_block(one, one_depth)
    one_sides = grid.from_sides(one_block)
    two_depth = grid.from_depth(two)
    one_sides, two_depth, rows_low_sent = together(one_sides, two_depth, rows_low_sent)

    all_low = lax.all_gather(rows_low_sent, "seq", axis=0, tiled=True)
    one_corners = grid.from_corners(one_sides)
    two_block = grid.depth_block(two, two_depth)
    one_corners, two_block = together(one_corners, two_block)

    two_sides = grid.from_sides(two_block)
    one_block_other, one_sides_other, one_corners_other = grid.swap(
        (one_block, one_sides, one_corners)
    )
    one_all = grid.whole(
        (one_block, one_sides, one_corners),
        (one_block_other, one_sides_other, one_corners_other),
    )
    self_query, self_context = one_all[:, :width], one_all[:, width : 3 * width]
    self_query_bias = one_all[:, 3 * width].astype(f32)
    query_self = (dense(rows_low, self_query) + self_query_bias).astype(bf16)
    two_sides, query_self, all_low, expand_weight = together(
        two_sides, query_self, all_low, expand_weight
    )

    two_corners = grid.from_corners(two_sides)
    expand_depth = grid.from_depth(expand_weight)
    context_self = dense(all_low, self_context).astype(bf16)
    blended_self, total_self = attend_forward(query_self, context_self, places, True)
    blended_self, two_corners, expand_depth, reduce_weight = together(
        blended_self, two_corners, expand_depth, reduce_weight
    )

    expand_block = grid.depth_block(expand_weight, expand_depth)
    two_block_other, two_sides_other, two_corners_other = grid.swap(
        (two_block, two_sides, two_corners)
    )
    two_block_other, two_sides_other, two_corners_other, expand_block = together(
        two_block_other, two_sides_other, two_corners_other, expand_block
    )
    expand_sides = grid.from_sides(expand_block)
    reduce_depth = grid.from_depth(reduce_weight)
    two_all = grid.whole(
        (two_block, two_sides, two_corners),
        (two_block_other, two_sides_other, two_corners_other),
    )
    packed = two_all[:, 5 * width : 5 * width + spread].astype(f32)
    (
        self_query_bias,
        self_value_bias,
        self_output_bias,
        first_gain,
        first_shift,
        cross_query_bias,
        cross_value_bias,
        cross_output_bias,
        second_gain,
        second_shift,
        reduce_bias,
        third_gain,
        third_shift,
    ) = [line for line in packed[:, : len(vectors)].T]
    expand_bias = packed[:, len(vectors) :].reshape(-1)
    self_outward, cross_query, cross_outward = [
        two_all[:, i * width : (i + 1) * width] for i in range(3)
    ]
    cross_context = two_all[:, 3 * width : 5 * width]
    blended_self = (blended_self + self_value_bias).astype(bf16)
    pre_first = residual_scale * rows_in + dense(blended_self, self_outward) + self_output_bias
    after_self = norm_layer(pre_first, first_gain, first_shift)
    after_self_low = after_self.astype(bf16)
    query_cross = (dense(after_self_low, cross_query) + cross_query_bias).astype(bf16)
    query_cross, expand_sides, reduce_depth, memory_low = together(
        query_cross, expand_sides, reduce_depth, memory_low
    )

    all_memory = lax.all_gather(memory_low, "seq", axis=0, tiled=True)
    reduce_block = grid.depth_block(reduce_weight, reduce_depth)
    expand_corners = grid.from_corners(expand_sides)
    reduce_sides = grid.from_sides(reduce_block)
    (expand_corners,) = together(expand_corners)
    expand_block_other, expand_sides_other, expand_corners_other = grid.swap(
        (expand_block, expand_sides, expand_corners)
    )
    expand_all = grid.whole(
        (expand_block, expand_sides, expand_corners),
        (expand_block_other, expand_sides_other, expand_corners_other),
        expand_weight.shape[1] // width,
    )
    picks = [
        grid.picked(left) for left in (rows_low, blended_self, after_self_low)
    ] + [turned(all_low)]
    expand_all, reduce_sides, all_memory, picks = together(
        expand_all, reduce_sides, all_memory, picks
    )

    reduce_corners = grid.from_corners(reduce_sides)
    reduce_block_other = grid.swap(reduce_block)
    reduce_sides_other = grid.swap(reduce_sides)
    context_cross = dense(all_memory, cross_context).astype(bf16)
    blended_cross, total_cross = attend_forward(query_cross, context_cross, places, False)
    reduce_corners, blended_cross, reduce_block_other, reduce_sides_other = together(
        reduce_corners, blended_cross, reduce_block_other, reduce_sides_other
    )

    reduce_corners_other = grid.swap(reduce_corners)
    blended_cross = (blended_cross + cross_value_bias).astype(bf16)
    pre_second = (
        residual_scale * after_self + dense(blended_cross, cross_outward) + cross_output_bias
    )
    after_cross = norm_layer(pre_second, second_gain, second_shift)
    cross_low = after_cross.astype(bf16)
    reduce_all = grid.whole(
        (reduce_block, reduce_sides, reduce_corners),
        (reduce_block_other, reduce_sides_other, reduce_corners_other),
    )
    expanded, hidden, reduced = feed_forward(cross_low, expand_all, reduce_all, expand_bias)
    pre_third = residual_scale * after_cross + reduced + reduce_bias
    result = norm_layer(pre_third, third_gain, third_shift)

    grad_out = cotangent.reshape(group_len, width) * pair_mask.astype(f32)[0]
    norm_back = jax.vjp(norm_layer, pre_third, third_gain, third_shift)[1]
    grad_third, third_gain_grad, third_shift_grad = norm_back(grad_out)
    reduce_bias_grad = jnp.sum(grad_third, axis=0)
    low_third = grad_third.astype(bf16)
    expanded_low, expand_bias_grad, grad_cross = feed_backward(
        low_third, expand_all, reduce_all, expanded
    )
    hidden_other, hidden_own = grid.picked(hidden)
    (reduce_sent,) = grid.halves((hidden_other,), low_third)
    reduce_sent, expanded_low, grad_cross, low_third = together(
        reduce_sent, expanded_low, grad_cross, low_third
    )

    reduce_got = grid.swap(reduce_sent)
    expand_sent, expand_kept = grid.halves(grid.picked(cross_low), expanded_low)
    grad_cross = residual_scale * grad_third + grad_cross
    norm_back = jax.vjp(norm_layer, pre_second, second_gain, second_shift)[1]
    grad_second, second_gain_grad, second_shift_grad = norm_back(grad_cross)
    cross_output_bias_grad = jnp.sum(grad_second, axis=0)
    second_low = grad_second.astype(bf16)
    grad_blended = times_transposed(second_low, cross_outward).astype(bf16)
    out_sent, out_kept = grid.halves(grid.picked(blended_cross), second_low)
    (reduce_kept,) = grid.halves((hidden_own,), low_third)
    (
        grad_blended,
        reduce_got,
        reduce_kept,
        expand_sent,
        expand_kept,
        out_sent,
        out_kept,
    ) = together(
        grad_blended, reduce_got, reduce_kept, expand_sent, expand_kept, out_sent, out_kept
    )

    reduce_group = [[reduce_kept, reduce_got]]
    reduce_sends = grid.corner_sends(reduce_group)
    reduce_sends, grad_blended, expand_sent, out_sent = together(
        reduce_sends, grad_blended, expand_sent, out_sent
    )
    reduce_corners = grid.corner_moves(reduce_sends)
    expand_got, out_got = grid.swap((expand_sent, out_sent))
    grad_query_cross, grad_context_cross = attend_backward(
        query_cross, context_cross, places, total_cross, grad_blended, False
    )
    grad_query_cross, grad_context_cross, reduce_corners, expand_got, out_got = together(
        grad_query_cross, grad_context_cross, reduce_corners, expand_got, out_got
    )

    reduce_sends = grid.side_sends(reduce_group, reduce_corners)
    reduce_sends, grad_query_cross, grad_context_cross = together(
        reduce_sends, grad_query_cross, grad_context_cross
    )
    reduce_sides = grid.side_moves(reduce_sends)
    memory_part = context_back(grad_context_cross, two_all, 3)
    context_sent, context_kept = grid.context_halves(
        turned(all_memory), grad_context_cross
    )
    grad_query_cross, memory_part, reduce_sides, context_sent, context_kept = together(
        grad_query_cross, memory_part, reduce_sides, context_sent, context_kept
    )

    expand_group = [[expand_kept, expand_got], [out_kept, out_got]]
    expand_sends = grid.corner_sends(expand_group)
    reduce_chip = grid.chip_sum(reduce_group, reduce_sides)
    expand_sends, reduce_chip, grad_query_cross, memory_part = together(
        expand_sends, reduce_chip, grad_query_cross, memory_part
    )
    expand_corners = grid.corner_moves(expand_sends)
    joined = lax.psum_scatter(
        jnp.concatenate([reduce_chip, memory_part.reshape(-1, group_len, width)], axis=1),
        "seq",
        scatter_dimension=0,
    )
    cross_query_bias_grad = jnp.sum(grad_query_cross, axis=0)
    query_cross_low = grad_query_cross.astype(bf16)
    grad_self = residual_scale * grad_second + times_transposed(query_cross_low, cross_query)
    norm_back = jax.vjp(norm_layer, pre_first, first_gain, first_shift)[1]
    grad_first, first_gain_grad, first_shift_grad = norm_back(grad_self)
    self_output_bias_grad = jnp.sum(grad_first, axis=0)
    first_low = grad_first.astype(bf16)
    outward_sent, outward_kept = grid.halves(picks[1], first_low)
    grad_blended = times_transposed(first_low, self_outward).astype(bf16)
    query_sent, query_kept = grid.halves(picks[2], query_cross_low)
    grad_blended, expand_corners, outward_sent, outward_kept, query_sent, query_kept = together(
        grad_blended, expand_corners, outward_sent, outward_kept, query_sent, query_kept
    )

    expand_sends = grid.side_sends(expand_group, expand_corners)
    expand_sends, grad_blended, context_sent, query_sent, outward_sent = together(
        expand_sends, grad_blended, context_sent, query_sent, outward_sent
    )
    expand_sides = grid.side_moves(expand_sends)
    context_got, query_got, outward_got = grid.swap((context_sent, query_sent, outward_sent))
    cross_group = [
        [query_kept, query_got],
        [context_kept, context_got],
        [outward_kept, outward_got],
    ]
    grad_query_self, grad_context_self = attend_backward(
        query_self, context_self, places, total_self, grad_blended, True
    )
    inputs_part = context_back(grad_context_self, one_all, 1)
    context_sent, context_kept = grid.context_halves(picks[3], grad_context_self)
    query_self_low = grad_query_self.astype(bf16)
    query_sent, query_kept = grid.halves(picks[0], query_self_low)
    (
        cross_group,
        expand_sides,
        grad_query_self,
        grad_context_self,
        query_self_low,
        query_sent,
        context_sent,
        query_kept,
        context_kept,
        inputs_part,
    ) = together(
        cross_group,
        expand_sides,
        grad_query_self,
        grad_context_self,
        query_self_low,
        query_sent,
        context_sent,
        query_kept,
        context_kept,
        inputs_part,
    )

    inputs_grad = lax.psum_scatter(inputs_part, "seq", scatter_dimension=0, tiled=True)
    cross_sends = grid.corner_sends(cross_group)
    lines = (
        self_output_bias_grad,
        first_gain_grad,
        first_shift_grad,
        cross_query_bias_grad,
        cross_output_bias_grad,
        second_gain_grad,
        second_shift_grad,
        reduce_bias_grad,
        third_gain_grad,
        third_shift_grad,
        expand_bias_grad,
    )
    cross_sends, grad_query_self, grad_context_self, grad_context_cross, lines = together(
        cross_sends, grad_query_self, grad_context_self, grad_context_cross, lines
    )
    cross_corners = grid.corner_moves(cross_sends)
    expand_chip = grid.chip_sum(expand_group, expand_sides)
    expand_grad = lax.psum_scatter(expand_chip, "seq", scatter_dimension=0)
    self_query_bias_grad = jnp.sum(grad_query_self, axis=0)
    self_value_bias_grad = jnp.sum(grad_context_self[:, width:].astype(f32), axis=0)
    cross_value_bias_grad = jnp.sum(grad_context_cross[:, width:].astype(f32), axis=0)
    vector_grads = jnp.concatenate(
        [
            jnp.stack(
                (self_query_bias_grad, self_value_bias_grad)
                + tuple(lines[:4])
                + (cross_value_bias_grad,)
                + tuple(lines[4:10])
            ).T,
            lines[10].reshape(width, -1),
        ],
        axis=1,
    )
    vector_grads = jnp.pad(vector_grads, ((0, 0), (0, lane - spread)))
    vector_grads = vector_grads.reshape(devices, rows, lane)
    vector_sent, vector_kept = grid.vector_halves(vector_grads)
    cross_corners, vector_sent, vector_kept, expand_chip, joined = together(
        cross_corners, vector_sent, vector_kept, expand_chip, joined
    )
    reduce_grad, memory_grad = joined[:-group_len], joined[-group_len:]

    cross_sends = grid.side_sends(cross_group, cross_corners)
    cross_sends, query_sent, context_sent, vector_sent = together(
        cross_sends, query_sent, context_sent, vector_sent
    )
    cross_sides = grid.side_moves(cross_sends)
    query_got, context_got, vector_got = grid.swap((query_sent, context_sent, vector_sent))
    cross_sides, query_got, context_got, vector_got = together(
        cross_sides, query_got, context_got, vector_got
    )

    self_group = [
        [query_kept, query_got],
        [context_kept, context_got],
        [vector_kept, vector_got],
    ]
    self_sends = grid.corner_sends(self_group)
    cross_chip = grid.chip_sum(cross_group, cross_sides)
    self_sends, query_self_low = together(self_sends, query_self_low)
    self_corners = grid.corner_moves(self_sends)
    cross_grad = lax.psum_scatter(cross_chip, "seq", scatter_dimension=0)
    inputs_base = residual_scale * grad_first + times_transposed(query_self_low, self_query)
    inputs_base, self_corners, inputs_grad, cross_chip = together(
        inputs_base, self_corners, inputs_grad, cross_chip
    )

    self_sends = grid.side_sends(self_group, self_corners)
    self_sides = grid.side_moves(self_sends)
    reduce_grad = reduce_grad.astype(f32)
    expand_grad = expand_grad.astype(f32)
    expand_grad, cross_out_grad = expand_grad[:, :-width], expand_grad[:, -width:]
    memory_grad = memory_grad.astype(f32)
    inputs_grad = inputs_base + inputs_grad.astype(f32)
    self_sides, reduce_grad, expand_grad, cross_out_grad, memory_grad, inputs_grad = together(
        self_sides, reduce_grad, expand_grad, cross_out_grad, memory_grad, inputs_grad
    )

    self_chip = grid.chip_sum(self_group, self_sides)
    self_sends = grid.depth_sends(self_chip)
    self_depths = grid.depth_moves(self_sends)
    self_depths, cross_grad = together(self_depths, cross_grad)
    cross_grad = cross_grad.astype(f32)
    cross_query_grad = cross_grad[:, :width]
    cross_context_grad = cross_grad[:, width : 3 * width]
    self_out_grad = cross_grad[:, 3 * width :]
    self_grad = grid.share(self_chip, self_depths)
    self_inward_grad, share = self_grad[:, : 3 * width], self_grad[:, 3 * width :]
    (
        self_query_bias_grad,
        self_value_bias_grad,
        self_output_bias_grad,
        first_gain_grad,
        first_shift_grad,
        cross_query_bias_grad,
        cross_value_bias_grad,
        cross_output_bias_grad,
        second_gain_grad,
        second_shift_grad,
        reduce_bias_grad,
        third_gain_grad,
        third_shift_grad,
    ) = [line for line in share[:, : len(vectors)].T]
    expand_bias_grad = share[:, len(vectors) : spread].reshape(-1)

    return (
        result.reshape(pair_count, group_len, width),
        inputs_grad.reshape(pair_count, group_len, width),
        memory_grad.reshape(pair_count, group_len, width),
        self_inward_grad,
        self_out_grad,
        self_query_bias_grad,
        self_value_bias_grad,
        self_output_bias_grad,
        first_gain_grad,
        first_shift_grad,
        cross_query_grad,
        cross_context_grad,
        cross_out_grad,
        cross_query_bias_grad,
        cross_value_bias_grad,
        cross_output_bias_grad,
        second_gain_grad,
        second_shift_grad,
        expand_grad,
        expand_bias_grad,
        reduce_grad,
        reduce_bias_grad,
        third_gain_grad,
        third_shift_grad,
    )


def solution(mesh):
    rows = P(("dp", "seq"), None)
    vector = P(("dp", "seq"))
    tokens = P("dp", "seq", None)
    in_specs = (
        (tokens, tokens, P("dp", None), P("dp"), tokens)
        + (rows, rows)
        + (vector,) * 5
        + (rows,) * 3
        + (vector,) * 5
        + (rows, vector, rows)
        + (vector,) * 3
    )
    out_specs = (
        (tokens,) * 3
        + (rows, rows)
        + (vector,) * 5
        + (rows,) * 3
        + (vector,) * 5
        + (rows, vector, rows)
        + (vector,) * 3
    )
    return jax.shard_map(
        functools.partial(local, Grid(mesh)),
        mesh=mesh,
        in_specs=in_specs,
        out_specs=out_specs,
        check_vma=False,
    )
```
